32 devices in a mesh: rep: 4 (over z), fsdp: 8 (over y, x, core).
Axes of the slice: x: 2, y: 2, z: 4, core: 2. Of those that a mesh axis runs over, the one named last changes fastest.
Arguments:
- tokens: bfloat16 [64, 512, 768], P(('rep', 'fsdp')), may hold values from -6 to 6
- doc_lengths: int32 [64, 16], P(('rep', 'fsdp')), may hold values from 0 to 512, as said below
- query_weight: bfloat16 [768, 768], P('fsdp'), may hold values from -0.21875 to 0.21875
- key_weight: bfloat16 [768, 768], P('fsdp'), may hold values from -0.21875 to 0.21875
- value_weight: bfloat16 [768, 768], P('fsdp'), may hold values from -0.21875 to 0.21875
- output_weight: bfloat16 [768, 768], P('fsdp'), may hold values from -0.625 to 0.625
- inner_weight: bfloat16 [768, 3072], P('fsdp'), may hold values from -0.21875 to 0.21875
- outer_weight: bfloat16 [3072, 768], P('fsdp'), may hold values from -0.109375 to 0.109375
- query_bias: bfloat16 [768], P('fsdp'), may hold values from -3 to 3
- value_bias: bfloat16 [768], P('fsdp'), may hold values from -3 to 3
- output_bias: bfloat16 [768], P('fsdp'), may hold values from -3 to 3
- inner_bias: bfloat16 [3072], P('fsdp'), may hold values from -3 to 3
- outer_bias: bfloat16 [768], P('fsdp'), may hold values from -3 to 3
- first_gain: bfloat16 [768], P('fsdp'), may hold values from 0.5 to 1.5
- first_shift: bfloat16 [768], P('fsdp'), may hold values from -3 to 3
- second_gain: bfloat16 [768], P('fsdp'), may hold values from 0.5 to 1.5
- second_shift: bfloat16 [768], P('fsdp'), may hold values from -3 to 3
- cotangent: float32 [64, 512, 768], P(('rep', 'fsdp')), may hold values from -6 to 6
Outputs:
- encoded: bfloat16 [64, 512, 768], P(('rep', 'fsdp'))
- tokens_grad: float32 [64, 512, 768], P(('rep', 'fsdp'))
- query_grad: float32 [768, 768], P('fsdp')
- key_grad: float32 [768, 768], P('fsdp')
- value_grad: float32 [768, 768], P('fsdp')
- output_grad: float32 [768, 768], P('fsdp')
- inner_grad: float32 [768, 3072], P('fsdp')
- outer_grad: float32 [3072, 768], P('fsdp')
- querybias_grad: float32 [768], P('fsdp')
- valuebias_grad: float32 [768], P('fsdp')
- outputbias_grad: float32 [768], P('fsdp')
- innerbias_grad: float32 [3072], P('fsdp')
- outerbias_grad: float32 [768], P('fsdp')
- firstgain_grad: float32 [768], P('fsdp')
- firstshift_grad: float32 [768], P('fsdp')
- secondgain_grad: float32 [768], P('fsdp')
- secondshift_grad: float32 [768], P('fsdp')
The draws below stay inside these ranges and needn't reach their ends.
Inputs may be any that keep to these rules, and one draw needn't show every extreme that they name: `doc_lengths`: each row's lengths sum to at most 512; nonzero lengths stand first and the first is 1 or more; in every draw some row holds one document of 512 slots.
All inputs are finite; a program needn't handle non-finite values.
Results may differ from the reference program's by a relative error of at most 0.017.
Values may be sent and summed in bfloat16 or wider, within the bound.
No kernel may reach another device: no remote copies, remote signals or barrier semaphores. Data moves between devices by JAX's collectives and lax.ppermute only.
A program may use at most 192 MiB of HBM per device.

```python
import math
import jax
import jax.numpy as jnp
from jax import lax

HD = 64
D = 768
FF = 3072
SLOTS = 512
DOCS = 16
ROWS = 64


def draw_doc_lengths(key, part):
    key = jax.random.fold_in(key, 11)
    key_count, key_length, key_page = jax.random.split(key, 3)
    counts = jax.random.randint(key_count, (ROWS, 1), 1, DOCS + 1)
    lengths = jax.random.randint(key_length, (ROWS, DOCS), SLOTS // 64 + 1, SLOTS // 8 + 1)
    places = jnp.arange(DOCS, dtype=jnp.int32)[None, :]
    lengths = jnp.where(places < counts, lengths, 0)
    pages = (jax.random.randint(key_page, (ROWS, 1), 0, 4) == 0) | (jnp.arange(ROWS, dtype=jnp.int32)[:, None] == 0)
    lengths = jnp.where(pages, jnp.where(places == 0, SLOTS, 0), lengths)
    before = jnp.cumsum(lengths, axis=-1) - lengths
    lengths = jnp.minimum(lengths, jnp.maximum(SLOTS - before, 0))
    return lengths.astype(jnp.int32)


def shard_levels(stream_key, extent, shards, least, high):
    factor_of, own = 1.0, jax.random.fold_in(stream_key, 6)
    for position, shards_of in shards:
        heights = jnp.exp(jax.random.uniform(jax.random.fold_in(own, position), (shards_of,), jnp.float32, least / len(shards), high / len(shards)))
        factor_of = factor_of * jnp.repeat(heights, extent[position] // shards_of).reshape([-1 if axis == position else 1 for axis in range(len(extent))])
    return factor_of


def centred(rng, extent, scale, bound, cuts=(), kind=jnp.bfloat16):
    values = scale * jax.random.normal(rng, extent, jnp.float32)
    if cuts:
        values = values * shard_levels(rng, extent, cuts, -0.22, 0.18)
    return jnp.clip(values, -bound, bound).astype(kind)


def setup_inputs(seed: int = 0) -> dict:
    arg_keys = jax.random.split(jax.random.key(seed), 19)
    tokens = centred(arg_keys[0], (ROWS, SLOTS, D), 1.0, 6.0, ((0, 32),))
    doc_lengths = draw_doc_lengths(jax.random.fold_in(arg_keys[18], 71), 0)
    query_weight = centred(arg_keys[2], (D, D), D ** -0.5, 0.21875, ((0, 8),))
    key_weight = centred(arg_keys[3], (D, D), D ** -0.5, 0.21875, ((0, 8),))
    value_weight = centred(arg_keys[4], (D, D), D ** -0.5, 0.21875, ((0, 8),))
    output_weight = centred(arg_keys[5], (D, D), (D // 8) ** -0.5, 0.625, ((0, 8),))
    inner_weight = centred(arg_keys[6], (D, FF), D ** -0.5, 0.21875, ((0, 8),))
    outer_weight = centred(arg_keys[7], (FF, D), FF ** -0.5, 0.109375, ((0, 8),))
    query_bias = centred(arg_keys[8], (D,), 0.5, 3.0, ((0, 8),))
    value_bias = centred(arg_keys[9], (D,), 0.5, 3.0, ((0, 8),))
    output_bias = centred(arg_keys[10], (D,), 0.5, 3.0, ((0, 8),))
    inner_bias = centred(arg_keys[11], (FF,), 0.5, 3.0, ((0, 8),))
    outer_bias = centred(arg_keys[12], (D,), 0.5, 3.0, ((0, 8),))
    first_gain = jnp.clip(1.0 + 0.1 * jax.random.normal(arg_keys[13], (D,), jnp.float32), 0.5, 1.5).astype(jnp.bfloat16)
    first_shift = centred(arg_keys[14], (D,), 0.5, 3.0, ((0, 8),))
    second_gain = jnp.clip(1.0 + 0.1 * jax.random.normal(arg_keys[15], (D,), jnp.float32), 0.5, 1.5).astype(jnp.bfloat16)
    second_shift = centred(arg_keys[16], (D,), 0.5, 3.0, ((0, 8),))
    cotangent = centred(arg_keys[17], (ROWS, SLOTS, D), 1.0, 6.0, ((0, 32),), jnp.float32)
    return dict(tokens=tokens, doc_lengths=doc_lengths, query_weight=query_weight, key_weight=key_weight, value_weight=value_weight, output_weight=output_weight, inner_weight=inner_weight, outer_weight=outer_weight, query_bias=query_bias, value_bias=value_bias, output_bias=output_bias, inner_bias=inner_bias, outer_bias=outer_bias, first_gain=first_gain, first_shift=first_shift, second_gain=second_gain, second_shift=second_shift, cotangent=cotangent)


EPSILON = 1e-05
HIGHEST = lax.Precision.HIGHEST

@jax.custom_vjp
def low(v):
    return lax.optimization_barrier(v.astype(jnp.bfloat16)).astype(jnp.float32)

@jax.custom_vjp
def low_back(v):
    return v

def low_keep(v):
    return (low(v), None)

def low_pass(kept, grad):
    return (grad,)

def back_keep(v):
    return (v, None)

def back_low(kept, grad):
    return (low(grad),)
low.defvjp(low_keep, low_pass)
low_back.defvjp(back_keep, back_low)

def segments_of(doc_lengths, slots):
    ends = jnp.cumsum(doc_lengths, axis=-1).astype(jnp.int32)
    places = jnp.arange(slots, dtype=jnp.int32)
    return lax.optimization_barrier(jnp.sum((places[:, None] >= ends[..., None, :]).astype(jnp.int32), axis=-1)).astype(jnp.int32)

def norm_layer(values, gain, shift):
    center = values - lax.optimization_barrier(jnp.mean(values, axis=-1, keepdims=True))
    spread = lax.optimization_barrier(jnp.mean(center * center, axis=-1, keepdims=True))
    return center * lax.rsqrt(spread + EPSILON) * gain + shift

def dense(values, weight):
    return jnp.einsum('...d,de->...e', values, weight, precision=HIGHEST)

def attend(query, keys, values, segment):
    scale = 1.0 / math.sqrt(query.shape[-1])
    scores = low_back(jnp.einsum('qhd,khd->hqk', query, keys, precision=HIGHEST) * scale)
    allowed = (segment[:, None] == segment[None, :])[None]
    scores = jnp.where(allowed, scores, -1e+30)
    total = jax.nn.logsumexp(scores, axis=-1, keepdims=True)
    probs = low(jnp.exp(scores - total))
    return jnp.einsum('hqk,khd->qhd', probs, values, precision=HIGHEST)

def layer(params, tokens, segment):
    query_weight, key_weight, value_weight, output_weight, inner_weight, outer_weight, query_bias, value_bias, output_bias, inner_bias, outer_bias, first_gain, first_shift, second_gain, second_shift = params
    rows, slots, width = tokens.shape
    heads = width // HD
    query = low(low_back(dense(tokens, query_weight) + query_bias)).reshape(rows, slots, heads, HD)
    keys = low(low_back(dense(tokens, key_weight))).reshape(rows, slots, heads, HD)
    values = low(low_back(dense(tokens, value_weight) + value_bias)).reshape(rows, slots, heads, HD)
    mixed = jax.vmap(attend)(query, keys, values, segment).reshape(rows, slots, width)
    mixed = low(low_back(mixed))
    branch = low_back(dense(mixed, output_weight) + output_bias)
    hidden = norm_layer(tokens + branch, first_gain, first_shift)
    inner = low_back(dense(low(hidden), inner_weight) + inner_bias)
    activated = low(jax.nn.gelu(inner, approximate=False))
    outer = low_back(dense(activated, outer_weight) + outer_bias)
    return norm_layer(hidden + outer, second_gain, second_shift)

def reference(tokens, doc_lengths, query_weight, key_weight, value_weight, output_weight, inner_weight, outer_weight, query_bias, value_bias, output_bias, inner_bias, outer_bias, first_gain, first_shift, second_gain, second_shift, cotangent):
    segment = segments_of(doc_lengths, SLOTS)
    valid = (segment < DOCS).astype(cotangent.dtype)
    params = tuple((item.astype(jnp.float32) for item in (query_weight, key_weight, value_weight, output_weight, inner_weight, outer_weight, query_bias, value_bias, output_bias, inner_bias, outer_bias, first_gain, first_shift, second_gain, second_shift)))
    group = math.gcd(ROWS, 8)
    inputs = tokens.astype(jnp.float32).reshape(ROWS // group, group, SLOTS, D)
    seg_groups = segment.reshape(ROWS // group, group, SLOTS)

    def forward(weights, values):
        block = jax.checkpoint(lambda pair: layer(weights, pair[0], pair[1]))
        return lax.map(block, (values, seg_groups))
    encoded, pullback = jax.vjp(forward, params, inputs)
    seed_grad = (cotangent * valid[..., None]).astype(jnp.float32).reshape(ROWS // group, group, SLOTS, D)
    weight_grads, token_grads = pullback(seed_grad)
    factor = 1.0 / math.sqrt(ROWS * SLOTS)
    scaled = [item * factor for item in weight_grads]
    return (encoded.reshape(ROWS, SLOTS, D).astype(jnp.bfloat16), token_grads.reshape(ROWS, SLOTS, D), scaled[0], scaled[1], scaled[2], scaled[3], scaled[4], scaled[5], scaled[6], scaled[7], scaled[8], scaled[9], scaled[10], scaled[11], scaled[12], scaled[13], scaled[14])
```

```python
import functools
import math

import jax
import jax.numpy as jnp
from jax import lax
from jax.experimental import pallas as pl
from jax.experimental.pallas import tpu as pltpu
from jax.sharding import PartitionSpec as P

HD = 64
EPSILON = 1e-05
BF = jnp.bfloat16
F32 = jnp.float32
NT = ((1,), (1,))
VMEM_BYTES = 60 * 2**20
CORE, X, Y = 1, 2, 4
ROW_TILE = 256
FF_CHUNK = 768


def dot(a, b, dims=((1,), (0,))):
    return lax.dot_general(a, b, (dims, ((), ())), preferred_element_type=F32)


def params():
    return pltpu.CompilerParams(
        vmem_limit_bytes=VMEM_BYTES, dimension_semantics=("arbitrary",)
    )


def cost(flops, nbytes, trans=0):
    return pl.CostEstimate(
        flops=int(flops), bytes_accessed=int(nbytes), transcendentals=int(trans)
    )


def whole(shape):
    return pl.BlockSpec(
        shape, lambda *i: (0,) * len(shape), pipeline_mode=pl.Buffered(1)
    )


def anywhere(count):
    return [pl.BlockSpec(memory_space=pl.ANY)] * count


def flip(array, axis, bit):
    size = lax.axis_size(axis)
    return lax.ppermute(array, axis, [(i, i ^ bit) for i in range(size)])


def piece_copies(pieces, refs, target, sems, first):
    copies = []
    for slot, (which, start, rows, rel) in enumerate(pieces):
        if rel is None:
            place = 0
        else:
            place = pl.multiple_of((lax.axis_index("fsdp") ^ rel) * rows, rows)
        copies.append(
            pltpu.make_async_copy(
                refs[which].at[pl.ds(start, rows), :],
                target.at[pl.ds(place, rows), :],
                sems.at[first + slot],
            )
        )
    return copies


def index_pieces(weights):
    arrays, numbered = [], []
    for pieces in weights:
        mine = []
        for array, start, rows, rel in pieces:
            for n, seen in enumerate(arrays):
                if seen is array:
                    break
            else:
                n = len(arrays)
                arrays.append(array)
            mine.append((n, start, rows, rel))
        numbered.append(mine)
    return arrays, numbered


def gather_pair(one, two, sizes_one, sizes_two):
    def spread(block, first, second, sizes):
        near = flip(block, "fsdp", first)
        far = flip(jnp.concatenate([block, near], axis=0), "fsdp", second)
        rows = block.shape[0]
        held = [(block, 0, 0), (near, 0, first), (far, 0, second), (far, rows, first | second)]
        other = {id(a): flip(a, "fsdp", CORE) for a in (block, near, far)}
        held += [(other[id(a)], at, rel | CORE) for a, at, rel in held]
        out, place = [], 0
        for size in sizes:
            out.append([(a, at + place, size, rel) for a, at, rel in held])
            place += size
        return out

    return spread(one, X, Y, sizes_one) + spread(two, Y, X, sizes_two)


def column_of(row):
    return jnp.broadcast_to(row, (128, row.shape[1])).T[:, :1]


def attend_kernel(numbered, n_arrays, heads, tok_ref, seg_ref, vec_ref, *refs):
    pieces = refs[:n_arrays]
    q_ref, k_ref, v_ref, mt_ref, tt_ref, lse_ref, w_ref, bias_ref, qs_ref, sems = refs[n_arrays:]
    step = pl.program_id(0)

    def copies(which):
        first = sum(len(p) for p in numbered[:which])
        return piece_copies(numbered[which], pieces, w_ref.at[which], sems, first)

    @pl.when(step == 0)
    def _():
        for which in range(3):
            for copy in copies(which):
                copy.start()

    x = tok_ref[...]
    tt_ref[...] = x.T
    seg = seg_ref[0:1, :]
    bias_ref[...] = jnp.where(column_of(seg) == seg, 0.0, -1e30)

    @pl.when(step == 0)
    def _():
        for which in range(3):
            for copy in copies(which):
                copy.wait()

    q = (dot(x, w_ref[0]) + vec_ref[0:1, :]).astype(BF)
    q_ref[...] = q
    qs_ref[...] = q * BF(1.0 / math.sqrt(HD))
    k_ref[...] = dot(x, w_ref[1]).astype(BF)
    v_ref[...] = (dot(x, w_ref[2]) + vec_ref[1:2, :]).astype(BF)
    lane = lax.broadcasted_iota(jnp.int32, (1, 2 * HD), 1)
    for pair in range(heads // 2):
        sl = slice(pair * 2 * HD, (pair + 1) * 2 * HD)
        queries, keys = qs_ref[:, sl], k_ref[:, sl]
        values_t = v_ref[:, sl].T
        outs = []
        for half in range(2):
            mine = (lane >= HD) if half else (lane < HD)
            scores = dot(jnp.where(mine, keys, BF(0)), queries, NT) + bias_ref[...]
            top = jnp.max(scores, axis=0, keepdims=True)
            weights = jnp.exp(scores - top)
            total = jnp.sum(weights, axis=0, keepdims=True)
            head = 2 * pair + half
            lse_ref[head : head + 1, :] = top + jnp.log(total)
            out = dot(values_t[half * HD : (half + 1) * HD], weights.astype(BF))
            outs.append(out * (1.0 / total))
        mt_ref[sl, :] = jnp.concatenate(outs, axis=0).astype(BF)


def attend(tokens, seg, vec, weights):
    count, width = tokens.shape
    rows = seg.shape[0] // 8
    slots = count // rows
    heads = width // HD
    padded = -(-heads // 8) * 8
    arrays, numbered = index_pieces(weights)
    row = pl.BlockSpec((slots, width), lambda i: (i, 0))
    col = pl.BlockSpec((width, slots), lambda i: (0, i))
    return pl.pallas_call(
        functools.partial(attend_kernel, numbered, len(arrays), heads),
        grid=(rows,),
        in_specs=[row, pl.BlockSpec((8, slots), lambda i: (i, 0)), whole(vec.shape)]
        + anywhere(len(arrays)),
        out_specs=[row, row, row, col, col, pl.BlockSpec((padded, slots), lambda i: (i, 0))],
        out_shape=[jax.ShapeDtypeStruct((count, width), BF)] * 3
        + [jax.ShapeDtypeStruct((width, count), BF)] * 2
        + [jax.ShapeDtypeStruct((rows * padded, slots), F32)],
        scratch_shapes=[
            pltpu.VMEM((3, width, width), BF),
            pltpu.VMEM((slots, slots), F32),
            pltpu.VMEM((slots, width), BF),
            pltpu.SemaphoreType.DMA((sum(len(p) for p in numbered),)),
        ],
        compiler_params=params(),
        cost_estimate=cost(2.2e10, 2e7),
        name="attend",
    )(tokens, seg, vec, *arrays)


def gelu_pair(v):
    u = jnp.abs(v)
    d = 1.0 + u * (0.3275911 * math.sqrt(0.5))
    t = pltpu.reciprocal(d, approx=True)
    t = t * (2.0 - d * t)
    e = jnp.exp(v * v * -0.5)
    poly = 0.5 * 1.061405429
    for c in (-1.453152027, 1.421413741, -0.284496736, 0.254829592):
        poly = poly * t + 0.5 * c
    tail = poly * t * e
    area = jnp.where(v >= 0, 1.0 - tail, tail)
    return v * area, area + v * e * (1.0 / math.sqrt(2.0 * math.pi))


def norm(z):
    center = z - jnp.mean(z, axis=-1, keepdims=True)
    scale = lax.rsqrt(jnp.mean(center * center, axis=-1, keepdims=True) + EPSILON)
    return center * scale, scale


def norm_back(grad, n, scale, gain):
    dn = grad * gain
    return (
        dn - jnp.mean(dn, axis=-1, keepdims=True) - n * jnp.mean(dn * n, axis=-1, keepdims=True)
    ) * scale


def column_sum(x):
    return jnp.sum(x.reshape(x.shape[0] // 8, 8, x.shape[1]), axis=0)


def feed_kernel(numbered, n_arrays, docs, mt_ref, tok_ref, cot_ref, seg_ref, vec_ref, bi_ref, *refs):
    pieces = refs[:n_arrays]
    (enc_ref, ht_ref, act_ref, dot_ref, din_ref, dfirst_ref, dbr_ref, dm_ref, sums_ref, sumi_ref) = refs[
        n_arrays : n_arrays + 10
    ]
    wo_ref, wi_ref, w2_ref, dg_ref, sems = refs[n_arrays + 10 :]
    targets = (wo_ref, wi_ref, w2_ref)
    step = pl.program_id(0)

    def copies(which):
        first = sum(len(p) for p in numbered[:which])
        return piece_copies(numbered[which], pieces, targets[which], sems, first)

    @pl.when(step == 0)
    def _():
        for which in range(3):
            for copy in copies(which):
                copy.start()
        sums_ref[...] = jnp.zeros_like(sums_ref)
        sumi_ref[...] = jnp.zeros_like(sumi_ref)
        for which in range(3):
            for copy in copies(which):
                copy.wait()

    vec = lambda i: vec_ref[i : i + 1, :]
    inner_width = wi_ref.shape[1]
    z1 = tok_ref[...].astype(F32) + dot(mt_ref[...].T, wo_ref[...]) + vec(2)
    n1, r1 = norm(z1)
    hidden = n1 * vec(4) + vec(5)
    hidden_low = hidden.astype(BF)
    ht_ref[...] = hidden_low.T
    total = hidden + vec(3)
    for c in range(0, inner_width, FF_CHUNK):
        sl = slice(c, c + FF_CHUNK)
        inner = dot(hidden_low, wi_ref[:, sl]) + bi_ref[:, sl]
        act, slope = gelu_pair(inner)
        act = act.astype(BF)
        act_ref[:, sl] = act
        dg_ref[:, sl] = slope
        total = total + dot(act, w2_ref[sl, :])
    n2, r2 = norm(total)
    enc_ref[...] = (n2 * vec(6) + vec(7)).astype(BF)
    grad = cot_ref[...] * column_of((seg_ref[0:1, :] < docs).astype(F32))
    d_second = norm_back(grad, n2, r2, vec(6))
    d_outer = d_second.astype(BF)
    dot_ref[...] = d_outer.T
    d_hidden = d_second
    for c in range(0, inner_width, FF_CHUNK):
        sl = slice(c, c + FF_CHUNK)
        d_inner = (dot(d_outer, w2_ref[sl, :], NT) * dg_ref[:, sl]).astype(BF)
        din_ref[:, sl] = d_inner
        sumi_ref[:, sl] += column_sum(d_inner.astype(F32))
        d_hidden = d_hidden + dot(d_inner, wi_ref[:, sl], NT)
    d_first = norm_back(d_hidden, n1, r1, vec(4))
    dfirst_ref[...] = d_first
    d_branch = d_first.astype(BF)
    dbr_ref[...] = d_branch
    dm_ref[...] = dot(d_branch, wo_ref[...], NT).astype(BF)
    for i, item in enumerate(
        (d_branch.astype(F32), d_outer.astype(F32), d_hidden * n1, d_hidden, grad * n2, grad)
    ):
        sums_ref[i] += column_sum(item)


def feed(mixed_t, tokens, cotangent, seg, vec, bias_inner, weights, docs):
    count, width = tokens.shape
    slots = seg.shape[1]
    inner_width = bias_inner.shape[1]
    arrays, numbered = index_pieces(weights)
    tile = ROW_TILE
    per_row = slots // tile
    row = pl.BlockSpec((tile, width), lambda i: (i, 0))
    wide = pl.BlockSpec((tile, inner_width), lambda i: (i, 0))
    col = pl.BlockSpec((width, tile), lambda i: (0, i))
    out = jax.ShapeDtypeStruct
    return pl.pallas_call(
        functools.partial(feed_kernel, numbered, len(arrays), docs),
        grid=(count // tile,),
        in_specs=[
            col,
            row,
            row,
            pl.BlockSpec((8, tile), lambda i: (i // per_row, i % per_row)),
            whole(vec.shape),
            whole(bias_inner.shape),
        ]
        + anywhere(len(arrays)),
        out_specs=[row, col, wide, col, wide, row, row, row]
        + [
            pl.BlockSpec((6, 8, width), lambda i: (0, 0, 0)),
            pl.BlockSpec((8, inner_width), lambda i: (0, 0)),
        ],
        out_shape=[
            out((count, width), BF),
            out((width, count), BF),
            out((count, inner_width), BF),
            out((width, count), BF),
            out((count, inner_width), BF),
            out((count, width), F32),
            out((count, width), BF),
            out((count, width), BF),
            out((6, 8, width), F32),
            out((8, inner_width), F32),
        ],
        scratch_shapes=[
            pltpu.VMEM((width, width), BF),
            pltpu.VMEM((width, inner_width), BF),
            pltpu.VMEM((inner_width, width), BF),
            pltpu.VMEM((tile, inner_width), F32),
            pltpu.SemaphoreType.DMA((sum(len(p) for p in numbered),)),
        ],
        compiler_params=params(),
        cost_estimate=cost(5e10, 4e7),
        name="feed",
    )(mixed_t, tokens, cotangent, seg, vec, bias_inner, *arrays)


def attend_back_kernel(heads, q_ref, k_ref, v_ref, dm_ref, lse_ref, seg_ref, dqkv_ref, sums_ref, bias_ref):
    @pl.when(pl.program_id(0) == 0)
    def _():
        sums_ref[...] = jnp.zeros_like(sums_ref)

    width = q_ref.shape[1]
    scale = 1.0 / math.sqrt(HD)
    seg = seg_ref[0:1, :]
    bias_ref[...] = jnp.where(column_of(seg) == seg, 0.0, -1e30)
    low_half = lax.broadcasted_iota(jnp.int32, (1, 2 * HD), 1) < HD
    for pair in range(heads // 2):
        first = pair * 2 * HD
        sl = slice(first, first + 2 * HD)
        queries = q_ref[:, sl] * BF(scale)
        keys, values, d_mixed = k_ref[:, sl], v_ref[:, sl], dm_ref[:, sl]
        keys_t = keys.T
        d_values, d_keys, d_queries = [], [], []
        for half in range(2):
            mine = jnp.logical_not(low_half) if half else low_half
            head = 2 * pair + half
            scores = dot(jnp.where(mine, keys, BF(0)), queries, NT) + bias_ref[...]
            probs = jnp.exp(scores - lse_ref[head : head + 1, :])
            d_probs = dot(jnp.where(mine, values, BF(0)), d_mixed, NT)
            weighted = probs * d_probs
            rows = jnp.sum(weighted, axis=0, keepdims=True)
            d_scores = (weighted - probs * rows).astype(BF)
            d_values.append(dot(probs.astype(BF), d_mixed))
            d_keys.append(dot(d_scores, queries))
            d_queries.append(dot(keys_t[half * HD : (half + 1) * HD], d_scores))
        d_query = (jnp.concatenate(d_queries, axis=0) * scale).astype(BF).T
        d_key = jnp.where(low_half, d_keys[0], d_keys[1]).astype(BF)
        d_value = jnp.where(low_half, d_values[0], d_values[1]).astype(BF)
        for i, item in enumerate((d_query, d_key, d_value)):
            dqkv_ref[:, i * width + first : i * width + first + 2 * HD] = item
        sums_ref[0, :, sl] += column_sum(d_query.astype(F32))
        sums_ref[1, :, sl] += column_sum(d_value.astype(F32))


def attend_back(query, keys, values, d_mixed, lse, seg):
    count, width = query.shape
    rows = seg.shape[0] // 8
    slots = seg.shape[1]
    heads = width // HD
    row = pl.BlockSpec((slots, width), lambda i: (i, 0))
    return pl.pallas_call(
        functools.partial(attend_back_kernel, heads),
        grid=(rows,),
        in_specs=[row] * 4
        + [
            pl.BlockSpec((lse.shape[0] // rows, slots), lambda i: (i, 0)),
            pl.BlockSpec((8, slots), lambda i: (i, 0)),
        ],
        out_specs=[
            pl.BlockSpec((slots, 3 * width), lambda i: (i, 0)),
            pl.BlockSpec((2, 8, width), lambda i: (0, 0, 0)),
        ],
        out_shape=[
            jax.ShapeDtypeStruct((count, 3 * width), BF),
            jax.ShapeDtypeStruct((2, 8, width), F32),
        ],
        scratch_shapes=[pltpu.VMEM((slots, slots), F32)],
        compiler_params=params(),
        cost_estimate=cost(2.2e10, 2e7),
        name="attend_back",
    )(query, keys, values, d_mixed, lse, seg)


def tokens_kernel(numbered, n_arrays, dfirst_ref, dqkv_ref, *refs):
    pieces = refs[:n_arrays]
    out_ref, w_ref, sems = refs[n_arrays:]
    width = dfirst_ref.shape[1]

    @pl.when(pl.program_id(0) == 0)
    def _():
        every = []
        for which in range(3):
            first = sum(len(p) for p in numbered[:which])
            every += piece_copies(numbered[which], pieces, w_ref.at[which], sems, first)
        for copy in every:
            copy.start()
        for copy in every:
            copy.wait()

    total = dfirst_ref[...]
    for which in range(3):
        total = total + dot(dqkv_ref[:, which * width : (which + 1) * width], w_ref[which], NT)
    out_ref[...] = total


def tokens_back(d_first, dqkv, weights):
    count, width = d_first.shape
    arrays, numbered = index_pieces(weights)
    tile = ROW_TILE
    return pl.pallas_call(
        functools.partial(tokens_kernel, numbered, len(arrays)),
        grid=(count // tile,),
        in_specs=[
            pl.BlockSpec((tile, width), lambda i: (i, 0)),
            pl.BlockSpec((tile, 3 * width), lambda i: (i, 0)),
        ]
        + anywhere(len(arrays)),
        out_specs=pl.BlockSpec((tile, width), lambda i: (i, 0)),
        out_shape=jax.ShapeDtypeStruct((count, width), F32),
        scratch_shapes=[
            pltpu.VMEM((3, width, width), BF),
            pltpu.SemaphoreType.DMA((sum(len(p) for p in numbered),)),
        ],
        compiler_params=params(),
        cost_estimate=cost(3.6e9, 1.5e7),
        name="tokens_back",
    )(d_first, dqkv, *arrays)


def rows_kernel(order, chunks, *refs):
    n = len(chunks)
    lefts, rights = refs[:n], refs[n : 2 * n]
    outs, acc_ref = refs[2 * n : -1], refs[-1]
    step = pl.program_id(0)
    first = 0
    for left, right, count in zip(lefts, rights, chunks):

        @pl.when((step >= first) & (step < first + count))
        def _():
            acc_ref[...] = dot(left[...], right[...])

        first += count
    if order is None:
        outs[0][0] = acc_ref[...].astype(BF)
        return
    me = lax.axis_index("fsdp")
    size = outs[0].shape[1]
    for out, core in zip(outs, (0, CORE)):
        for place, rel in enumerate(order):
            start = pl.multiple_of((me ^ (rel | core)) * size, size)
            out[place] = acc_ref[pl.ds(start, size), :].astype(BF)


def rows_grad(products, order, shards, chunk=768):
    height, depth = products[0][0].shape
    spans = [(right.shape[1] if stop is None else stop - start, start) for _, right, start, stop in products]
    chunks = [span // chunk for span, _ in spans]
    firsts = [sum(chunks[:i]) for i in range(len(chunks))]

    def right_spec(i):
        offset = spans[i][1] // chunk

        def index(g):
            return (0, offset + jnp.clip(g - firsts[i], 0, chunks[i] - 1))

        return pl.BlockSpec((depth, chunk), index)

    total = chunk * sum(chunks)
    if order is None:
        blocks = [(1, height)]
    else:
        blocks = [(len(order), height // shards)] * 2
    got = pl.pallas_call(
        functools.partial(rows_kernel, order, chunks),
        grid=(sum(chunks),),
        in_specs=[whole((height, depth)) for _ in products]
        + [right_spec(i) for i in range(len(products))],
        out_specs=[pl.BlockSpec((*b, chunk), lambda g: (0, 0, g)) for b in blocks],
        out_shape=[jax.ShapeDtypeStruct((*b, total), BF) for b in blocks],
        scratch_shapes=[pltpu.VMEM((height, chunk), F32)],
        compiler_params=params(),
        cost_estimate=cost(2 * height * depth * total, 2 * depth * total + 2 * height * total),
        name="rows_grad",
    )(*[p[0] for p in products], *[p[1] for p in products])
    return got


def columns_kernel(left_ref, right_ref, out_ref):
    out_ref[0] = dot(left_ref[...], right_ref[...]).astype(BF)


def columns_grad(left, right, order, shards):
    height, depth = left.shape
    size = right.shape[1] // shards
    if order is None:
        size, order = right.shape[1] // 8, None
    count = 8 if order is None else len(order)

    def rel_of(g):
        if order is None:
            return g
        rel = jnp.int32(order[-1])
        for place, item in enumerate(order[:-1]):
            rel = jnp.where(g == place, jnp.int32(item), rel)
        return lax.axis_index("fsdp") ^ rel

    if order is None:
        index, shape, out_index = (lambda g: (0, g)), (1, height, 8 * size), (lambda g: (0, 0, g))
        pieces = None
    else:
        index, shape, out_index = None, (count, height, size), (lambda g, p: (g, 0, 0))
        pieces = jnp.stack([lax.axis_index("fsdp") ^ rel for rel in order]).astype(jnp.int32)
    common = dict(
        out_shape=jax.ShapeDtypeStruct(shape, BF),
        compiler_params=params(),
        cost_estimate=cost(2 * height * depth * size * count, 4 * depth * size * count),
        name="columns_grad",
    )
    if pieces is None:
        return pl.pallas_call(
            columns_kernel,
            grid=(count,),
            in_specs=[whole((height, depth)), pl.BlockSpec((depth, size), index)],
            out_specs=pl.BlockSpec((1, height, size), out_index),
            **common,
        )(left, right)
    return pl.pallas_call(
        lambda p, *refs: columns_kernel(*refs),
        grid_spec=pltpu.PrefetchScalarGridSpec(
            num_scalar_prefetch=1,
            grid=(count,),
            in_specs=[
                pl.BlockSpec((height, depth), lambda g, p: (0, 0), pipeline_mode=pl.Buffered(1)),
                pl.BlockSpec((depth, size), lambda g, p: (0, p[g])),
            ],
            out_specs=pl.BlockSpec((1, height, size), out_index),
        ),
        **common,
    )(pieces, left, right)


def up(x):
    return x.astype(F32)


def scatter_sum(keep, send, first, second):
    cores = flip(send, "fsdp", CORE)
    far = flip((up(keep[2:]) + up(cores[2:])).astype(BF), "fsdp", first)
    near = flip((up(keep[1]) + up(cores[1]) + up(far[1])).astype(BF), "fsdp", second)
    return up(keep[0]) + up(cores[0]) + up(far[0]) + up(near)


def rep_sum(total):
    n = lax.axis_size("rep")
    rows = total.shape[0]
    if n & (n - 1) or rows % n:
        return up(lax.psum(total.astype(BF), "rep"))
    me = lax.axis_index("rep")
    low = total.astype(BF).reshape(n, rows // n, total.shape[1])
    part = lambda k: lax.dynamic_index_in_dim(low, me ^ k, 0, keepdims=False)
    mine = up(part(0))
    for k in range(1, n):
        mine = mine + up(flip(part(k), "rep", k))
    mine = mine.astype(BF)
    parts = [mine] + [flip(mine, "rep", k) for k in range(1, n)]
    bit = 1
    while bit < n:
        odd = (me & bit) > 0
        parts = [jnp.where(odd, parts[k ^ bit], parts[k]) for k in range(n)]
        bit *= 2
    return up(jnp.concatenate(parts, axis=0))


def all_sum(values):
    for axis in ("fsdp", "rep"):
        n = lax.axis_size(axis)
        if n & (n - 1):
            values = lax.psum(values, axis)
            continue
        bit = 1
        while bit < n:
            values = values + flip(values, axis, bit)
            bit *= 2
    return values


def body(
    tokens,
    doc_lengths,
    query_weight,
    key_weight,
    value_weight,
    output_weight,
    inner_weight,
    outer_weight,
    query_bias,
    value_bias,
    output_bias,
    inner_bias,
    outer_bias,
    first_gain,
    first_shift,
    second_gain,
    second_shift,
    cotangent,
):
    rows, slots, width = tokens.shape
    count = rows * slots
    docs = doc_lengths.shape[1]
    n_fsdp = lax.axis_size("fsdp")
    n_rep = lax.axis_size("rep")
    shard = query_weight.shape[0]
    outer_shard = outer_weight.shape[0]
    inner_width = inner_weight.shape[1]
    direct = n_fsdp == 8 and shard % 16 == 0

    if direct:
        qw, kw, vw, ow = gather_pair(
            jnp.concatenate([query_weight, key_weight], axis=0),
            jnp.concatenate([value_weight, output_weight], axis=0),
            (shard, shard),
            (shard, shard),
        )
        iw, w2 = gather_pair(inner_weight, outer_weight, (shard,), (outer_shard,))
    else:
        qw, kw, vw, ow, iw, w2 = [
            [(lax.all_gather(w, "fsdp", axis=0, tiled=True), 0, w.shape[0] * n_fsdp, None)]
            for w in (query_weight, key_weight, value_weight, output_weight, inner_weight, outer_weight)
        ]
    small = jnp.concatenate(
        [
            query_bias,
            value_bias,
            output_bias,
            outer_bias,
            first_gain,
            first_shift,
            second_gain,
            second_shift,
            inner_bias,
        ]
    )
    small = lax.all_gather(small[None], "fsdp", axis=0, tiled=True).astype(F32)
    vec = small[:, : 8 * shard].reshape(n_fsdp, 8, shard).transpose(1, 0, 2).reshape(8, width)
    bias_inner = small[:, 8 * shard :].reshape(1, inner_width)

    places = jnp.arange(docs, dtype=jnp.int32)
    ends = jnp.sum(
        jnp.where(places[None, :, None] >= places[None, None, :], doc_lengths[:, None, :], 0), axis=-1
    )
    slot = jnp.arange(slots, dtype=jnp.int32)
    segment = jnp.sum((slot[None, None, :] >= ends[:, :, None]).astype(jnp.int32), axis=1)
    seg = jnp.broadcast_to(segment[:, None, :].astype(F32), (rows, 8, slots)).reshape(rows * 8, slots)

    flat = tokens.reshape(count, width)
    query, keys, values, mixed_t, tokens_t, lse = attend(flat, seg, vec, (qw, kw, vw))
    encoded, hidden_t, activated, d_outer_t, d_inner, d_first, d_branch, d_mixed, sums, sums_inner = feed(
        mixed_t, flat, cotangent.reshape(count, width), seg, vec, bias_inner, (ow, iw, w2), docs
    )
    order_xy, order_yx = ((0, Y, X, X | Y), (0, X, Y, X | Y)) if direct else (None, None)
    wide = [(hidden_t, d_inner, 0, None), (mixed_t, d_branch, 0, None)]
    if direct:
        outer_send = columns_grad(d_outer_t, activated, [r | CORE for r in order_yx], n_fsdp)
        outer_keep = columns_grad(d_outer_t, activated, order_yx, n_fsdp)
        outer_sum = scatter_sum(outer_keep, outer_send, Y, X)
        inner_sum = scatter_sum(*rows_grad(wide, order_xy, n_fsdp), X, Y)
    else:
        outer_sum = up(
            lax.psum_scatter(
                columns_grad(d_outer_t, activated, None, 8)[0], "fsdp", scatter_dimension=1, tiled=True
            )
        )
        inner_sum = up(
            lax.psum_scatter(rows_grad(wide, None, 1)[0][0], "fsdp", scatter_dimension=0, tiled=True)
        )
    dqkv, sums_qv = attend_back(query, keys, values, d_mixed, lse, seg)
    if direct:
        q_sum = scatter_sum(*rows_grad([(tokens_t, dqkv, 0, width)], order_xy, n_fsdp), X, Y)
        kv_sum = scatter_sum(*rows_grad([(tokens_t, dqkv, width, 3 * width)], order_yx, n_fsdp), Y, X)
    else:
        qkv_sum = up(
            lax.psum_scatter(
                rows_grad([(tokens_t, dqkv, 0, None)], None, 1)[0][0],
                "fsdp",
                scatter_dimension=0,
                tiled=True,
            )
        )
        q_sum, kv_sum = qkv_sum[:, :width], qkv_sum[:, width:]
    tokens_grad = tokens_back(d_first, dqkv, (qw, kw, vw))

    factor = 1.0 / math.sqrt(rows * n_rep * n_fsdp * slots)
    outer_all = rep_sum(outer_sum) * factor
    inner_all = rep_sum(inner_sum) * factor
    q_all = rep_sum(q_sum) * factor
    kv_all = rep_sum(kv_sum) * factor
    vectors = jnp.concatenate(
        [
            jnp.sum(sums_qv, axis=1),
            jnp.sum(sums, axis=1),
            jnp.sum(sums_inner, axis=0).reshape(inner_width // width, width),
        ],
        axis=0,
    )
    vectors = all_sum(vectors) * factor
    me = lax.axis_index("fsdp")
    short = lax.dynamic_slice_in_dim(vectors[:8], me * shard, shard, axis=1)
    long = lax.dynamic_slice_in_dim(vectors[8:].reshape(inner_width), me * outer_shard, outer_shard, axis=0)
    return (
        encoded.reshape(rows, slots, width),
        tokens_grad.reshape(rows, slots, width),
        q_all,
        kv_all[:, :width],
        kv_all[:, width:],
        inner_all[:, inner_width:],
        inner_all[:, :inner_width],
        outer_all.T,
        short[0],
        short[1],
        short[2],
        long,
        short[3],
        short[4],
        short[5],
        short[6],
        short[7],
    )


def solution(mesh):
    data = P(("rep", "fsdp"), None, None)
    matrix, vector = P("fsdp", None), P("fsdp")
    return jax.shard_map(
        body,
        mesh=mesh,
        in_specs=(data, P(("rep", "fsdp"), None)) + (matrix,) * 6 + (vector,) * 9 + (data,),
        out_specs=(data, data) + (matrix,) * 6 + (vector,) * 9,
        check_vma=False,
    )
```

```python
import functools
import math

import jax
import jax.numpy as jnp
from jax import lax
from jax.experimental import pallas as pl
from jax.experimental.pallas import tpu as pltpu
from jax.sharding import PartitionSpec as P

HD = 64
EPSILON = 1e-05
BF = jnp.bfloat16
F32 = jnp.float32
NT = ((1,), (1,))
VMEM_BYTES = 60 * 2**20
CORE, X, Y = 1, 2, 4
ROW_TILE = 256
FF_CHUNK = 768


def dot(a, b, dims=((1,), (0,))):
    return lax.dot_general(a, b, (dims, ((), ())), preferred_element_type=F32)


def params():
    return pltpu.CompilerParams(
        vmem_limit_bytes=VMEM_BYTES, dimension_semantics=("arbitrary",)
    )


def cost(flops, nbytes, trans=0):
    return pl.CostEstimate(
        flops=int(flops), bytes_accessed=int(nbytes), transcendentals=int(trans)
    )


def whole(shape):
    return pl.BlockSpec(
        shape, lambda *i: (0,) * len(shape), pipeline_mode=pl.Buffered(1)
    )


def anywhere(count):
    return [pl.BlockSpec(memory_space=pl.ANY)] * count


def flip(array, axis, bit):
    size = lax.axis_size(axis)
    return lax.ppermute(array, axis, [(i, i ^ bit) for i in range(size)])


def piece_copies(pieces, refs, target, sems, first):
    copies = []
    for slot, (which, start, rows, rel, shard, offset, column) in enumerate(pieces):
        place = 0
        if rel is not None:
            place = pl.multiple_of((lax.axis_index("fsdp") ^ rel) * shard + offset, math.gcd(shard, offset))
        copies.append(
            pltpu.make_async_copy(
                refs[which].at[pl.ds(start, rows), pl.ds(column, target.shape[1])],
                target.at[pl.ds(place, rows), :],
                sems.at[first + slot],
            )
        )
    return copies


def group_copies(numbered, refs, targets, sems):
    copies = []
    for pieces, target in zip(numbered, targets):
        copies.append(piece_copies(pieces, refs, target, sems, sum(len(c) for c in copies)))
    return copies


def index_pieces(weights):
    arrays, numbered = [], []
    for pieces in weights:
        mine = []
        for array, *rest in pieces:
            for n, seen in enumerate(arrays):
                if seen is array:
                    break
            else:
                n = len(arrays)
                arrays.append(array)
            mine.append((n, *rest))
        numbered.append(mine)
    return arrays, numbered


class Gather:
    def __init__(self, block, first, second):
        self.rows, self.bits, self.block = block.shape[0], (first, second), block
        self.got = flip(block, "fsdp", first)

    def far(self, zero=None):
        self.pair = with_zero(jnp.concatenate([self.block, self.got], axis=0), zero)
        self.got = flip(self.pair, "fsdp", self.bits[1])
        return self.pair

    def held(self, zero=None):
        first, second = self.bits
        chips = with_zero(jnp.concatenate([self.pair, self.got], axis=0), zero)
        cores = flip(chips, "fsdp", CORE)
        rels = (0, first, second, first | second)
        return [
            (array, place * self.rows, rel | core)
            for core, array in ((0, chips), (CORE, cores))
            for place, rel in enumerate(rels)
        ]


def with_zero(array, zero):
    return array if zero is None else array + zero.reshape(()).astype(array.dtype)


def pack_kernel(half, query_ref, key_ref, value_ref, *refs):
    vectors, (one_ref, two_ref) = refs[:-2], refs[-2:]
    shard, width = query_ref.shape
    one_ref[:shard, :] = query_ref[...]
    one_ref[shard : shard + half, :] = key_ref[:half, :]
    two_ref[:shard, :] = value_ref[...]
    two_ref[shard:, :] = key_ref[half:, :]
    rows = []
    for ref in vectors:
        size = ref.shape[0]
        rows.append(
            jnp.concatenate([ref[...].astype(F32).reshape(1, size), jnp.zeros((1, width - size), F32)], axis=1)
        )
    rows.append(jnp.zeros((16 - len(rows), width), F32))
    one_ref[shard + half :, :] = jnp.concatenate(rows, axis=0).astype(BF)


def pack(query, key, value, vectors):
    shard, width = query.shape
    half = shard // 2
    return pl.pallas_call(
        functools.partial(pack_kernel, half),
        out_shape=[
            jax.ShapeDtypeStruct((shard + half + 16, width), BF),
            jax.ShapeDtypeStruct((shard + half, width), BF),
        ],
        name="pack",
    )(query, key, value, *vectors)


def unpack_kernel(numbered, n_arrays, shard, long, *refs):
    pieces = refs[:n_arrays]
    vec_ref, inner_ref, held_ref, sems = refs[n_arrays:]
    copies = piece_copies(numbered[0], pieces, held_ref, sems, 0)
    for copy in copies:
        copy.start()
    for copy in copies:
        copy.wait()
    n = len(copies)
    parts = [held_ref[16 * i : 16 * i + 16, :] for i in range(n)]
    slot = lax.broadcasted_iota(jnp.int32, (n * 128, n * shard), 0)
    place = lax.broadcasted_iota(jnp.int32, (n * 128, n * shard), 1)
    at = slot % 128
    spread = ((at < shard) & (place == slot // 128 * shard + at)).astype(BF)
    vec_ref[...] = dot(jnp.concatenate([p[:, :128] for p in parts], axis=1), spread)[:8]
    for i, p in enumerate(parts):
        inner_ref[:, i * long : (i + 1) * long] = p[8:9, :long].astype(F32)


def unpack(pieces, shard, long):
    arrays, numbered = index_pieces([pieces])
    n, width = len(pieces), pieces[0][0].shape[1]
    return pl.pallas_call(
        functools.partial(unpack_kernel, numbered, len(arrays), shard, long),
        in_specs=anywhere(len(arrays)),
        out_shape=[
            jax.ShapeDtypeStruct((8, n * shard), F32),
            jax.ShapeDtypeStruct((1, n * long), F32),
        ],
        scratch_shapes=[pltpu.VMEM((16 * n, width), BF), pltpu.SemaphoreType.DMA((n,))],
        name="unpack",
    )(*arrays)


def part(held, start, rows, shard, offset=0):
    return [(a, at + start, rows, rel, shard, offset, 0) for a, at, rel in held]


def zero_out():
    return pl.BlockSpec(memory_space=pltpu.SMEM), jax.ShapeDtypeStruct((1, 1), F32)


def column_of(row):
    return jnp.broadcast_to(row, (128, row.shape[1])).T[:, :1]


def split_lanes(pair):
    low = lax.broadcasted_iota(jnp.int32, (1, 2 * HD), 1) < HD
    return jnp.concatenate([jnp.where(low, pair, BF(0)), jnp.where(low, BF(0), pair)], axis=0)


def split_rows(pair_t):
    low = lax.broadcasted_iota(jnp.int32, (2 * HD, 1), 0) < HD
    return jnp.concatenate([jnp.where(low, pair_t, BF(0)), jnp.where(low, BF(0), pair_t)], axis=1)


def attend_kernel(numbered, n_arrays, n_after, heads, tok_ref, seg_ref, vec_ref, *refs):
    pieces = refs[:n_arrays]
    q_ref, k_ref, v_ref, mt_ref, tt_ref, lse_ref, zero_ref, w_ref, bias_ref, qs_ref, sems = refs[n_arrays + n_after :]
    zero_ref[0, 0] = 0.0
    ready = load_weights(numbered, pieces, [w_ref.at[which] for which in range(3)], sems)
    x = tok_ref[...]
    tt_ref[...] = x.T
    seg = seg_ref[0:1, :]
    bias_ref[...] = jnp.where(column_of(seg) == seg, 0.0, -1e30)

    for which in range(3):
        ready(which)
    q = (dot(x, w_ref[0]) + vec_ref[0:1, :]).astype(BF)
    q_ref[...] = q
    qs_ref[...] = q * BF(1.0 / math.sqrt(HD))
    k_ref[...] = dot(x, w_ref[1]).astype(BF)
    v_ref[...] = (dot(x, w_ref[2]) + vec_ref[1:2, :]).astype(BF)
    for pair in range(heads // 2):
        sl = slice(pair * 2 * HD, (pair + 1) * 2 * HD)
        scores = dot(split_lanes(k_ref[:, sl]), qs_ref[:, sl], NT)
        slots = scores.shape[0] // 2
        weights, inverse = [], []
        for half in range(2):
            mine = scores[half * slots : (half + 1) * slots] + bias_ref[...]
            top = jnp.max(mine, axis=0, keepdims=True)
            exps = jnp.exp(mine - top)
            total = jnp.sum(exps, axis=0, keepdims=True)
            head = 2 * pair + half
            lse_ref[head : head + 1, :] = top + jnp.log(total)
            weights.append(exps.astype(BF))
            inverse.append(1.0 / total)
        out = dot(split_rows(v_ref[:, sl].T), jnp.concatenate(weights, axis=0))
        low_rows = lax.broadcasted_iota(jnp.int32, (2 * HD, 1), 0) < HD
        mt_ref[sl, :] = (out * jnp.where(low_rows, inverse[0], inverse[1])).astype(BF)


def attend(tokens, seg, vec, weights, after=()):
    count, width = tokens.shape
    rows = seg.shape[0] // 8
    slots = count // rows
    heads = width // HD
    padded = -(-heads // 8) * 8
    arrays, numbered = index_pieces(weights)
    row = pl.BlockSpec((slots, width), lambda i: (i, 0))
    col = pl.BlockSpec((width, slots), lambda i: (0, i))
    zero_spec, zero_shape = zero_out()
    return pl.pallas_call(
        functools.partial(attend_kernel, numbered, len(arrays), len(after), heads),
        grid=(rows,),
        in_specs=[row, pl.BlockSpec((8, slots), lambda i: (i, 0)), whole(vec.shape)]
        + anywhere(len(arrays) + len(after)),
        out_specs=[row, row, row, col, col, pl.BlockSpec((padded, slots), lambda i: (i, 0)), zero_spec],
        out_shape=[jax.ShapeDtypeStruct((count, width), BF)] * 3
        + [jax.ShapeDtypeStruct((width, count), BF)] * 2
        + [jax.ShapeDtypeStruct((rows * padded, slots), F32), zero_shape],
        scratch_shapes=[
            pltpu.VMEM((3, width, width), BF),
            pltpu.VMEM((slots, slots), F32),
            pltpu.VMEM((slots, width), BF),
            pltpu.SemaphoreType.DMA((sum(len(p) for p in numbered),)),
        ],
        compiler_params=params(),
        cost_estimate=cost(2.2e10, 2e7),
        name="attend",
    )(tokens, seg, vec, *arrays, *after)


def gelu_pair(v):
    area = 0.5 + 0.5 * lax.erf(v * math.sqrt(0.5))
    density = jnp.exp2(v * v * (-0.5 / math.log(2.0))) * (1.0 / math.sqrt(2.0 * math.pi))
    return v * area, area + v * density


def norm(z):
    center = z - jnp.mean(z, axis=-1, keepdims=True)
    scale = lax.rsqrt(jnp.mean(center * center, axis=-1, keepdims=True) + EPSILON)
    return center * scale, scale


def norm_back(grad, n, scale, gain):
    dn = grad * gain
    return (
        dn - jnp.mean(dn, axis=-1, keepdims=True) - n * jnp.mean(dn * n, axis=-1, keepdims=True)
    ) * scale


def column_sum(x):
    return jnp.sum(x.reshape(x.shape[0] // 8, 8, x.shape[1]), axis=0)


def load_weights(numbered, pieces, targets, sems):
    groups = group_copies(numbered, pieces, targets, sems)
    first_step = pl.program_id(0) == 0

    @pl.when(first_step)
    def _():
        for copies in groups:
            for copy in copies:
                copy.start()

    def ready(which):
        @pl.when(first_step)
        def _():
            for copy in groups[which]:
                copy.wait()

    return ready


def vector(vec_ref, i):
    return vec_ref[i : i + 1, :]


def inner_kernel(numbered, n_arrays, n_after, mt_ref, tok_ref, vec_ref, bi_ref, *refs):
    pieces = refs[:n_arrays]
    ht_ref, n1_ref, r1_ref, act_ref, dg_ref, zero_ref, wo_ref, wi_ref, sems = refs[n_arrays + n_after :]
    zero_ref[0, 0] = 0.0

    ready = load_weights(numbered, pieces, (wo_ref, wi_ref), sems)
    ready(0)
    z1 = tok_ref[...].astype(F32) + dot(mt_ref[...].T, wo_ref[...]) + vector(vec_ref, 2)
    n1, r1 = norm(z1)
    n1_ref[...] = n1
    r1_ref[...] = jnp.broadcast_to(r1, r1_ref.shape)
    hidden = (n1 * vector(vec_ref, 4) + vector(vec_ref, 5)).astype(BF)
    ht_ref[...] = hidden.T
    ready(1)
    for c in range(0, wi_ref.shape[1], FF_CHUNK):
        sl = slice(c, c + FF_CHUNK)
        act, slope = gelu_pair(dot(hidden, wi_ref[:, sl]) + bi_ref[:, sl])
        act_ref[:, sl] = act.astype(BF)
        dg_ref[:, sl] = slope.astype(BF)


def outer_kernel(
    numbered, n_arrays, n_after, docs, n1_ref, act_ref, dg_ref, cot_ref, seg_ref, vec_ref, *refs
):
    pieces = refs[:n_arrays]
    enc_ref, dot_ref, dsecond_ref, din_ref, sums_ref, sumi_ref, w2_ref, sems = refs[n_arrays + n_after :]
    ready = load_weights(numbered, pieces, (w2_ref,), sems)

    @pl.when(pl.program_id(0) == 0)
    def _():
        sums_ref[...] = jnp.zeros_like(sums_ref)
        sumi_ref[...] = jnp.zeros_like(sumi_ref)

    hidden = n1_ref[...] * vector(vec_ref, 4) + vector(vec_ref, 5)
    ready(0)
    n2, r2 = norm(hidden + dot(act_ref[...], w2_ref[...]) + vector(vec_ref, 3))
    gain = vector(vec_ref, 6)
    enc_ref[...] = (n2 * gain + vector(vec_ref, 7)).astype(BF)
    grad = cot_ref[...] * column_of((seg_ref[0:1, :] < docs).astype(F32))
    d_second = norm_back(grad, n2, r2, gain)
    dsecond_ref[...] = d_second
    d_outer = d_second.astype(BF)
    dot_ref[...] = d_outer.T
    for i, item in enumerate((d_outer.astype(F32), grad * n2, grad)):
        sums_ref[i] += column_sum(item)
    for c in range(0, w2_ref.shape[0], 2 * FF_CHUNK):
        sl = slice(c, c + 2 * FF_CHUNK)
        d_inner = (dot(d_outer, w2_ref[sl, :], NT) * dg_ref[:, sl].astype(F32)).astype(BF)
        din_ref[:, sl] = d_inner
        sumi_ref[:, sl] += column_sum(d_inner.astype(F32))


def hidden_kernel(numbered, n_arrays, n_after, din_ref, dsecond_ref, n1_ref, r1_ref, vec_ref, *refs):
    pieces = refs[:n_arrays]
    dfirst_ref, dbr_ref, dm_ref, sums_ref, zero_ref, wi_ref, wo_ref, sems = refs[n_arrays + n_after :]
    zero_ref[0, 0] = 0.0
    ready = load_weights(numbered, pieces, (wi_ref, wo_ref), sems)

    @pl.when(pl.program_id(0) == 0)
    def _():
        sums_ref[...] = jnp.zeros_like(sums_ref)

    ready(0)
    d_hidden = dsecond_ref[...] + dot(din_ref[...], wi_ref[...], NT)
    n1 = n1_ref[...]
    d_first = norm_back(d_hidden, n1, r1_ref[:, :1], vector(vec_ref, 4))
    dfirst_ref[...] = d_first
    d_branch = d_first.astype(BF)
    dbr_ref[...] = d_branch
    ready(1)
    dm_ref[...] = dot(d_branch, wo_ref[...], NT).astype(BF)
    for i, item in enumerate((d_branch.astype(F32), d_hidden * n1, d_hidden)):
        sums_ref[i] += column_sum(item)


def tiled(count, width, wide):
    tile = ROW_TILE
    return (
        tile,
        pl.BlockSpec((tile, width), lambda i: (i, 0)),
        pl.BlockSpec((width, tile), lambda i: (0, i)),
        pl.BlockSpec((tile, wide), lambda i: (i, 0)),
    )


def sums_of(n, width):
    return pl.BlockSpec((n, 8, width), lambda i: (0, 0, 0)), jax.ShapeDtypeStruct((n, 8, width), F32)


def feed_inner(mixed_t, tokens, vec, bias_inner, weights, after=()):
    count, width = tokens.shape
    inner_width = bias_inner.shape[1]
    arrays, numbered = index_pieces(weights)
    tile, row, col, wide = tiled(count, width, inner_width)
    out = jax.ShapeDtypeStruct
    zero_spec, zero_shape = zero_out()
    return pl.pallas_call(
        functools.partial(inner_kernel, numbered, len(arrays), len(after)),
        grid=(count // tile,),
        in_specs=[col, row, whole(vec.shape), whole(bias_inner.shape)] + anywhere(len(arrays) + len(after)),
        out_specs=[col, row, pl.BlockSpec((tile, 128), lambda i: (i, 0)), wide, wide, zero_spec],
        out_shape=[
            out((width, count), BF),
            out((count, width), F32),
            out((count, 128), F32),
            out((count, inner_width), BF),
            out((count, inner_width), BF),
            zero_shape,
        ],
        scratch_shapes=[
            pltpu.VMEM((width, width), BF),
            pltpu.VMEM((width, inner_width), BF),
            pltpu.SemaphoreType.DMA((sum(len(p) for p in numbered),)),
        ],
        compiler_params=params(),
        cost_estimate=cost(2e10, 4e7),
        name="feed_inner",
    )(mixed_t, tokens, vec, bias_inner, *arrays, *after)


def feed_outer(n1, act, slope, cotangent, seg, vec, weights, docs, after=()):
    count, width = n1.shape
    inner_width = act.shape[1]
    arrays, numbered = index_pieces(weights)
    tile, row, col, wide = tiled(count, width, inner_width)
    per_row = seg.shape[1] // tile
    out = jax.ShapeDtypeStruct
    sums_spec, sums_shape = sums_of(3, width)
    return pl.pallas_call(
        functools.partial(outer_kernel, numbered, len(arrays), len(after), docs),
        grid=(count // tile,),
        in_specs=[row, wide, wide, row, pl.BlockSpec((8, tile), lambda i: (i // per_row, i % per_row))]
        + [whole(vec.shape)]
        + anywhere(len(arrays) + len(after)),
        out_specs=[row, col, row, wide, sums_spec, pl.BlockSpec((8, inner_width), lambda i: (0, 0))],
        out_shape=[
            out((count, width), BF),
            out((width, count), BF),
            out((count, width), F32),
            out((count, inner_width), BF),
            sums_shape,
            out((8, inner_width), F32),
        ],
        scratch_shapes=[
            pltpu.VMEM((inner_width, width), BF),
            pltpu.SemaphoreType.DMA((sum(len(p) for p in numbered),)),
        ],
        compiler_params=params(),
        cost_estimate=cost(1.8e10, 4e7),
        name="feed_outer",
    )(n1, act, slope, cotangent, seg, vec, *arrays, *after)


def feed_hidden(d_inner, d_second, n1, r1, vec, weights, after=()):
    count, width = n1.shape
    inner_width = d_inner.shape[1]
    arrays, numbered = index_pieces(weights)
    tile, row, _, wide = tiled(count, width, inner_width)
    out = jax.ShapeDtypeStruct
    zero_spec, zero_shape = zero_out()
    sums_spec, sums_shape = sums_of(3, width)
    return pl.pallas_call(
        functools.partial(hidden_kernel, numbered, len(arrays), len(after)),
        grid=(count // tile,),
        in_specs=[wide, row, row, pl.BlockSpec((tile, 128), lambda i: (i, 0)), whole(vec.shape)]
        + anywhere(len(arrays) + len(after)),
        out_specs=[row, row, row, sums_spec, zero_spec],
        out_shape=[out((count, width), F32), out((count, width), BF), out((count, width), BF), sums_shape, zero_shape],
        scratch_shapes=[
            pltpu.VMEM((width, inner_width), BF),
            pltpu.VMEM((width, width), BF),
            pltpu.SemaphoreType.DMA((sum(len(p) for p in numbered),)),
        ],
        compiler_params=params(),
        cost_estimate=cost(1.2e10, 3e7),
        name="feed_hidden",
    )(d_inner, d_second, n1, r1, vec, *arrays, *after)


def attend_back_kernel(first_head, n_after, q_ref, k_ref, v_ref, dm_ref, lse_ref, seg_ref, *refs):
    dqkv_ref, sums_ref, zero_ref, bias_ref = refs[n_after:]
    zero_ref[0, 0] = 0.0

    @pl.when(pl.program_id(0) == 0)
    def _():
        sums_ref[...] = jnp.zeros_like(sums_ref)

    width = q_ref.shape[1]
    scale = 1.0 / math.sqrt(HD)
    seg = seg_ref[0:1, :]
    bias_ref[...] = jnp.where(column_of(seg) == seg, 0.0, -1e30)
    low = lax.broadcasted_iota(jnp.int32, (1, 2 * HD), 1) < HD
    slots = q_ref.shape[0]
    halves = lambda a: (a[:slots], a[slots:])
    for pair in range(width // (2 * HD)):
        first = pair * 2 * HD
        sl = slice(first, first + 2 * HD)
        queries = q_ref[:, sl] * BF(scale)
        keys, d_mixed = k_ref[:, sl], dm_ref[:, sl]
        scores = halves(dot(split_lanes(keys), queries, NT))
        d_probs = halves(dot(split_lanes(v_ref[:, sl]), d_mixed, NT))
        probs_low, d_scores = [], []
        for half in range(2):
            head = first_head + 2 * pair + half
            probs = jnp.exp(scores[half] + bias_ref[...] - lse_ref[head : head + 1, :])
            probs_low.append(probs.astype(BF))
            weighted = probs * d_probs[half]
            rows = jnp.sum(weighted, axis=0, keepdims=True)
            d_scores.append((weighted - probs * rows).astype(BF))
        d_scores = jnp.concatenate(d_scores, axis=0)
        d_value = jnp.where(low, *halves(dot(jnp.concatenate(probs_low, axis=0), d_mixed))).astype(BF)
        d_key = jnp.where(low, *halves(dot(d_scores, queries))).astype(BF)
        d_query = (dot(split_rows(keys.T), d_scores) * scale).astype(BF).T
        for i, item in enumerate((d_query, d_key, d_value)):
            dqkv_ref[:, i * width + first : i * width + first + 2 * HD] = item
        sums_ref[0, :, sl] += column_sum(d_query.astype(F32))
        sums_ref[1, :, sl] += column_sum(d_value.astype(F32))


def attend_back(query, keys, values, d_mixed, lse, seg, group, groups, after=()):
    count = query.shape[0]
    width = query.shape[1] // groups
    rows = seg.shape[0] // 8
    slots = seg.shape[1]
    heads = width // HD
    row = pl.BlockSpec((slots, width), lambda i: (i, group))
    sums_spec, sums_shape = sums_of(2, width)
    zero_spec, zero_shape = zero_out()
    return pl.pallas_call(
        functools.partial(attend_back_kernel, group * heads, len(after)),
        grid=(rows,),
        in_specs=[row] * 4
        + [
            pl.BlockSpec((lse.shape[0] // rows, slots), lambda i: (i, 0)),
            pl.BlockSpec((8, slots), lambda i: (i, 0)),
        ]
        + anywhere(len(after)),
        out_specs=[pl.BlockSpec((slots, 3 * width), lambda i: (i, 0)), sums_spec, zero_spec],
        out_shape=[jax.ShapeDtypeStruct((count, 3 * width), BF), sums_shape, zero_shape],
        scratch_shapes=[pltpu.VMEM((slots, slots), F32)],
        compiler_params=params(),
        cost_estimate=cost(2.2e10 / groups, 1e7),
        name="attend_back",
    )(query, keys, values, d_mixed, lse, seg, *after)


def tokens_kernel(numbered, n_arrays, n_after, groups, dfirst_ref, *refs):
    dqkv_refs = refs[:groups]
    pieces = refs[groups : groups + n_arrays]
    out_ref, zero_ref, w_ref, sems = refs[groups + n_arrays + n_after :]
    zero_ref[0, 0] = 0.0
    width = dfirst_ref.shape[1]
    part_width = width // groups

    ready = load_weights(numbered, pieces, [w_ref.at[which] for which in range(3)], sems)
    total = dfirst_ref[...]
    for which in range(3):
        ready(which)
        sl = slice(which * part_width, (which + 1) * part_width)
        joined = jnp.concatenate([ref[:, sl] for ref in dqkv_refs], axis=1)
        total = total + dot(joined, w_ref[which], NT)
    out_ref[...] = total


def tokens_back(d_first, dqkv, weights, after=()):
    count, width = d_first.shape
    arrays, numbered = index_pieces(weights)
    tile = ROW_TILE
    zero_spec, zero_shape = zero_out()
    return pl.pallas_call(
        functools.partial(tokens_kernel, numbered, len(arrays), len(after), len(dqkv)),
        grid=(count // tile,),
        in_specs=[pl.BlockSpec((tile, width), lambda i: (i, 0))]
        + [pl.BlockSpec((tile, item.shape[1]), lambda i: (i, 0)) for item in dqkv]
        + anywhere(len(arrays) + len(after)),
        out_specs=[pl.BlockSpec((tile, width), lambda i: (i, 0)), zero_spec],
        out_shape=[jax.ShapeDtypeStruct((count, width), F32), zero_shape],
        scratch_shapes=[
            pltpu.VMEM((3, width, width), BF),
            pltpu.SemaphoreType.DMA((sum(len(p) for p in numbered),)),
        ],
        compiler_params=params(),
        cost_estimate=cost(6e9, 1.5e7),
        name="tokens_back",
    )(d_first, *dqkv, *arrays, *after)


def rows_kernel(order, spans, n_after, *refs):
    n = len(spans)
    lefts, rights = refs[:n], refs[n : 2 * n]
    outs, zero_ref, left_ref = refs[2 * n + n_after : -2], refs[-2], refs[-1]
    zero_ref[0, 0] = 0.0
    step = pl.program_id(0)
    pieces, size, _ = outs[0].shape
    first = 0
    for left, right, (chunks, chunk, column) in zip(lefts, rights, spans):

        @pl.when(step == first)
        def _():
            if order is None:
                left_ref[...] = left[...]
                return
            for which in range(2):
                for place, rel in enumerate(order):
                    start = pl.multiple_of((lax.axis_index("fsdp") ^ (rel | which * CORE)) * size, size)
                    at = (which * pieces + place) * size
                    left_ref[at : at + size, :] = left[pl.ds(start, size), :]

        @pl.when((step >= first) & (step < first + chunks))
        def _():
            got = dot(left_ref[...], right[...]).astype(BF)
            for which, out in enumerate(outs):
                for place in range(pieces):
                    at = (which * pieces + place) * size
                    rows = got[at : at + size, :]
                    if n == 1:
                        out[place] = rows
                    else:
                        out[place, :, pl.ds(pl.multiple_of(column + (step - first) * chunk, 128), chunk)] = rows

        first += chunks


def rows_grad(products, order, size, after=()):
    height, depth = products[0][0].shape
    spans, column = [], 0
    for _, right, chunk in products:
        spans.append((right.shape[1] // chunk, chunk, column))
        column += right.shape[1]
    firsts = [sum(s[0] for s in spans[:i]) for i in range(len(spans))]
    zero_spec, zero_shape = zero_out()
    pieces, n_out = (1, 1) if order is None else (len(order), 2)

    def right_spec(i):
        chunks, chunk, _ = spans[i]
        return pl.BlockSpec((depth, chunk), lambda g: (0, jnp.clip(g - firsts[i], 0, chunks - 1)))

    if len(products) == 1:
        out_spec = pl.BlockSpec((pieces, size, spans[0][1]), lambda g: (0, 0, g))
    else:
        out_spec = pl.BlockSpec((pieces, size, column), lambda g: (0, 0, 0))
    return pl.pallas_call(
        functools.partial(rows_kernel, order, spans, len(after)),
        grid=(sum(s[0] for s in spans),),
        in_specs=[whole((height, depth)) for _ in products]
        + [right_spec(i) for i in range(len(products))]
        + anywhere(len(after)),
        out_specs=[out_spec] * n_out + [zero_spec],
        out_shape=[jax.ShapeDtypeStruct((pieces, size, column), BF)] * n_out + [zero_shape],
        scratch_shapes=[pltpu.VMEM((height, depth), BF)],
        compiler_params=params(),
        cost_estimate=cost(3.5 * height * depth * column, 2 * depth * column + 2 * height * column),
        name="rows_grad",
    )(*[p[0] for p in products], *[p[1] for p in products], *after)


def columns_kernel(direct, n_after, _, left_ref, right_ref, *refs):
    outs, acc_ref = refs[n_after:-1], refs[-1]
    acc_ref[...] = dot(left_ref[...], right_ref[...])
    if not direct:
        outs[0][0] = acc_ref[...].astype(BF)
        return
    size = outs[0].shape[2]
    core = lax.axis_index("fsdp") & CORE
    for which, out in enumerate(outs):
        start = pl.multiple_of((core ^ which) * size, 128)
        out[0] = acc_ref[:, pl.ds(start, size)].astype(BF)


def columns_grad(left, right, order, size, after=()):
    height, depth = left.shape
    direct = order is not None
    if direct:
        chips = lax.axis_index("fsdp") // 2
        places = jnp.stack([chips ^ (rel // 2) for rel in order]).astype(jnp.int32)
        chunk, n_out = 2 * size, 2
    else:
        places = jnp.arange(right.shape[1] // size, dtype=jnp.int32)
        chunk, n_out = size, 1
    count = places.shape[0]
    return pl.pallas_call(
        functools.partial(columns_kernel, direct, len(after)),
        grid_spec=pltpu.PrefetchScalarGridSpec(
            num_scalar_prefetch=1,
            grid=(count,),
            in_specs=[
                pl.BlockSpec((height, depth), lambda g, p: (0, 0), pipeline_mode=pl.Buffered(1)),
                pl.BlockSpec((depth, chunk), lambda g, p: (0, p[g])),
            ]
            + anywhere(len(after)),
            out_specs=[pl.BlockSpec((1, height, size), lambda g, p: (g, 0, 0))] * n_out,
            scratch_shapes=[pltpu.VMEM((height, chunk), F32)],
        ),
        out_shape=[jax.ShapeDtypeStruct((count, height, size), BF)] * n_out,
        compiler_params=params(),
        cost_estimate=cost(3.5 * height * depth * chunk * count, 4 * depth * chunk * count),
        name="columns_grad",
    )(places, left, right, *after)


def up(x):
    return x.astype(F32)


def add(zero, *items):
    total = up(items[0])
    for item in items[1:]:
        total = total + up(item)
    return with_zero(total, zero)


class Scatter:
    def __init__(self, send, first, second):
        self.first, self.second = first, second
        self.got = [flip(send, "fsdp", CORE)]

    def far(self, keep, zero=None):
        self.keep = keep
        self.out = add(zero, keep[2:], self.got[0][2:]).astype(BF)
        self.got.append(flip(self.out, "fsdp", self.first))
        return self.out

    def near(self, zero=None):
        self.out = add(zero, self.keep[1], self.got[0][1], self.got[1][1]).astype(BF)
        self.got.append(flip(self.out, "fsdp", self.second))
        return self.out

    def total(self, zero=None):
        return add(zero, self.keep[0], self.got[0][0], self.got[1][0], self.got[2]).astype(BF)


def rep_plain(total):
    n = lax.axis_size("rep")
    return n != 4 or total.shape[0] % n != 0


class RepSteps:
    def __init__(self, total):
        self.plain, self.low = rep_plain(total), total
        if self.plain:
            return
        me = lax.axis_index("rep")
        self.bits = me & 1, me // 2
        self.low = total.reshape(2, 2, total.shape[0] // 4, total.shape[1])
        self.got = flip(self.take(self.low, 1 - self.bits[0], 1), "rep", 1)

    def take(self, array, index, axis):
        return lax.dynamic_index_in_dim(array, index, axis, keepdims=False)

    def second(self, zero=None):
        self.half = add(zero, self.take(self.low, self.bits[0], 1), self.got).astype(BF)
        self.got = flip(self.take(self.half, 1 - self.bits[1], 0), "rep", 2)
        return self.half

    def third(self, zero=None):
        self.mine = add(zero, self.take(self.half, self.bits[1], 0), self.got).astype(BF)
        self.got = flip(self.mine, "rep", 2)
        return self.mine

    def join(self, bit, axis):
        pair = [self.mine, self.got]
        return jnp.stack([jnp.where(bit == i, *pair) for i in range(2)], axis=axis)

    def fourth(self, zero=None):
        self.mine = with_zero(self.join(self.bits[1], 0), zero)
        self.got = flip(self.mine, "rep", 1)
        return self.mine

    def total(self, factor):
        if self.plain:
            return up(lax.psum(self.low, "rep")) * factor
        joined = self.join(self.bits[0], 1)
        return up(joined.reshape(-1, joined.shape[-1])) * factor


def rep_double(total, factor):
    if rep_plain(total):
        return up(lax.psum(total, "rep")) * factor
    near = add(None, total, flip(total, "rep", 1)).astype(BF)
    return add(None, near, flip(near, "rep", 2)) * factor


def all_sum(values, axes=("fsdp", "rep")):
    for axis in axes:
        n = lax.axis_size(axis)
        if n & (n - 1):
            values = lax.psum(values, axis)
            continue
        bit = 1
        while bit < n:
            values = values + flip(values, axis, bit)
            bit *= 2
    return values


def body(
    tokens,
    doc_lengths,
    query_weight,
    key_weight,
    value_weight,
    output_weight,
    inner_weight,
    outer_weight,
    query_bias,
    value_bias,
    output_bias,
    inner_bias,
    outer_bias,
    first_gain,
    first_shift,
    second_gain,
    second_shift,
    cotangent,
):
    rows, slots, width = tokens.shape
    count = rows * slots
    docs = doc_lengths.shape[1]
    n_fsdp = lax.axis_size("fsdp")
    n_rep = lax.axis_size("rep")
    shard = query_weight.shape[0]
    outer_shard = outer_weight.shape[0]
    inner_width = inner_weight.shape[1]
    direct = n_fsdp == 8 and shard % 16 == 0

    vectors = (
        query_bias,
        value_bias,
        output_bias,
        outer_bias,
        first_gain,
        first_shift,
        second_gain,
        second_shift,
        inner_bias,
    )
    if direct:
        half, outer_half = shard // 2, outer_shard // 2
        block_x, block_y = pack(query_weight, key_weight, value_weight, vectors)
        one, two = Gather(block_x, X, Y), Gather(block_y, Y, X)
        both = jnp.concatenate([inner_weight, output_weight], axis=1)
        three, four = Gather(both[:half], X, Y), Gather(both[half:], Y, X)
        five, six = Gather(outer_weight[:outer_half], X, Y), Gather(outer_weight[outer_half:], Y, X)
        pairs = [item.far() for item in (one, two, three, four)][2:] + [five.got, six.got]
        held_x, held_y = one.held(), two.held()
        qw = part(held_x, 0, shard, shard)
        kw = part(held_x, shard, half, shard) + part(held_y, shard, half, shard, half)
        vw = part(held_y, 0, shard, shard)
        vec, bias_inner = unpack(part(held_x, shard + half, 16, 16), shard, outer_shard)
    else:
        qw, kw, vw, ow, iw, w2 = [
            [(lax.all_gather(w, "fsdp", axis=0, tiled=True), 0, w.shape[0] * n_fsdp, None, 0, 0, 0)]
            for w in (query_weight, key_weight, value_weight, output_weight, inner_weight, outer_weight)
        ]
        small = lax.all_gather(jnp.concatenate(vectors)[None], "fsdp", axis=0, tiled=True).astype(F32)
        vec = small[:, : 8 * shard].reshape(n_fsdp, 8, shard).transpose(1, 0, 2).reshape(8, width)
        bias_inner = small[:, 8 * shard :].reshape(1, inner_width)
        pairs = ()

    places = jnp.arange(docs, dtype=jnp.int32)
    ends = jnp.sum(
        jnp.where(places[None, :, None] >= places[None, None, :], doc_lengths[:, None, :], 0), axis=-1
    )
    slot = jnp.arange(slots, dtype=jnp.int32)
    segment = jnp.sum((slot[None, None, :] >= ends[:, :, None]).astype(jnp.int32), axis=1)
    seg = jnp.broadcast_to(segment[:, None, :].astype(F32), (rows, 8, slots)).reshape(rows * 8, slots)

    flat = tokens.reshape(count, width)
    query, keys, values, mixed_t, tokens_t, lse, zero = attend(flat, seg, vec, (qw, kw, vw), pairs)
    if direct:
        pairs = five.far(zero), six.far(zero)
        held_x, held_y = three.held(zero), four.held(zero)
        iw = part(held_x, 0, half, shard) + part(held_y, 0, half, shard, half)
        ow = [(*piece[:-1], inner_width) for piece in iw]
    hidden_t, n1, r1, activated, slope, zero = feed_inner(mixed_t, flat, vec, bias_inner, (ow, iw), pairs)
    if direct:
        held_x, held_y = five.held(zero), six.held(zero)
        w2 = part(held_x, 0, outer_half, outer_shard) + part(held_y, 0, outer_half, outer_shard, outer_half)
    encoded, d_outer_t, d_second, d_inner, sums_outer, sums_inner = feed_outer(
        n1, activated, slope, cotangent.reshape(count, width), seg, vec, (w2,), docs
    )
    factor = 1.0 / math.sqrt(rows * n_rep * n_fsdp * slots)
    if direct:
        order_xy, order_yx = (0, Y, X, X | Y), (0, X, Y, X | Y)
        keep_o, send_o = columns_grad(d_outer_t, activated, order_yx, outer_shard)
        outer = Scatter(send_o, Y, X)
        keep_i, send_i, zero = rows_grad([(hidden_t, d_inner, 768)], order_xy, shard, (send_o,))
        inner = Scatter(send_i, X, Y)
        d_first, d_branch, d_mixed, sums_first, zero = feed_hidden(
            d_inner, d_second, n1, r1, vec, (iw, ow), (outer.far(keep_o, zero), inner.far(keep_i, zero))
        )
        back = lambda group, after: attend_back(query, keys, values, d_mixed, lse, seg, group, 2, after)
        dqkv_a, sums_a, zero = back(0, ())
        products = [(tokens_t, dqkv_a, dqkv_a.shape[1]), (mixed_t, d_branch, width)]
        keep_a, send_a, zero = rows_grad(products, order_yx, shard, (outer.near(zero), inner.near(zero)))
        scatter_a = Scatter(send_a, Y, X)
        dqkv_b, sums_b, zero = back(1, (send_a,))
        products = [(tokens_t, dqkv_b, dqkv_b.shape[1])]
        rep_outer = RepSteps(outer.total(zero))
        rep_inner = RepSteps(inner.total(zero))
        keep_b, send_b, zero = rows_grad(
            products, order_xy, shard, (scatter_a.far(keep_a, zero), rep_outer.low, rep_inner.low)
        )
        scatter_b = Scatter(send_b, X, Y)
        tokens_grad, zero = tokens_back(
            d_first, [dqkv_a, dqkv_b], (qw, kw, vw), (rep_outer.second(zero), scatter_b.far(keep_b, zero))
        )
        scatter_a.near(zero)
        rep_inner.second(zero)
        rep_outer.third(zero)
        scatter_b.near(zero)
        rep_a = RepSteps(scatter_a.total())
        rep_outer.fourth()
        rep_inner.third()
        rep_a.second()
        b_all = rep_double(scatter_b.total(), factor)
        rep_inner.fourth()
        rep_a.third()
        rep_a.fourth()
        a_all = rep_a.total(factor)
        outer_all = rep_outer.total(factor)
        inner_all = rep_inner.total(factor)
        q_all, k_all, v_all = [
            jnp.concatenate([a_all[:, i * width // 2 : (i + 1) * width // 2], b_all[:, i * width // 2 : (i + 1) * width // 2]], axis=1)
            for i in range(3)
        ]
        o_all = a_all[:, 3 * width // 2 :]
    else:
        d_first, d_branch, d_mixed, sums_first, _ = feed_hidden(d_inner, d_second, n1, r1, vec, (iw, ow))
        (dqkv_a, sums_a, _), (dqkv_b, sums_b, _) = [
            attend_back(query, keys, values, d_mixed, lse, seg, group, 2) for group in range(2)
        ]
        tokens_grad, zero = tokens_back(d_first, [dqkv_a, dqkv_b], (qw, kw, vw))

        def shared(total, axis):
            return up(lax.psum(lax.psum_scatter(total, "fsdp", scatter_dimension=axis, tiled=True), "rep")) * factor

        def rows_all(left, right, chunk):
            return shared(rows_grad([(left, right, chunk)], None, width)[0][0], 0)

        outer_all = shared(
            columns_grad(d_outer_t, activated, None, inner_width // 4)[0]
            .transpose(1, 0, 2)
            .reshape(width, inner_width),
            1,
        )
        inner_all = rows_all(hidden_t, d_inner, 768)
        o_all = rows_all(mixed_t, d_branch, width)
        both = [jnp.split(d, 3, axis=1) for d in (dqkv_a, dqkv_b)]
        q_all, k_all, v_all = [
            rows_all(tokens_t, jnp.concatenate([a, b], axis=1), width) for a, b in zip(*both)
        ]
    vectors = jnp.concatenate(
        [
            jnp.concatenate([jnp.sum(sums_a, axis=1), jnp.sum(sums_b, axis=1)], axis=1),
            jnp.sum(sums_first[:1], axis=1),
            jnp.sum(sums_outer[:1], axis=1),
            jnp.sum(sums_first[1:], axis=1),
            jnp.sum(sums_outer[1:], axis=1),
            jnp.sum(sums_inner, axis=0).reshape(inner_width // width, width),
        ],
        axis=0,
    )
    vectors = all_sum(with_zero(vectors, zero)) * factor
    me = lax.axis_index("fsdp")
    short = lax.dynamic_slice_in_dim(vectors[:8], me * shard, shard, axis=1)
    long = lax.dynamic_slice_in_dim(vectors[8:].reshape(inner_width), me * outer_shard, outer_shard, axis=0)
    return (
        encoded.reshape(rows, slots, width),
        tokens_grad.reshape(rows, slots, width),
        q_all,
        k_all,
        v_all,
        o_all,
        inner_all,
        outer_all.T,
        short[0],
        short[1],
        short[2],
        long,
        short[3],
        short[4],
        short[5],
        short[6],
        short[7],
    )


def solution(mesh):
    data = P(("rep", "fsdp"), None, None)
    matrix, vector = P("fsdp", None), P("fsdp")
    return jax.shard_map(
        body,
        mesh=mesh,
        in_specs=(data, P(("rep", "fsdp"), None)) + (matrix,) * 6 + (vector,) * 9 + (data,),
        out_specs=(data, data) + (matrix,) * 6 + (vector,) * 9,
        check_vma=False,
    )
```

```python
import functools
import math

import jax
import jax.numpy as jnp
from jax import lax
from jax.experimental import pallas as pl
from jax.experimental.pallas import tpu as pltpu
from jax.sharding import PartitionSpec as P

HD = 64
EPSILON = 1e-05
BF = jnp.bfloat16
F32 = jnp.float32
NT = ((1,), (1,))
VMEM_BYTES = 60 * 2**20
CORE, X, Y = 1, 2, 4
ROW_TILE = 256
FF_CHUNK = 1536


def dot(a, b, dims=((1,), (0,))):
    return lax.dot_general(a, b, (dims, ((), ())), preferred_element_type=F32)


def params():
    return pltpu.CompilerParams(
        vmem_limit_bytes=VMEM_BYTES, dimension_semantics=("arbitrary",)
    )


def cost(flops, nbytes, trans=0):
    return pl.CostEstimate(
        flops=int(flops), bytes_accessed=int(nbytes), transcendentals=int(trans)
    )


def whole(shape):
    return pl.BlockSpec(
        shape, lambda *i: (0,) * len(shape), pipeline_mode=pl.Buffered(1)
    )


def anywhere(count):
    return [pl.BlockSpec(memory_space=pl.ANY)] * count


def flip(array, axis, bit):
    size = lax.axis_size(axis)
    return lax.ppermute(array, axis, [(i, i ^ bit) for i in range(size)])


def pinned(values, *others):
    return lax.optimization_barrier((values, others))[0]


def piece_copies(pieces, refs, target, sems, first):
    copies = []
    for slot, (which, start, rows, rel, shard, offset, column) in enumerate(pieces):
        place = 0
        if rel is not None:
            place = pl.multiple_of((lax.axis_index("fsdp") ^ rel) * shard + offset, math.gcd(shard, offset))
        copies.append(
            pltpu.make_async_copy(
                refs[which].at[pl.ds(start, rows), pl.ds(column, target.shape[1])],
                target.at[pl.ds(place, rows), :],
                sems.at[first + slot],
            )
        )
    return copies


def group_copies(numbered, refs, targets, sems):
    copies = []
    for pieces, target in zip(numbered, targets):
        copies.append(piece_copies(pieces, refs, target, sems, sum(len(c) for c in copies)))
    return copies


def index_pieces(weights):
    arrays, numbered = [], []
    for pieces in weights:
        mine = []
        for array, *rest in pieces:
            for n, seen in enumerate(arrays):
                if seen is array:
                    break
            else:
                n = len(arrays)
                arrays.append(array)
            mine.append((n, *rest))
        numbered.append(mine)
    return arrays, numbered


class Gather:
    def __init__(self, block, first, second):
        self.block, self.bits = block, (first, second)
        self.near = flip(block, "fsdp", first)

    def go(self, pair):
        self.pair = pair
        self.far = flip(pair, "fsdp", self.bits[1])
        return pair

    def parts(self):
        first, second = self.bits
        rows = self.block.shape[0]
        return [(self.pair, 0, 0), (self.pair, rows, first), (self.far, 0, second), (self.far, rows, first | second)]

    def held(self):
        other = {id(a): flip(a, "fsdp", CORE) for a in (self.pair, self.far)}
        return self.parts() + [(other[id(a)], at, rel | CORE) for a, at, rel in self.parts()]

    def held_whole(self, chips):
        first, second = self.bits
        rels = (0, first, second, first | second)
        return [
            (array, place * self.block.shape[0], rel | core)
            for core, array in ((0, chips), (CORE, flip(chips, "fsdp", CORE)))
            for place, rel in enumerate(rels)
        ]


def stack_kernel(n_after, one, two, three, four, *refs):
    for out, parts in zip(refs[n_after:], ((one, two), (three, four))):
        at = 0
        for ref in parts:
            rows = ref.shape[0]
            out[at : at + rows, :] = ref[...]
            at += rows


def stacked(one, two, three, four, after=()):
    full = lambda a: pl.BlockSpec(a.shape, lambda g: (0, 0))
    outs = [
        jax.ShapeDtypeStruct((a.shape[0] + b.shape[0], a.shape[1]), BF) for a, b in ((one, two), (three, four))
    ]
    return pl.pallas_call(
        functools.partial(stack_kernel, len(after)),
        grid=(1,),
        in_specs=[full(a) for a in (one, two, three, four)] + anywhere(len(after)),
        out_specs=[full(a) for a in outs],
        out_shape=outs,
        compiler_params=params(),
        cost_estimate=cost(2e9, 3e6),
        name="stacked",
    )(one, two, three, four, *after)


def pack_kernel(half, query_ref, key_ref, value_ref, wi_ref, wo_ref, w2_ref, *refs):
    vectors, (one_ref, two_ref, three_ref, four_ref) = refs[:-4], refs[-4:]
    shard, width = query_ref.shape
    one_ref[:shard, :] = query_ref[...]
    one_ref[shard : shard + half, :] = key_ref[:half, :]
    two_ref[:shard, :] = value_ref[...]
    two_ref[shard:, :] = key_ref[half:, :]
    rows = []
    for ref in vectors:
        size = ref.shape[0]
        rows.append(
            jnp.concatenate([ref[...].astype(F32).reshape(1, size), jnp.zeros((1, width - size), F32)], axis=1)
        )
    rows.append(jnp.zeros((16 - len(rows), width), F32))
    one_ref[shard + half :, :] = jnp.concatenate(rows, axis=0).astype(BF)
    wide = wi_ref.shape[1]
    blocks = w2_ref.shape[0] // (2 * half)
    for place, ref in enumerate((three_ref, four_ref)):
        ref[:, :wide] = wi_ref[place * half : (place + 1) * half, :]
        ref[:, wide : wide + width] = wo_ref[place * half : (place + 1) * half, :]
        for block in range(blocks):
            row, column = (place * blocks + block) * half, wide + (1 + block) * width
            ref[:, column : column + width] = w2_ref[row : row + half, :]


def pack(query, key, value, inner, output, outer, vectors):
    shard, width = query.shape
    half = shard // 2
    wide = inner.shape[1] + width * (1 + outer.shape[0] // (2 * half))
    return pl.pallas_call(
        functools.partial(pack_kernel, half),
        out_shape=[
            jax.ShapeDtypeStruct((shard + half + 16, width), BF),
            jax.ShapeDtypeStruct((shard + half, width), BF),
            jax.ShapeDtypeStruct((half, wide), BF),
            jax.ShapeDtypeStruct((half, wide), BF),
        ],
        compiler_params=pltpu.CompilerParams(vmem_limit_bytes=VMEM_BYTES),
        name="pack",
    )(query, key, value, inner, output, outer, *vectors)


def unpack_kernel(numbered, n_arrays, shard, long, *refs):
    pieces = refs[:n_arrays]
    vec_ref, inner_ref, held_ref, sems = refs[n_arrays:]
    copies = piece_copies(numbered[0], pieces, held_ref, sems, 0)
    for copy in copies:
        copy.start()
    for copy in copies:
        copy.wait()
    n = len(copies)
    parts = [held_ref[16 * i : 16 * i + 16, :] for i in range(n)]
    slot = lax.broadcasted_iota(jnp.int32, (n * 128, n * shard), 0)
    place = lax.broadcasted_iota(jnp.int32, (n * 128, n * shard), 1)
    at = slot % 128
    spread = ((at < shard) & (place == slot // 128 * shard + at)).astype(BF)
    vec_ref[...] = dot(jnp.concatenate([p[:, :128] for p in parts], axis=1), spread)[:8]
    for i, p in enumerate(parts):
        inner_ref[:, i * long : (i + 1) * long] = p[8:9, :long].astype(F32)


def unpack(pieces, shard, long):
    arrays, numbered = index_pieces([pieces])
    n, width = len(pieces), pieces[0][0].shape[1]
    return pl.pallas_call(
        functools.partial(unpack_kernel, numbered, len(arrays), shard, long),
        in_specs=anywhere(len(arrays)),
        out_shape=[
            jax.ShapeDtypeStruct((8, n * shard), F32),
            jax.ShapeDtypeStruct((1, n * long), F32),
        ],
        scratch_shapes=[pltpu.VMEM((16 * n, width), BF), pltpu.SemaphoreType.DMA((n,))],
        name="unpack",
    )(*arrays)


def part(held, start, rows, shard, offset=0):
    return [(a, at + start, rows, rel, shard, offset, 0) for a, at, rel in held]


def column_of(row):
    return jnp.broadcast_to(row, (128, row.shape[1])).T[:, :1]


def split_lanes(pair):
    low = lax.broadcasted_iota(jnp.int32, (1, 2 * HD), 1) < HD
    return jnp.concatenate([jnp.where(low, pair, BF(0)), jnp.where(low, BF(0), pair)], axis=0)


def split_rows(pair_t):
    low = lax.broadcasted_iota(jnp.int32, (2 * HD, 1), 0) < HD
    return jnp.concatenate([jnp.where(low, pair_t, BF(0)), jnp.where(low, BF(0), pair_t)], axis=1)


def attend_kernel(numbered, n_arrays, n_after, heads, tok_ref, seg_ref, vec_ref, *refs):
    pieces = refs[:n_arrays]
    q_ref, k_ref, v_ref, mt_ref, tt_ref, lse_ref, w_ref, bias_ref, qs_ref, sems = refs[n_arrays + n_after :]
    ready = load_weights(numbered, pieces, [w_ref.at[which] for which in range(3)], sems)
    x = tok_ref[...]
    tt_ref[...] = x.T
    seg = seg_ref[0:1, :]
    bias_ref[...] = jnp.where(column_of(seg) == seg, 0.0, -1e30)

    for which in range(3):
        ready(which)
    q = (dot(x, w_ref[0]) + vec_ref[0:1, :]).astype(BF)
    q_ref[...] = q
    qs_ref[...] = q * BF(1.0 / math.sqrt(HD))
    k_ref[...] = dot(x, w_ref[1]).astype(BF)
    v_ref[...] = (dot(x, w_ref[2]) + vec_ref[1:2, :]).astype(BF)
    for pair in range(heads // 2):
        sl = slice(pair * 2 * HD, (pair + 1) * 2 * HD)
        scores = dot(split_lanes(k_ref[:, sl]), qs_ref[:, sl], NT)
        slots = scores.shape[0] // 2
        weights, inverse = [], []
        for half in range(2):
            mine = scores[half * slots : (half + 1) * slots] + bias_ref[...]
            top = jnp.max(mine, axis=0, keepdims=True)
            exps = jnp.exp(mine - top)
            total = jnp.sum(exps, axis=0, keepdims=True)
            head = 2 * pair + half
            lse_ref[head : head + 1, :] = top + jnp.log(total)
            weights.append(exps.astype(BF))
            inverse.append(1.0 / total)
        out = dot(split_rows(v_ref[:, sl].T), jnp.concatenate(weights, axis=0))
        low_rows = lax.broadcasted_iota(jnp.int32, (2 * HD, 1), 0) < HD
        mt_ref[sl, :] = (out * jnp.where(low_rows, inverse[0], inverse[1])).astype(BF)


def attend(tokens, seg, vec, weights, after=()):
    count, width = tokens.shape
    rows = seg.shape[0] // 8
    slots = count // rows
    heads = width // HD
    padded = -(-heads // 8) * 8
    arrays, numbered = index_pieces(weights)
    row = pl.BlockSpec((slots, width), lambda i: (i, 0))
    col = pl.BlockSpec((width, slots), lambda i: (0, i))
    return pl.pallas_call(
        functools.partial(attend_kernel, numbered, len(arrays), len(after), heads),
        grid=(rows,),
        in_specs=[row, pl.BlockSpec((8, slots), lambda i: (i, 0)), whole(vec.shape)]
        + anywhere(len(arrays) + len(after)),
        out_specs=[row, row, row, col, col, pl.BlockSpec((padded, slots), lambda i: (i, 0))],
        out_shape=[jax.ShapeDtypeStruct((count, width), BF)] * 3
        + [jax.ShapeDtypeStruct((width, count), BF)] * 2
        + [jax.ShapeDtypeStruct((rows * padded, slots), F32)],
        scratch_shapes=[
            pltpu.VMEM((3, width, width), BF),
            pltpu.VMEM((slots, slots), F32),
            pltpu.VMEM((slots, width), BF),
            pltpu.SemaphoreType.DMA((sum(len(p) for p in numbered),)),
        ],
        compiler_params=params(),
        cost_estimate=cost(1e9, 1e6),
        name="attend",
    )(tokens, seg, vec, *arrays, *after)


def gelu_pair(v):
    area = 0.5 + 0.5 * lax.erf(v * math.sqrt(0.5))
    density = jnp.exp2(v * v * (-0.5 / math.log(2.0))) * (1.0 / math.sqrt(2.0 * math.pi))
    return v * area, area + v * density


def norm(z):
    center = z - jnp.mean(z, axis=-1, keepdims=True)
    scale = lax.rsqrt(jnp.mean(center * center, axis=-1, keepdims=True) + EPSILON)
    return center * scale, scale


def norm_back(grad, n, scale, gain):
    dn = grad * gain
    return (
        dn - jnp.mean(dn, axis=-1, keepdims=True) - n * jnp.mean(dn * n, axis=-1, keepdims=True)
    ) * scale


def column_sum(x):
    return jnp.sum(x.reshape(x.shape[0] // 8, 8, x.shape[1]), axis=0)


def load_weights(numbered, pieces, targets, sems):
    groups = group_copies(numbered, pieces, targets, sems)
    first_step = pl.program_id(0) == 0

    @pl.when(first_step)
    def _():
        for copies in groups:
            for copy in copies:
                copy.start()

    def ready(which):
        @pl.when(first_step)
        def _():
            for copy in groups[which]:
                copy.wait()

    return ready


def vector(vec_ref, i):
    return vec_ref[i : i + 1, :]


def feed_kernel(numbered, n_arrays, docs, mt_ref, tok_ref, cot_ref, seg_ref, vec_ref, bi_ref, *refs):
    pieces = refs[:n_arrays]
    outs = refs[n_arrays:]
    enc_ref, ht_ref, act_ref, dot_ref, din_ref, dfirst_ref, dbr_ref, dm_ref, total_ref = outs[:9]
    wo_ref, wi_ref, w2_ref, slope_ref, sums_ref, sumi_ref, sems = outs[9:]
    ready = load_weights(numbered, pieces, (wo_ref, wi_ref, w2_ref), sems)

    @pl.when(pl.program_id(0) == 0)
    def _():
        sums_ref[...] = jnp.zeros_like(sums_ref)
        sumi_ref[...] = jnp.zeros_like(sumi_ref)

    width, inner_width = wi_ref.shape
    ready(0)
    z1 = tok_ref[...].astype(F32) + dot(mt_ref[...].T, wo_ref[...]) + vector(vec_ref, 2)
    n1, r1 = norm(z1)
    hidden = n1 * vector(vec_ref, 4) + vector(vec_ref, 5)
    hidden_low = hidden.astype(BF)
    ht_ref[...] = hidden_low.T
    ready(1)
    z2 = hidden + vector(vec_ref, 3)
    for c in range(0, inner_width, FF_CHUNK):
        sl = slice(c, c + FF_CHUNK)
        act, slope = gelu_pair(dot(hidden_low, wi_ref[:, sl]) + bi_ref[:, sl])
        act = act.astype(BF)
        act_ref[:, sl] = act
        slope_ref[:, sl] = slope
        if c == 0:
            ready(2)
        z2 = z2 + dot(act, w2_ref[sl, :])
    n2, r2 = norm(z2)
    gain = vector(vec_ref, 6)
    enc_ref[...] = (n2 * gain + vector(vec_ref, 7)).astype(BF)
    grad = cot_ref[...] * column_of((seg_ref[0:1, :] < docs).astype(F32))
    d_second = norm_back(grad, n2, r2, gain)
    d_outer = d_second.astype(BF)
    dot_ref[...] = d_outer.T
    d_hidden = d_second
    for c in range(0, inner_width, FF_CHUNK):
        sl = slice(c, c + FF_CHUNK)
        d_inner = (dot(d_outer, w2_ref[sl, :], NT) * slope_ref[:, sl]).astype(BF)
        din_ref[:, sl] = d_inner
        sumi_ref[:, sl] += column_sum(d_inner.astype(F32))
        d_hidden = d_hidden + dot(d_inner, wi_ref[:, sl], NT)
    d_first = norm_back(d_hidden, n1, r1, vector(vec_ref, 4))
    dfirst_ref[...] = d_first
    d_branch = d_first.astype(BF)
    dbr_ref[...] = d_branch
    dm_ref[...] = dot(d_branch, wo_ref[...], NT).astype(BF)
    for i, item in enumerate(
        (d_branch.astype(F32), d_outer.astype(F32), d_hidden * n1, d_hidden, grad * n2, grad)
    ):
        sums_ref[i] += column_sum(item)

    @pl.when(pl.program_id(0) == pl.num_programs(0) - 1)
    def _():
        total_ref[...] = jnp.zeros_like(total_ref)
        for i in range(6):
            total_ref[2 + i : 3 + i, :] = jnp.sum(sums_ref[i], axis=0, keepdims=True)
        for i in range(inner_width // width):
            part_sum = jnp.sum(sumi_ref[:, i * width : (i + 1) * width], axis=0, keepdims=True)
            total_ref[8 + i : 9 + i, :] = part_sum


def feed(mixed_t, tokens, cotangent, seg, vec, bias_inner, weights, docs):
    count, width = tokens.shape
    inner_width = bias_inner.shape[1]
    arrays, numbered = index_pieces(weights)
    tile = ROW_TILE
    row = pl.BlockSpec((tile, width), lambda i: (i, 0))
    col = pl.BlockSpec((width, tile), lambda i: (0, i))
    wide = pl.BlockSpec((tile, inner_width), lambda i: (i, 0))
    per_row = seg.shape[1] // tile
    sum_rows = -(-(8 + inner_width // width) // 8) * 8
    out = jax.ShapeDtypeStruct
    return pl.pallas_call(
        functools.partial(feed_kernel, numbered, len(arrays), docs),
        grid=(count // tile,),
        in_specs=[
            col,
            row,
            row,
            pl.BlockSpec((8, tile), lambda i: (i // per_row, i % per_row)),
            whole(vec.shape),
            whole(bias_inner.shape),
        ]
        + anywhere(len(arrays)),
        out_specs=[row, col, wide, col, wide, row, row, row, pl.BlockSpec((sum_rows, width), lambda i: (0, 0))],
        out_shape=[
            out((count, width), BF),
            out((width, count), BF),
            out((count, inner_width), BF),
            out((width, count), BF),
            out((count, inner_width), BF),
            out((count, width), F32),
            out((count, width), BF),
            out((count, width), BF),
            out((sum_rows, width), F32),
        ],
        scratch_shapes=[
            pltpu.VMEM((width, width), BF),
            pltpu.VMEM((width, inner_width), BF),
            pltpu.VMEM((inner_width, width), BF),
            pltpu.VMEM((tile, inner_width), F32),
            pltpu.VMEM((6, 8, width), F32),
            pltpu.VMEM((8, inner_width), F32),
            pltpu.SemaphoreType.DMA((sum(len(p) for p in numbered),)),
        ],
        compiler_params=params(),
        cost_estimate=cost(4e10, 5e7),
        name="feed",
    )(mixed_t, tokens, cotangent, seg, vec, bias_inner, *arrays)


def attend_back_kernel(n_after, q_ref, k_ref, v_ref, dm_ref, lse_ref, seg_ref, table_ref, *refs):
    dqkv_ref, total_ref, bias_ref, sums_ref = refs[n_after:]

    @pl.when(pl.program_id(0) == 0)
    def _():
        sums_ref[...] = jnp.zeros_like(sums_ref)

    width = q_ref.shape[1]
    scale = 1.0 / math.sqrt(HD)
    seg = seg_ref[0:1, :]
    bias_ref[...] = jnp.where(column_of(seg) == seg, 0.0, -1e30)
    low = lax.broadcasted_iota(jnp.int32, (1, 2 * HD), 1) < HD
    slots = q_ref.shape[0]
    halves = lambda a: (a[:slots], a[slots:])
    for pair in range(width // (2 * HD)):
        first = pair * 2 * HD
        sl = slice(first, first + 2 * HD)
        queries = q_ref[:, sl] * BF(scale)
        keys, d_mixed = k_ref[:, sl], dm_ref[:, sl]
        scores = halves(dot(split_lanes(keys), queries, NT))
        d_probs = halves(dot(split_lanes(v_ref[:, sl]), d_mixed, NT))
        probs_low, d_scores = [], []
        for half in range(2):
            head = 2 * pair + half
            probs = jnp.exp(scores[half] + bias_ref[...] - lse_ref[head : head + 1, :])
            probs_low.append(probs.astype(BF))
            weighted = probs * d_probs[half]
            rows = jnp.sum(weighted, axis=0, keepdims=True)
            d_scores.append((weighted - probs * rows).astype(BF))
        d_scores = jnp.concatenate(d_scores, axis=0)
        d_value = jnp.where(low, *halves(dot(jnp.concatenate(probs_low, axis=0), d_mixed))).astype(BF)
        d_key = jnp.where(low, *halves(dot(d_scores, queries))).astype(BF)
        d_query = (dot(split_rows(keys.T), d_scores) * scale).astype(BF).T
        for i, item in enumerate((d_query, d_key, d_value)):
            dqkv_ref[:, i * width + first : i * width + first + 2 * HD] = item
        sums_ref[0, :, sl] += column_sum(d_query.astype(F32))
        sums_ref[1, :, sl] += column_sum(d_value.astype(F32))

    @pl.when(pl.program_id(0) == pl.num_programs(0) - 1)
    def _():
        total_ref[...] = table_ref[...]
        for i in range(2):
            total_ref[i : i + 1, :] = jnp.sum(sums_ref[i], axis=0, keepdims=True)


def attend_back(query, keys, values, d_mixed, lse, seg, table, after=()):
    count, width = query.shape
    rows = seg.shape[0] // 8
    slots = seg.shape[1]
    row = pl.BlockSpec((slots, width), lambda i: (i, 0))
    return pl.pallas_call(
        functools.partial(attend_back_kernel, len(after)),
        grid=(rows,),
        in_specs=[row] * 4
        + [
            pl.BlockSpec((lse.shape[0] // rows, slots), lambda i: (i, 0)),
            pl.BlockSpec((8, slots), lambda i: (i, 0)),
            whole(table.shape),
        ]
        + anywhere(len(after)),
        out_specs=[
            pl.BlockSpec((slots, 3 * width), lambda i: (i, 0)),
            pl.BlockSpec(table.shape, lambda i: (0, 0)),
        ],
        out_shape=[jax.ShapeDtypeStruct((count, 3 * width), BF), jax.ShapeDtypeStruct(table.shape, F32)],
        scratch_shapes=[pltpu.VMEM((slots, slots), F32), pltpu.VMEM((2, 8, width), F32)],
        compiler_params=params(),
        cost_estimate=cost(2.1e10, 1.5e7),
        name="attend_back",
    )(query, keys, values, d_mixed, lse, seg, table, *after)


def tokens_kernel(numbered, n_arrays, n_after, dfirst_ref, dqkv_ref, *refs):
    pieces = refs[:n_arrays]
    out_ref, w_ref, sems = refs[n_arrays + n_after :]
    width = dfirst_ref.shape[1]
    ready = load_weights(numbered, pieces, [w_ref.at[which] for which in range(3)], sems)
    total = dfirst_ref[...]
    for which in range(3):
        ready(which)
        total = total + dot(dqkv_ref[:, which * width : (which + 1) * width], w_ref[which], NT)
    out_ref[...] = total


def tokens_back(d_first, dqkv, weights, after=()):
    count, width = d_first.shape
    arrays, numbered = index_pieces(weights)
    tile = ROW_TILE
    return pl.pallas_call(
        functools.partial(tokens_kernel, numbered, len(arrays), len(after)),
        grid=(count // tile,),
        in_specs=[
            pl.BlockSpec((tile, width), lambda i: (i, 0)),
            pl.BlockSpec((tile, 3 * width), lambda i: (i, 0)),
        ]
        + anywhere(len(arrays) + len(after)),
        out_specs=pl.BlockSpec((tile, width), lambda i: (i, 0)),
        out_shape=jax.ShapeDtypeStruct((count, width), F32),
        scratch_shapes=[
            pltpu.VMEM((3, width, width), BF),
            pltpu.SemaphoreType.DMA((sum(len(p) for p in numbered),)),
        ],
        compiler_params=params(),
        cost_estimate=cost(1e10, 1.5e7),
        name="tokens_back",
    )(d_first, dqkv, *arrays, *after)


ORDER_ONE, ORDER_TWO = (0, Y, X, X | Y), (0, X, Y, X | Y)


def arrange(left_ref, left, order):
    size = left.shape[0] // (2 * len(order))
    for which in range(2):
        for place, rel in enumerate(order):
            start = pl.multiple_of((lax.axis_index("fsdp") ^ (rel | which * CORE)) * size, size)
            at = (which * len(order) + place) * size
            left_ref[at : at + size, :] = left[pl.ds(start, size), :]


def place_rows(got, keep, send):
    places, size, _ = keep.shape
    for which, out in enumerate((keep, send)):
        for place in range(places):
            at = (which * places + place) * size
            out[place] = got[at : at + size, :]


def inner_grad_kernel(order, n_after, left, right, *refs):
    keep, send, left_ref = refs[n_after:]

    @pl.when(pl.program_id(0) == 0)
    def _():
        arrange(left_ref, left, order)

    place_rows(dot(left_ref[...], right[...]).astype(BF), keep, send)


def inner_grad(left, right, shards, after=()):
    height, depth = left.shape
    wide = right.shape[1]
    chunk = height
    shape = (4, height // shards, wide)
    return pl.pallas_call(
        functools.partial(inner_grad_kernel, ORDER_ONE, len(after)),
        grid=(wide // chunk,),
        in_specs=[whole((height, depth)), pl.BlockSpec((depth, chunk), lambda g: (0, g))] + anywhere(len(after)),
        out_specs=[pl.BlockSpec((*shape[:2], chunk), lambda g: (0, 0, g))] * 2,
        out_shape=[jax.ShapeDtypeStruct(shape, BF)] * 2,
        scratch_shapes=[pltpu.VMEM((height, depth), BF)],
        compiler_params=params(),
        cost_estimate=cost(3.5 * height * depth * wide, 4 * height * wide),
        name="inner_grad",
    )(left, right, *after)


def outer_grad_kernel(_, left, right, keep, send, acc_ref):
    acc_ref[...] = dot(left[...], right[...])
    rows = keep.shape[1]
    wide = acc_ref.shape[1] // 2
    core = lax.axis_index("fsdp") & CORE
    for which, out in enumerate((keep, send)):
        start = pl.multiple_of((core ^ which) * wide, 128)
        for block in range(acc_ref.shape[0] // rows):
            part_rows = acc_ref[block * rows : (block + 1) * rows, pl.ds(start, wide)]
            out[0, :, block * wide : (block + 1) * wide] = part_rows.astype(BF)


def outer_grad(left, right, shards):
    height, depth = left.shape
    wide = right.shape[1]
    chips = lax.axis_index("fsdp") // 2
    places = jnp.stack([chips ^ (rel // 2) for rel in ORDER_TWO]).astype(jnp.int32)
    chunk = 2 * wide // shards
    shape = (4, height // shards, wide)
    return pl.pallas_call(
        outer_grad_kernel,
        grid_spec=pltpu.PrefetchScalarGridSpec(
            num_scalar_prefetch=1,
            grid=(4,),
            in_specs=[
                pl.BlockSpec((height, depth), lambda g, p: (0, 0), pipeline_mode=pl.Buffered(1)),
                pl.BlockSpec((depth, chunk), lambda g, p: (0, p[g])),
            ],
            out_specs=[pl.BlockSpec((1, *shape[1:]), lambda g, p: (g, 0, 0))] * 2,
            scratch_shapes=[pltpu.VMEM((height, chunk), F32)],
        ),
        out_shape=[jax.ShapeDtypeStruct(shape, BF)] * 2,
        compiler_params=params(),
        cost_estimate=cost(3.5 * height * depth * wide, 4 * height * wide),
        name="outer_grad",
    )(places, left, right)


def square_grad_kernel(n_after, tokens, mixed, dqkv, d_branch, *refs):
    keep_one, send_one, keep_two, send_two, left_ref = refs[n_after:]
    step = pl.program_id(0)
    for at, left, order in ((0, tokens, ORDER_ONE), (2, tokens, ORDER_TWO), (3, mixed, ORDER_TWO)):

        @pl.when(step == at)
        def _():
            arrange(left_ref, left, order)

    @pl.when(step < 2)
    def _():
        place_rows(dot(left_ref[...], dqkv[...]).astype(BF), keep_one, send_one)

    @pl.when(step == 2)
    def _():
        place_rows(dot(left_ref[...], dqkv[...]).astype(BF), keep_two, send_two)

    @pl.when(step == 3)
    def _():
        place_rows(dot(left_ref[...], d_branch[...]).astype(BF), keep_two, send_two)


def square_grad(tokens_t, mixed_t, dqkv, d_branch, shards, after=()):
    height, depth = tokens_t.shape
    shape = (4, height // shards, 2 * height)
    block = (*shape[:2], height)
    one = pl.BlockSpec(block, lambda g: (0, 0, jnp.minimum(g, 1)))
    two = pl.BlockSpec(block, lambda g: (0, 0, jnp.maximum(g - 2, 0)))
    return pl.pallas_call(
        functools.partial(square_grad_kernel, len(after)),
        grid=(4,),
        in_specs=[
            whole((height, depth)),
            whole((height, depth)),
            pl.BlockSpec((depth, height), lambda g: (0, jnp.minimum(g, 2))),
            whole((depth, height)),
        ]
        + anywhere(len(after)),
        out_specs=[one, one, two, two],
        out_shape=[jax.ShapeDtypeStruct(shape, BF)] * 4,
        scratch_shapes=[pltpu.VMEM((height, depth), BF)],
        compiler_params=params(),
        cost_estimate=cost(1.1e10, 1.5e7),
        name="square_grad",
    )(tokens_t, mixed_t, dqkv, d_branch, *after)


def up(x):
    return x.astype(F32)


def fetch(terms, held_ref, sems):
    at, copies, found = 0, [], []
    for i, (ref, first, count) in enumerate(terms):
        copies.append(pltpu.make_async_copy(ref.at[pl.ds(first, count)], held_ref.at[pl.ds(at, count)], sems.at[i]))
        found.append(at)
        at += count
    for copy in copies:
        copy.start()
    for copy in copies:
        copy.wait()
    return found


def add_places(terms, places):
    total = up(terms[0][places])
    for term in terms[1:]:
        total = total + up(term[places])
    return total.astype(BF)


def total_kernel(n_after, *refs):
    table_ref = refs[8]
    keep, send, copy_ref, held_ref, sems = refs[9 + n_after :]
    copy_ref[...] = table_ref[...]
    size = keep.shape[2]
    me = lax.axis_index("rep")
    places = fetch([(ref, 0, 1) for ref in refs[:8]], held_ref, sems)
    for quarter in range(4):
        i, columns = quarter // 2, slice(quarter % 2 * size, (quarter % 2 + 1) * size)
        total = up(held_ref[places[4 * i], :, columns])
        for place in places[4 * i + 1 : 4 * i + 4]:
            total = total + up(held_ref[place, :, columns])
        rel = me ^ quarter
        for bit, out in enumerate((keep, send)):

            @pl.when(rel & 1 == bit)
            def _():
                out[rel // 2] = total.astype(BF)


def total_places(one, two, table, after):
    _, rows, wide = one[0].shape
    shape = (2, rows, wide // 2)
    return pl.pallas_call(
        functools.partial(total_kernel, len(after)),
        in_specs=anywhere(8) + [pl.BlockSpec(memory_space=pltpu.VMEM)] + anywhere(len(after)),
        out_shape=[jax.ShapeDtypeStruct(shape, BF)] * 2 + [jax.ShapeDtypeStruct(table.shape, F32)],
        scratch_shapes=[
            pltpu.VMEM((8, rows, wide), BF),
            pltpu.SemaphoreType.DMA((8,)),
        ],
        compiler_params=pltpu.CompilerParams(vmem_limit_bytes=VMEM_BYTES),
        cost_estimate=cost(3e10, 1e7),
        name="total",
    )(*one, *two, table, *after)


class Sum:
    def __init__(self, *groups):
        self.terms = [[keep, flip(send, "fsdp", CORE)] for keep, send in groups]
        self.bits = (X, Y), (Y, X)

    def far(self, group, *after):
        terms = pinned(self.terms[group], *after)
        out = add_places(terms, slice(2, 4))
        self.terms[group] = [*terms, flip(out, "fsdp", self.bits[group][0])]
        return out

    def near(self, group, *after):
        terms = pinned(self.terms[group], *after)
        out = add_places(terms, slice(1, 2))
        self.terms[group] = [*terms, flip(out, "fsdp", self.bits[group][1])]
        return out

    def total(self, table, after=()):
        self.part, send, table = total_places(*self.terms, table, after)
        self.rep = flip(send, "rep", 1)
        return self.part, table

    def rep_near(self):
        self.rep_far = flip((up(self.part[1]) + up(self.rep[1])).astype(BF), "rep", 2)

    def parts(self):
        self.mine = (up(self.part[0]) + up(self.rep[0]) + up(self.rep_far)).astype(BF)
        two = flip(self.mine, "rep", 2)
        return [self.mine, flip(self.mine, "rep", 1), two, flip(two, "rep", 1)]


def finish_kernel(factor, feed_weights, *refs):
    parts, outs, held_ref = refs[:4], refs[4:-1], refs[-1]
    me = lax.axis_index("rep")
    for rel, ref in enumerate(parts):
        held_ref[me ^ rel] = up(ref[...]) * factor
    if not feed_weights:
        for i, out in enumerate(outs):
            out[...] = held_ref[i]
        return
    inner_ref, outer_ref = outs
    size = held_ref.shape[2]
    for i in range(2):
        inner_ref[:, i * size : (i + 1) * size] = held_ref[i]
    rows, width = outer_ref.shape
    blocks = []
    for i in range(2):
        blocks += [held_ref[2 + i, :, at : at + rows] for at in range(0, size, rows)]
    outer_ref[...] = jnp.concatenate(blocks, axis=0).T


def finish(parts, factor, shapes, feed_weights):
    rows, size = parts[0].shape
    return pl.pallas_call(
        functools.partial(finish_kernel, factor, feed_weights),
        out_shape=[jax.ShapeDtypeStruct(shape, F32) for shape in shapes],
        scratch_shapes=[pltpu.VMEM((4, rows, size), F32)],
        compiler_params=pltpu.CompilerParams(vmem_limit_bytes=VMEM_BYTES),
        cost_estimate=cost(2e9, 1e7),
        name="finish",
    )(*parts)


def all_sum(values, axes=("fsdp", "rep")):
    for axis in axes:
        n = lax.axis_size(axis)
        if n & (n - 1):
            values = lax.psum(values, axis)
            continue
        bit = 1
        while bit < n:
            values = values + flip(values, axis, bit)
            bit *= 2
    return values


def body(
    tokens,
    doc_lengths,
    query_weight,
    key_weight,
    value_weight,
    output_weight,
    inner_weight,
    outer_weight,
    query_bias,
    value_bias,
    output_bias,
    inner_bias,
    outer_bias,
    first_gain,
    first_shift,
    second_gain,
    second_shift,
    cotangent,
):
    rows, slots, width = tokens.shape
    count = rows * slots
    docs = doc_lengths.shape[1]
    n_fsdp = lax.axis_size("fsdp")
    n_rep = lax.axis_size("rep")
    shard = query_weight.shape[0]
    outer_shard = outer_weight.shape[0]
    inner_width = inner_weight.shape[1]
    direct = n_fsdp == 8 and n_rep == 4 and shard % 16 == 0

    vectors = (
        query_bias,
        value_bias,
        output_bias,
        outer_bias,
        first_gain,
        first_shift,
        second_gain,
        second_shift,
        inner_bias,
    )
    if direct:
        half, outer_half = shard // 2, outer_shard // 2
        blocks = pack(query_weight, key_weight, value_weight, inner_weight, output_weight, outer_weight, vectors)
        one, two = Gather(blocks[0], X, Y), Gather(blocks[1], Y, X)
        blocks = pinned(blocks[2:], one.near, two.near)
        three, four = Gather(blocks[0], X, Y), Gather(blocks[1], Y, X)
        pairs = stacked(one.block, one.near, two.block, two.near)
        one.go(pairs[0])
        two.go(pairs[1])
        pairs = stacked(three.block, three.near, four.block, four.near, pairs)
        three.go(pairs[0])
        four.go(pairs[1])
        chips_x, chips_y = stacked(one.pair, one.far, two.pair, two.far, pairs)
        held_x, held_y = one.held_whole(chips_x), two.held_whole(chips_y)
        qw = part(held_x, 0, shard, shard)
        kw = part(held_x, shard, half, shard) + part(held_y, shard, half, shard, half)
        vw = part(held_y, 0, shard, shard)
        vec, bias_inner = unpack(part(held_x, shard + half, 16, 16), shard, outer_shard)
    else:
        qw, kw, vw, ow, iw, w2 = [
            [(lax.all_gather(w, "fsdp", axis=0, tiled=True), 0, w.shape[0] * n_fsdp, None, 0, 0, 0)]
            for w in (query_weight, key_weight, value_weight, output_weight, inner_weight, outer_weight)
        ]
        small = lax.all_gather(jnp.concatenate(vectors)[None], "fsdp", axis=0, tiled=True).astype(F32)
        vec = small[:, : 8 * shard].reshape(n_fsdp, 8, shard).transpose(1, 0, 2).reshape(8, width)
        bias_inner = small[:, 8 * shard :].reshape(1, inner_width)
        pairs = ()

    places = jnp.arange(docs, dtype=jnp.int32)
    ends = jnp.sum(
        jnp.where(places[None, :, None] >= places[None, None, :], doc_lengths[:, None, :], 0), axis=-1
    )
    slot = jnp.arange(slots, dtype=jnp.int32)
    segment = jnp.sum((slot[None, None, :] >= ends[:, :, None]).astype(jnp.int32), axis=1)
    seg = jnp.broadcast_to(segment[:, None, :].astype(F32), (rows, 8, slots)).reshape(rows * 8, slots)

    flat = tokens.reshape(count, width)
    query, keys, values, mixed_t, tokens_t, lse = attend(flat, seg, vec, (qw, kw, vw), pairs)
    if direct:
        three.far, four.far = pinned((three.far, four.far), lse)
        held_x, held_y = three.held(), four.held()
        iw = part(held_x, 0, half, shard) + part(held_y, 0, half, shard, half)
        ow = [(*piece[:-1], inner_width) for piece in iw]
        w2 = [
            (*piece[:4], outer_shard, which * outer_half + block * half, inner_width + (1 + block) * width)
            for which, held in enumerate((held_x, held_y))
            for block in range(outer_half // half)
            for piece in part(held, 0, half, shard)
        ]
    encoded, hidden_t, activated, d_outer_t, d_inner, d_first, d_branch, d_mixed, table = feed(
        mixed_t, flat, cotangent.reshape(count, width), seg, vec, bias_inner, (ow, iw, w2), docs
    )
    factor = 1.0 / math.sqrt(rows * n_rep * n_fsdp * slots)
    if direct:
        keep_outer, send_outer = outer_grad(d_outer_t, activated, n_fsdp)
        keep_inner, send_inner = inner_grad(hidden_t, d_inner, n_fsdp, (send_outer,))
        wide = Sum((keep_inner, send_inner), (keep_outer, send_outer))
        far = wide.far(1, send_inner)
        far = wide.far(0, far)
        dqkv, table = attend_back(query, keys, values, d_mixed, lse, seg, table, (far,))
        near = wide.near(1, dqkv)
        near = wide.near(0, near)
        keep_one, send_one, keep_two, send_two = square_grad(tokens_t, mixed_t, dqkv, d_branch, n_fsdp, (near,))
        square = Sum((keep_one, send_one), (keep_two, send_two))
        total, table = wide.total(table, (send_one,))
        far = square.far(0, total)
        far = square.far(1, far)
        tokens_grad = tokens_back(d_first, dqkv, (qw, kw, vw), (far,))
        wide.rep_near()
        wide_parts = wide.parts()
        near = square.near(0, tokens_grad, wide.mine)
        square.near(1, near)
        _, table = square.total(table)
        square.rep_near()
        inner_all, outer_all = finish(wide_parts, factor, (inner_weight.shape, outer_weight.shape), True)
        q_all, k_all, v_all, o_all = finish(square.parts(), factor, (query_weight.shape,) * 4, False)
    else:
        dqkv, table = attend_back(query, keys, values, d_mixed, lse, seg, table)
        tokens_grad = tokens_back(d_first, dqkv, (qw, kw, vw))

        def shared(left_t, right):
            total = lax.psum_scatter(dot(left_t, right), "fsdp", scatter_dimension=0, tiled=True)
            return up(lax.psum(total.astype(BF), "rep")) * factor

        outer_all = shared(activated.T, d_outer_t.T)
        inner_all = shared(hidden_t, d_inner)
        o_all = shared(mixed_t, d_branch)
        q_all, k_all, v_all = [shared(tokens_t, item) for item in jnp.split(dqkv, 3, axis=1)]
    vectors = all_sum(table[: 8 + inner_width // width]) * factor
    me = lax.axis_index("fsdp")
    short = lax.dynamic_slice_in_dim(vectors[:8], me * shard, shard, axis=1)
    long = lax.dynamic_slice_in_dim(vectors[8:].reshape(inner_width), me * outer_shard, outer_shard, axis=0)
    return (
        encoded.reshape(rows, slots, width),
        tokens_grad.reshape(rows, slots, width),
        q_all,
        k_all,
        v_all,
        o_all,
        inner_all,
        outer_all,
        short[0],
        short[1],
        short[2],
        long,
        short[3],
        short[4],
        short[5],
        short[6],
        short[7],
    )


def solution(mesh):
    data = P(("rep", "fsdp"), None, None)
    matrix, vector = P("fsdp", None), P("fsdp")
    return jax.shard_map(
        body,
        mesh=mesh,
        in_specs=(data, P(("rep", "fsdp"), None)) + (matrix,) * 6 + (vector,) * 9 + (data,),
        out_specs=(data, data) + (matrix,) * 6 + (vector,) * 9,
        check_vma=False,
    )
```

```python
import functools
import math

import jax
import jax.numpy as jnp
from jax import lax
from jax.experimental import pallas as pl
from jax.experimental.pallas import tpu as pltpu
from jax.sharding import PartitionSpec as P

HD = 64
EPSILON = 1e-05
BF = jnp.bfloat16
F32 = jnp.float32
NT = ((1,), (1,))
VMEM_BYTES = 60 * 2**20
CORE, X, Y = 1, 2, 4
ROW_TILE = 256
FF_CHUNK = 1536


def dot(a, b, dims=((1,), (0,))):
    return lax.dot_general(a, b, (dims, ((), ())), preferred_element_type=F32)


def params():
    return pltpu.CompilerParams(
        vmem_limit_bytes=VMEM_BYTES, dimension_semantics=("arbitrary",)
    )


def cost(flops, nbytes, trans=0):
    return pl.CostEstimate(
        flops=int(flops), bytes_accessed=int(nbytes), transcendentals=int(trans)
    )


def whole(shape):
    return pl.BlockSpec(
        shape, lambda *i: (0,) * len(shape), pipeline_mode=pl.Buffered(1)
    )


def anywhere(count):
    return [pl.BlockSpec(memory_space=pl.ANY)] * count


def flip(array, axis, bit):
    size = lax.axis_size(axis)
    return lax.ppermute(array, axis, [(i, i ^ bit) for i in range(size)])


def pinned(values, *others):
    return lax.optimization_barrier((values, others))[0]


def piece_copies(pieces, refs, target, sems, first):
    copies = []
    for slot, (which, start, rows, rel, shard, offset, column) in enumerate(pieces):
        place = 0
        if rel is not None:
            place = pl.multiple_of((lax.axis_index("fsdp") ^ rel) * shard + offset, math.gcd(shard, offset))
        copies.append(
            pltpu.make_async_copy(
                refs[which].at[pl.ds(start, rows), pl.ds(column, target.shape[1])],
                target.at[pl.ds(place, rows), :],
                sems.at[first + slot],
            )
        )
    return copies


def group_copies(numbered, refs, targets, sems):
    copies = []
    for pieces, target in zip(numbered, targets):
        copies.append(piece_copies(pieces, refs, target, sems, sum(len(c) for c in copies)))
    return copies


def index_pieces(weights):
    arrays, numbered = [], []
    for pieces in weights:
        mine = []
        for array, *rest in pieces:
            for n, seen in enumerate(arrays):
                if seen is array:
                    break
            else:
                n = len(arrays)
                arrays.append(array)
            mine.append((n, *rest))
        numbered.append(mine)
    return arrays, numbered


class Gather:
    def __init__(self, block, first, second):
        self.block, self.bits = block, (first, second)
        self.near = flip(block, "fsdp", first)

    def go(self, pair):
        self.pair = pair
        self.far = flip(pair, "fsdp", self.bits[1])
        return pair

    def parts(self):
        first, second = self.bits
        rows = self.block.shape[0]
        return [(self.pair, 0, 0), (self.pair, rows, first), (self.far, 0, second), (self.far, rows, first | second)]

    def held(self):
        other = {id(a): flip(a, "fsdp", CORE) for a in (self.pair, self.far)}
        return self.parts() + [(other[id(a)], at, rel | CORE) for a, at, rel in self.parts()]

    def held_whole(self, chips):
        first, second = self.bits
        rels = (0, first, second, first | second)
        return [
            (array, place * self.block.shape[0], rel | core)
            for core, array in ((0, chips), (CORE, flip(chips, "fsdp", CORE)))
            for place, rel in enumerate(rels)
        ]


def stack_kernel(n_after, one, two, three, four, *refs):
    for out, parts in zip(refs[n_after:], ((one, two), (three, four))):
        at = 0
        for ref in parts:
            rows = ref.shape[0]
            out[at : at + rows, :] = ref[...]
            at += rows


def stacked(one, two, three, four, after=()):
    full = lambda a: pl.BlockSpec(a.shape, lambda g: (0, 0))
    outs = [
        jax.ShapeDtypeStruct((a.shape[0] + b.shape[0], a.shape[1]), BF) for a, b in ((one, two), (three, four))
    ]
    return pl.pallas_call(
        functools.partial(stack_kernel, len(after)),
        grid=(1,),
        in_specs=[full(a) for a in (one, two, three, four)] + anywhere(len(after)),
        out_specs=[full(a) for a in outs],
        out_shape=outs,
        compiler_params=params(),
        cost_estimate=cost(2e9, 3e6),
        name="stacked",
    )(one, two, three, four, *after)


def pack_kernel(half, query_ref, key_ref, value_ref, wi_ref, wo_ref, w2_ref, *refs):
    vectors, (one_ref, two_ref, three_ref, four_ref) = refs[:-4], refs[-4:]
    shard, width = query_ref.shape
    one_ref[:shard, :] = query_ref[...]
    one_ref[shard : shard + half, :] = key_ref[:half, :]
    two_ref[:shard, :] = value_ref[...]
    two_ref[shard:, :] = key_ref[half:, :]
    rows = []
    for ref in vectors:
        size = ref.shape[0]
        rows.append(
            jnp.concatenate([ref[...].astype(F32).reshape(1, size), jnp.zeros((1, width - size), F32)], axis=1)
        )
    rows.append(jnp.zeros((16 - len(rows), width), F32))
    one_ref[shard + half :, :] = jnp.concatenate(rows, axis=0).astype(BF)
    wide = wi_ref.shape[1]
    blocks = w2_ref.shape[0] // (2 * half)
    for place, ref in enumerate((three_ref, four_ref)):
        ref[:, :wide] = wi_ref[place * half : (place + 1) * half, :]
        ref[:, wide : wide + width] = wo_ref[place * half : (place + 1) * half, :]
        for block in range(blocks):
            row, column = (place * blocks + block) * half, wide + (1 + block) * width
            ref[:, column : column + width] = w2_ref[row : row + half, :]


def pack(query, key, value, inner, output, outer, vectors):
    shard, width = query.shape
    half = shard // 2
    wide = inner.shape[1] + width * (1 + outer.shape[0] // (2 * half))
    return pl.pallas_call(
        functools.partial(pack_kernel, half),
        out_shape=[
            jax.ShapeDtypeStruct((shard + half + 16, width), BF),
            jax.ShapeDtypeStruct((shard + half, width), BF),
            jax.ShapeDtypeStruct((half, wide), BF),
            jax.ShapeDtypeStruct((half, wide), BF),
        ],
        compiler_params=pltpu.CompilerParams(vmem_limit_bytes=VMEM_BYTES),
        name="pack",
    )(query, key, value, inner, output, outer, *vectors)


def unpack_kernel(numbered, n_arrays, shard, long, *refs):
    pieces = refs[:n_arrays]
    vec_ref, inner_ref, held_ref, sems = refs[n_arrays:]
    copies = piece_copies(numbered[0], pieces, held_ref, sems, 0)
    for copy in copies:
        copy.start()
    for copy in copies:
        copy.wait()
    n = len(copies)
    parts = [held_ref[16 * i : 16 * i + 16, :] for i in range(n)]
    slot = lax.broadcasted_iota(jnp.int32, (n * 128, n * shard), 0)
    place = lax.broadcasted_iota(jnp.int32, (n * 128, n * shard), 1)
    at = slot % 128
    spread = ((at < shard) & (place == slot // 128 * shard + at)).astype(BF)
    vec_ref[...] = dot(jnp.concatenate([p[:, :128] for p in parts], axis=1), spread)[:8]
    for i, p in enumerate(parts):
        inner_ref[:, i * long : (i + 1) * long] = p[8:9, :long].astype(F32)


def unpack(pieces, shard, long):
    arrays, numbered = index_pieces([pieces])
    n, width = len(pieces), pieces[0][0].shape[1]
    return pl.pallas_call(
        functools.partial(unpack_kernel, numbered, len(arrays), shard, long),
        in_specs=anywhere(len(arrays)),
        out_shape=[
            jax.ShapeDtypeStruct((8, n * shard), F32),
            jax.ShapeDtypeStruct((1, n * long), F32),
        ],
        scratch_shapes=[pltpu.VMEM((16 * n, width), BF), pltpu.SemaphoreType.DMA((n,))],
        name="unpack",
    )(*arrays)


def part(held, start, rows, shard, offset=0):
    return [(a, at + start, rows, rel, shard, offset, 0) for a, at, rel in held]


def column_of(row):
    return jnp.broadcast_to(row, (128, row.shape[1])).T[:, :1]


def split_lanes(pair):
    low = lax.broadcasted_iota(jnp.int32, (1, 2 * HD), 1) < HD
    return jnp.concatenate([jnp.where(low, pair, BF(0)), jnp.where(low, BF(0), pair)], axis=0)


def split_rows(pair_t):
    low = lax.broadcasted_iota(jnp.int32, (2 * HD, 1), 0) < HD
    return jnp.concatenate([jnp.where(low, pair_t, BF(0)), jnp.where(low, BF(0), pair_t)], axis=1)


def attend_kernel(numbered, n_arrays, n_after, heads, tok_ref, seg_ref, vec_ref, *refs):
    pieces = refs[:n_arrays]
    q_ref, k_ref, v_ref, mt_ref, tt_ref, lse_ref, w_ref, bias_ref, qs_ref, sems = refs[n_arrays + n_after :]
    ready = load_weights(numbered, pieces, [w_ref.at[which] for which in range(3)], sems)
    x = tok_ref[...]
    tt_ref[...] = x.T
    seg = seg_ref[0:1, :]
    bias_ref[...] = jnp.where(column_of(seg) == seg, 0.0, -1e30)

    for which in range(3):
        ready(which)
    q = (dot(x, w_ref[0]) + vec_ref[0:1, :]).astype(BF)
    q_ref[...] = q
    qs_ref[...] = q * BF(1.0 / math.sqrt(HD))
    k_ref[...] = dot(x, w_ref[1]).astype(BF)
    v_ref[...] = (dot(x, w_ref[2]) + vec_ref[1:2, :]).astype(BF)
    for pair in range(heads // 2):
        sl = slice(pair * 2 * HD, (pair + 1) * 2 * HD)
        scores = dot(split_lanes(k_ref[:, sl]), qs_ref[:, sl], NT)
        slots = scores.shape[0] // 2
        weights, inverse = [], []
        for half in range(2):
            mine = scores[half * slots : (half + 1) * slots] + bias_ref[...]
            top = jnp.max(mine, axis=0, keepdims=True)
            exps = jnp.exp(mine - top)
            total = jnp.sum(exps, axis=0, keepdims=True)
            head = 2 * pair + half
            lse_ref[head : head + 1, :] = top + jnp.log(total)
            weights.append(exps.astype(BF))
            inverse.append(1.0 / total)
        out = dot(split_rows(v_ref[:, sl].T), jnp.concatenate(weights, axis=0))
        low_rows = lax.broadcasted_iota(jnp.int32, (2 * HD, 1), 0) < HD
        mt_ref[sl, :] = (out * jnp.where(low_rows, inverse[0], inverse[1])).astype(BF)


def attend(tokens, seg, vec, weights, after=()):
    count, width = tokens.shape
    rows = seg.shape[0] // 8
    slots = count // rows
    heads = width // HD
    padded = -(-heads // 8) * 8
    arrays, numbered = index_pieces(weights)
    row = pl.BlockSpec((slots, width), lambda i: (i, 0))
    col = pl.BlockSpec((width, slots), lambda i: (0, i))
    return pl.pallas_call(
        functools.partial(attend_kernel, numbered, len(arrays), len(after), heads),
        grid=(rows,),
        in_specs=[row, pl.BlockSpec((8, slots), lambda i: (i, 0)), whole(vec.shape)]
        + anywhere(len(arrays) + len(after)),
        out_specs=[row, row, row, col, col, pl.BlockSpec((padded, slots), lambda i: (i, 0))],
        out_shape=[jax.ShapeDtypeStruct((count, width), BF)] * 3
        + [jax.ShapeDtypeStruct((width, count), BF)] * 2
        + [jax.ShapeDtypeStruct((rows * padded, slots), F32)],
        scratch_shapes=[
            pltpu.VMEM((3, width, width), BF),
            pltpu.VMEM((slots, slots), F32),
            pltpu.VMEM((slots, width), BF),
            pltpu.SemaphoreType.DMA((sum(len(p) for p in numbered),)),
        ],
        compiler_params=params(),
        cost_estimate=cost(1e9, 1e6),
        name="attend",
    )(tokens, seg, vec, *arrays, *after)


def gelu_pair(v):
    area = 0.5 + 0.5 * lax.erf(v * math.sqrt(0.5))
    density = jnp.exp2(v * v * (-0.5 / math.log(2.0))) * (1.0 / math.sqrt(2.0 * math.pi))
    return v * area, area + v * density


def norm(z):
    center = z - jnp.mean(z, axis=-1, keepdims=True)
    scale = lax.rsqrt(jnp.mean(center * center, axis=-1, keepdims=True) + EPSILON)
    return center * scale, scale


def norm_back(grad, n, scale, gain):
    dn = grad * gain
    return (
        dn - jnp.mean(dn, axis=-1, keepdims=True) - n * jnp.mean(dn * n, axis=-1, keepdims=True)
    ) * scale


def column_sum(x):
    return jnp.sum(x.reshape(x.shape[0] // 8, 8, x.shape[1]), axis=0)


def load_weights(numbered, pieces, targets, sems):
    groups = group_copies(numbered, pieces, targets, sems)
    first_step = pl.program_id(0) == 0

    @pl.when(first_step)
    def _():
        for copies in groups:
            for copy in copies:
                copy.start()

    def ready(which):
        @pl.when(first_step)
        def _():
            for copy in groups[which]:
                copy.wait()

    return ready


def vector(vec_ref, i):
    return vec_ref[i : i + 1, :]


def feed_kernel(numbered, n_arrays, docs, mt_ref, tok_ref, cot_ref, seg_ref, vec_ref, bi_ref, *refs):
    pieces = refs[:n_arrays]
    outs = refs[n_arrays:]
    enc_ref, ht_ref, act_ref, dot_ref, din_ref, dfirst_ref, dbr_ref, dm_ref, total_ref = outs[:9]
    wo_ref, wi_ref, w2_ref, slope_ref, sums_ref, sumi_ref, sems = outs[9:]
    ready = load_weights(numbered, pieces, (wo_ref, wi_ref, w2_ref), sems)

    @pl.when(pl.program_id(0) == 0)
    def _():
        sums_ref[...] = jnp.zeros_like(sums_ref)
        sumi_ref[...] = jnp.zeros_like(sumi_ref)

    width, inner_width = wi_ref.shape
    ready(0)
    z1 = tok_ref[...].astype(F32) + dot(mt_ref[...].T, wo_ref[...]) + vector(vec_ref, 2)
    n1, r1 = norm(z1)
    hidden = n1 * vector(vec_ref, 4) + vector(vec_ref, 5)
    hidden_low = hidden.astype(BF)
    ht_ref[...] = hidden_low.T
    ready(1)
    z2 = hidden + vector(vec_ref, 3)
    for c in range(0, inner_width, FF_CHUNK):
        sl = slice(c, c + FF_CHUNK)
        act, slope = gelu_pair(dot(hidden_low, wi_ref[:, sl]) + bi_ref[:, sl])
        act = act.astype(BF)
        act_ref[:, sl] = act
        slope_ref[:, sl] = slope
        if c == 0:
            ready(2)
        z2 = z2 + dot(act, w2_ref[sl, :])
    n2, r2 = norm(z2)
    gain = vector(vec_ref, 6)
    enc_ref[...] = (n2 * gain + vector(vec_ref, 7)).astype(BF)
    grad = cot_ref[...] * column_of((seg_ref[0:1, :] < docs).astype(F32))
    d_second = norm_back(grad, n2, r2, gain)
    d_outer = d_second.astype(BF)
    dot_ref[...] = d_outer.T
    d_hidden = d_second
    for c in range(0, inner_width, FF_CHUNK):
        sl = slice(c, c + FF_CHUNK)
        d_inner = (dot(d_outer, w2_ref[sl, :], NT) * slope_ref[:, sl]).astype(BF)
        din_ref[:, sl] = d_inner
        sumi_ref[:, sl] += column_sum(d_inner.astype(F32))
        d_hidden = d_hidden + dot(d_inner, wi_ref[:, sl], NT)
    d_first = norm_back(d_hidden, n1, r1, vector(vec_ref, 4))
    dfirst_ref[...] = d_first
    d_branch = d_first.astype(BF)
    dbr_ref[...] = d_branch
    dm_ref[...] = dot(d_branch, wo_ref[...], NT).astype(BF)
    for i, item in enumerate(
        (d_branch.astype(F32), d_outer.astype(F32), d_hidden * n1, d_hidden, grad * n2, grad)
    ):
        sums_ref[i] += column_sum(item)

    @pl.when(pl.program_id(0) == pl.num_programs(0) - 1)
    def _():
        total_ref[...] = jnp.zeros_like(total_ref)
        for i in range(6):
            total_ref[2 + i : 3 + i, :] = jnp.sum(sums_ref[i], axis=0, keepdims=True)
        for i in range(inner_width // width):
            part_sum = jnp.sum(sumi_ref[:, i * width : (i + 1) * width], axis=0, keepdims=True)
            total_ref[8 + i : 9 + i, :] = part_sum


def feed(mixed_t, tokens, cotangent, seg, vec, bias_inner, weights, docs):
    count, width = tokens.shape
    inner_width = bias_inner.shape[1]
    arrays, numbered = index_pieces(weights)
    tile = ROW_TILE
    row = pl.BlockSpec((tile, width), lambda i: (i, 0))
    col = pl.BlockSpec((width, tile), lambda i: (0, i))
    wide = pl.BlockSpec((tile, inner_width), lambda i: (i, 0))
    per_row = seg.shape[1] // tile
    sum_rows = -(-(8 + inner_width // width) // 8) * 8
    out = jax.ShapeDtypeStruct
    return pl.pallas_call(
        functools.partial(feed_kernel, numbered, len(arrays), docs),
        grid=(count // tile,),
        in_specs=[
            col,
            row,
            row,
            pl.BlockSpec((8, tile), lambda i: (i // per_row, i % per_row)),
            whole(vec.shape),
            whole(bias_inner.shape),
        ]
        + anywhere(len(arrays)),
        out_specs=[row, col, wide, col, wide, row, row, row, pl.BlockSpec((sum_rows, width), lambda i: (0, 0))],
        out_shape=[
            out((count, width), BF),
            out((width, count), BF),
            out((count, inner_width), BF),
            out((width, count), BF),
            out((count, inner_width), BF),
            out((count, width), F32),
            out((count, width), BF),
            out((count, width), BF),
            out((sum_rows, width), F32),
        ],
        scratch_shapes=[
            pltpu.VMEM((width, width), BF),
            pltpu.VMEM((width, inner_width), BF),
            pltpu.VMEM((inner_width, width), BF),
            pltpu.VMEM((tile, inner_width), F32),
            pltpu.VMEM((6, 8, width), F32),
            pltpu.VMEM((8, inner_width), F32),
            pltpu.SemaphoreType.DMA((sum(len(p) for p in numbered),)),
        ],
        compiler_params=params(),
        cost_estimate=cost(4e10, 5e7),
        name="feed",
    )(mixed_t, tokens, cotangent, seg, vec, bias_inner, *arrays)


def attend_back_kernel(n_after, q_ref, k_ref, v_ref, dm_ref, lse_ref, seg_ref, table_ref, *refs):
    dqkv_ref, total_ref, bias_ref, sums_ref = refs[n_after:]

    @pl.when(pl.program_id(0) == 0)
    def _():
        sums_ref[...] = jnp.zeros_like(sums_ref)

    width = q_ref.shape[1]
    scale = 1.0 / math.sqrt(HD)
    seg = seg_ref[0:1, :]
    bias_ref[...] = jnp.where(column_of(seg) == seg, 0.0, -1e30)
    low = lax.broadcasted_iota(jnp.int32, (1, 2 * HD), 1) < HD
    slots = q_ref.shape[0]
    halves = lambda a: (a[:slots], a[slots:])
    for pair in range(width // (2 * HD)):
        first = pair * 2 * HD
        sl = slice(first, first + 2 * HD)
        queries = q_ref[:, sl] * BF(scale)
        keys, d_mixed = k_ref[:, sl], dm_ref[:, sl]
        scores = halves(dot(split_lanes(keys), queries, NT))
        d_probs = halves(dot(split_lanes(v_ref[:, sl]), d_mixed, NT))
        probs_low, d_scores = [], []
        for half in range(2):
            head = 2 * pair + half
            probs = jnp.exp(scores[half] + bias_ref[...] - lse_ref[head : head + 1, :])
            probs_low.append(probs.astype(BF))
            weighted = probs * d_probs[half]
            rows = jnp.sum(weighted, axis=0, keepdims=True)
            d_scores.append((weighted - probs * rows).astype(BF))
        d_scores = jnp.concatenate(d_scores, axis=0)
        d_value = jnp.where(low, *halves(dot(jnp.concatenate(probs_low, axis=0), d_mixed))).astype(BF)
        d_key = jnp.where(low, *halves(dot(d_scores, queries))).astype(BF)
        d_query = (dot(split_rows(keys.T), d_scores) * scale).astype(BF).T
        for i, item in enumerate((d_query, d_key, d_value)):
            dqkv_ref[:, i * width + first : i * width + first + 2 * HD] = item
        sums_ref[0, :, sl] += column_sum(d_query.astype(F32))
        sums_ref[1, :, sl] += column_sum(d_value.astype(F32))

    @pl.when(pl.program_id(0) == pl.num_programs(0) - 1)
    def _():
        total_ref[...] = table_ref[...]
        for i in range(2):
            total_ref[i : i + 1, :] = jnp.sum(sums_ref[i], axis=0, keepdims=True)


def attend_back(query, keys, values, d_mixed, lse, seg, table, after=()):
    count, width = query.shape
    rows = seg.shape[0] // 8
    slots = seg.shape[1]
    row = pl.BlockSpec((slots, width), lambda i: (i, 0))
    return pl.pallas_call(
        functools.partial(attend_back_kernel, len(after)),
        grid=(rows,),
        in_specs=[row] * 4
        + [
            pl.BlockSpec((lse.shape[0] // rows, slots), lambda i: (i, 0)),
            pl.BlockSpec((8, slots), lambda i: (i, 0)),
            whole(table.shape),
        ]
        + anywhere(len(after)),
        out_specs=[
            pl.BlockSpec((slots, 3 * width), lambda i: (i, 0)),
            pl.BlockSpec(table.shape, lambda i: (0, 0)),
        ],
        out_shape=[jax.ShapeDtypeStruct((count, 3 * width), BF), jax.ShapeDtypeStruct(table.shape, F32)],
        scratch_shapes=[pltpu.VMEM((slots, slots), F32), pltpu.VMEM((2, 8, width), F32)],
        compiler_params=params(),
        cost_estimate=cost(2.1e10, 1.5e7),
        name="attend_back",
    )(query, keys, values, d_mixed, lse, seg, table, *after)


def tokens_kernel(numbered, n_arrays, n_after, dfirst_ref, dqkv_ref, *refs):
    pieces = refs[:n_arrays]
    out_ref, w_ref, sems = refs[n_arrays + n_after :]
    width = dfirst_ref.shape[1]
    targets = [w_ref.at[:, pl.ds(which * width, width)] for which in range(3)]
    ready = load_weights(numbered, pieces, targets, sems)
    for which in range(3):
        ready(which)
    out_ref[...] = dfirst_ref[...] + dot(dqkv_ref[...], w_ref[...], NT)


def tokens_back(d_first, dqkv, weights, after=()):
    count, width = d_first.shape
    arrays, numbered = index_pieces(weights)
    tile = ROW_TILE
    return pl.pallas_call(
        functools.partial(tokens_kernel, numbered, len(arrays), len(after)),
        grid=(count // tile,),
        in_specs=[
            pl.BlockSpec((tile, width), lambda i: (i, 0)),
            pl.BlockSpec((tile, 3 * width), lambda i: (i, 0)),
        ]
        + anywhere(len(arrays) + len(after)),
        out_specs=pl.BlockSpec((tile, width), lambda i: (i, 0)),
        out_shape=jax.ShapeDtypeStruct((count, width), F32),
        scratch_shapes=[
            pltpu.VMEM((width, 3 * width), BF),
            pltpu.SemaphoreType.DMA((sum(len(p) for p in numbered),)),
        ],
        compiler_params=params(),
        cost_estimate=cost(1e10, 1.5e7),
        name="tokens_back",
    )(d_first, dqkv, *arrays, *after)


ORDER_ONE, ORDER_TWO = (0, Y, X, X | Y), (0, X, Y, X | Y)


def arrange(left_ref, left, order):
    size = left.shape[0] // (2 * len(order))
    for which in range(2):
        for place, rel in enumerate(order):
            start = pl.multiple_of((lax.axis_index("fsdp") ^ (rel | which * CORE)) * size, size)
            at = (which * len(order) + place) * size
            left_ref[at : at + size, :] = left[pl.ds(start, size), :]


def place_rows(got, keep, send):
    places, size, _ = keep.shape
    for which, out in enumerate((keep, send)):
        for place in range(places):
            at = (which * places + place) * size
            out[place] = got[at : at + size, :]


def vector_rows(table_ref, shard, size):
    width = table_ref.shape[1]
    row = lax.broadcasted_iota(jnp.int32, (width, 128), 0)
    column = lax.broadcasted_iota(jnp.int32, (width, 128), 1)
    chosen = ((row == shard * size + column) & (column < size)).astype(BF)
    short = dot(table_ref[:8, :].astype(BF), chosen)
    long_size = 4 * size
    per_row = width // long_size
    start = pl.multiple_of(shard % per_row * long_size, 128)
    long = table_ref[pl.ds(8 + shard // per_row, 1), pl.ds(start, long_size)]
    zeros = lambda rows, columns: jnp.zeros((rows, columns), F32)
    return jnp.concatenate(
        [
            jnp.concatenate([short, zeros(8, width - 128)], axis=1),
            jnp.concatenate([long, zeros(1, width - long_size)], axis=1),
            zeros(7, width),
        ],
        axis=0,
    ).astype(BF)


def inner_grad_kernel(order, n_after, left, right, *refs):
    keep, send, left_ref = refs[n_after:]

    @pl.when(pl.program_id(0) == 0)
    def _():
        arrange(left_ref, left, order)

    place_rows(dot(left_ref[...], right[...]).astype(BF), keep, send)


def inner_grad(left, right, shards, after=()):
    height, depth = left.shape
    wide = right.shape[1]
    chunk = height
    shape = (4, height // shards, wide)
    return pl.pallas_call(
        functools.partial(inner_grad_kernel, ORDER_ONE, len(after)),
        grid=(wide // chunk,),
        in_specs=[whole((height, depth)), pl.BlockSpec((depth, chunk), lambda g: (0, g))] + anywhere(len(after)),
        out_specs=[pl.BlockSpec((*shape[:2], chunk), lambda g: (0, 0, g))] * 2,
        out_shape=[jax.ShapeDtypeStruct(shape, BF)] * 2,
        scratch_shapes=[pltpu.VMEM((height, depth), BF)],
        compiler_params=params(),
        cost_estimate=cost(3.5 * height * depth * wide, 4 * height * wide),
        name="inner_grad",
    )(left, right, *after)


def outer_grad_kernel(_, left, right, keep, send, acc_ref):
    acc_ref[...] = dot(left[...], right[...])
    rows = keep.shape[1]
    wide = acc_ref.shape[1] // 2
    core = lax.axis_index("fsdp") & CORE
    for which, out in enumerate((keep, send)):
        start = pl.multiple_of((core ^ which) * wide, 128)
        for block in range(acc_ref.shape[0] // rows):
            part_rows = acc_ref[block * rows : (block + 1) * rows, pl.ds(start, wide)]
            out[0, :, block * wide : (block + 1) * wide] = part_rows.astype(BF)


def outer_grad(left, right, shards):
    height, depth = left.shape
    wide = right.shape[1]
    chips = lax.axis_index("fsdp") // 2
    places = jnp.stack([chips ^ (rel // 2) for rel in ORDER_TWO]).astype(jnp.int32)
    chunk = 2 * wide // shards
    shape = (4, height // shards, wide)
    return pl.pallas_call(
        outer_grad_kernel,
        grid_spec=pltpu.PrefetchScalarGridSpec(
            num_scalar_prefetch=1,
            grid=(4,),
            in_specs=[
                pl.BlockSpec((height, depth), lambda g, p: (0, 0), pipeline_mode=pl.Buffered(1)),
                pl.BlockSpec((depth, chunk), lambda g, p: (0, p[g])),
            ],
            out_specs=[pl.BlockSpec((1, *shape[1:]), lambda g, p: (g, 0, 0))] * 2,
            scratch_shapes=[pltpu.VMEM((height, chunk), F32)],
        ),
        out_shape=[jax.ShapeDtypeStruct(shape, BF)] * 2,
        compiler_params=params(),
        cost_estimate=cost(3.5 * height * depth * wide, 4 * height * wide),
        name="outer_grad",
    )(places, left, right)


def square_grad_kernel(n_after, tokens, mixed, dqkv, d_branch, table, *refs):
    keep_one, send_one, keep_two, send_two, left_ref = refs[n_after:]
    step = pl.program_id(0)
    size = keep_two.shape[1]
    for at, left, order in ((0, tokens, ORDER_ONE), (2, tokens, ORDER_TWO), (3, mixed, ORDER_TWO)):

        @pl.when(step == at)
        def _():
            arrange(left_ref, left, order)

    @pl.when(step < 2)
    def _():
        got = dot(left_ref[...], dqkv[...]).astype(BF)
        for which, out in enumerate((keep_one, send_one)):
            for place, rel in enumerate(ORDER_ONE):
                at = (which * len(ORDER_ONE) + place) * size
                out[place, :size, :] = got[at : at + size, :]

                @pl.when(step == 0)
                def _():
                    shard = lax.axis_index("fsdp") ^ (rel | which * CORE)
                    out[place, size:, :] = vector_rows(table, shard, size)

                @pl.when(step == 1)
                def _():
                    out[place, size:, :] = jnp.zeros((16, out.shape[2]), BF)

    @pl.when(step == 2)
    def _():
        place_rows(dot(left_ref[...], dqkv[...]).astype(BF), keep_two, send_two)

    @pl.when(step == 3)
    def _():
        place_rows(dot(left_ref[...], d_branch[...]).astype(BF), keep_two, send_two)


def square_grad(tokens_t, mixed_t, dqkv, d_branch, table, shards, after=()):
    height, depth = tokens_t.shape
    shape = (4, height // shards, 2 * height)
    block = (*shape[:2], height)
    tall = (shape[0], shape[1] + 16, shape[2])
    one = pl.BlockSpec((*tall[:2], height), lambda g: (0, 0, jnp.minimum(g, 1)))
    two = pl.BlockSpec(block, lambda g: (0, 0, jnp.maximum(g - 2, 0)))
    return pl.pallas_call(
        functools.partial(square_grad_kernel, len(after)),
        grid=(4,),
        in_specs=[
            whole((height, depth)),
            whole((height, depth)),
            pl.BlockSpec((depth, height), lambda g: (0, jnp.minimum(g, 2))),
            whole((depth, height)),
            whole(table.shape),
        ]
        + anywhere(len(after)),
        out_specs=[one, one, two, two],
        out_shape=[jax.ShapeDtypeStruct(tall, BF)] * 2 + [jax.ShapeDtypeStruct(shape, BF)] * 2,
        scratch_shapes=[pltpu.VMEM((height, depth), BF)],
        compiler_params=params(),
        cost_estimate=cost(1.1e10, 1.5e7),
        name="square_grad",
    )(tokens_t, mixed_t, dqkv, d_branch, table, *after)


def up(x):
    return x.astype(F32)


def fetch(terms, held_ref, sems):
    copies = [
        pltpu.make_async_copy(ref.at[0], held_ref.at[i, pl.ds(0, ref.shape[1])], sems.at[i])
        for i, ref in enumerate(terms)
    ]
    for copy in copies:
        copy.start()
    for copy in copies:
        copy.wait()


def add_places(terms, places):
    total = up(terms[0][places])
    for term in terms[1:]:
        total = total + up(term[places])
    return total.astype(BF)


def total_kernel(n_after, *refs):
    keep, send, held_ref, sems = refs[8 + n_after :]
    size = keep.shape[2]
    me = lax.axis_index("rep")
    fetch(refs[:8], held_ref, sems)
    for quarter in range(4):
        i, columns = quarter // 2, slice(quarter % 2 * size, (quarter % 2 + 1) * size)
        rows = refs[4 * i].shape[1]
        total = up(held_ref[4 * i, :rows, columns])
        for place in range(4 * i + 1, 4 * i + 4):
            total = total + up(held_ref[place, :rows, columns])
        rel = me ^ quarter
        for bit, out in enumerate((keep, send)):

            @pl.when(rel & 1 == bit)
            def _():
                out[rel // 2, :rows] = total.astype(BF)
                if rows < out.shape[1]:
                    out[rel // 2, rows:] = jnp.zeros((out.shape[1] - rows, size), BF)


def total_places(one, two, after):
    _, rows, wide = one[0].shape
    shape = (2, rows, wide // 2)
    return pl.pallas_call(
        functools.partial(total_kernel, len(after)),
        in_specs=anywhere(8 + len(after)),
        out_shape=[jax.ShapeDtypeStruct(shape, BF)] * 2,
        scratch_shapes=[
            pltpu.VMEM((8, rows, wide), BF),
            pltpu.SemaphoreType.DMA((8,)),
        ],
        compiler_params=pltpu.CompilerParams(vmem_limit_bytes=VMEM_BYTES),
        cost_estimate=cost(3e10, 1e7),
        name="total",
    )(*one, *two, *after)


class Sum:
    def __init__(self, *groups):
        self.terms = [[keep, flip(send, "fsdp", CORE)] for keep, send in groups]
        self.bits = (X, Y), (Y, X)

    def far(self, group, *after):
        terms = pinned(self.terms[group], *after)
        out = add_places(terms, slice(2, 4))
        self.terms[group] = [*terms, flip(out, "fsdp", self.bits[group][0])]
        return out

    def near(self, group, *after):
        terms = pinned(self.terms[group], *after)
        out = add_places(terms, slice(1, 2))
        self.terms[group] = [*terms, flip(out, "fsdp", self.bits[group][1])]
        return out

    def total(self, *after):
        self.part, self.send = total_places(*self.terms, after)
        return self.part

    def rep_first(self, *after):
        self.rep = flip(pinned(self.send, *after), "rep", 1)

    def rep_near(self, *after):
        part_far, rep_far = pinned((self.part, self.rep), *after)
        out = (up(part_far[1]) + up(rep_far[1])).astype(BF)
        self.rep_far = flip(out, "rep", 2)
        return out

    def own(self, *after):
        terms = pinned((self.part[0], self.rep[0], self.rep_far), *after)
        self.mine = add_places([t[None] for t in terms], 0)
        self.two = flip(self.mine, "rep", 2)
        return self.mine

    def own_near(self, *after):
        self.one = flip(pinned(self.mine, *after), "rep", 1)

    def parts(self, *after):
        three = flip(pinned(self.two, self.one, *after), "rep", 1)
        return [self.mine, self.one, self.two, three]


def finish_kernel(factor, feed_weights, *refs):
    parts, outs, held_ref = refs[:4], refs[4:-1], refs[-1]
    me = lax.axis_index("rep")
    for rel, ref in enumerate(parts):
        held_ref[me ^ rel] = up(ref[...]) * factor
    if not feed_weights:
        size = outs[0].shape[0]
        for i in range(4):
            outs[i][...] = held_ref[i, :size]
        for i, out in enumerate(outs[4:]):
            out[...] = held_ref[0, size + i, : out.shape[0]]
        return
    inner_ref, outer_ref = outs
    size = held_ref.shape[2]
    for i in range(2):
        inner_ref[:, i * size : (i + 1) * size] = held_ref[i]
    rows, width = outer_ref.shape
    blocks = []
    for i in range(2):
        blocks += [held_ref[2 + i, :, at : at + rows] for at in range(0, size, rows)]
    outer_ref[...] = jnp.concatenate(blocks, axis=0).T


def finish(parts, factor, shapes, feed_weights):
    rows, size = parts[0].shape
    return pl.pallas_call(
        functools.partial(finish_kernel, factor, feed_weights),
        out_shape=[jax.ShapeDtypeStruct(shape, F32) for shape in shapes],
        scratch_shapes=[pltpu.VMEM((4, rows, size), F32)],
        compiler_params=pltpu.CompilerParams(vmem_limit_bytes=VMEM_BYTES),
        cost_estimate=cost(2e9, 1e7),
        name="finish",
    )(*parts)


def all_sum(values, axes=("fsdp", "rep")):
    for axis in axes:
        n = lax.axis_size(axis)
        if n & (n - 1):
            values = lax.psum(values, axis)
            continue
        bit = 1
        while bit < n:
            values = values + flip(values, axis, bit)
            bit *= 2
    return values


def body(
    tokens,
    doc_lengths,
    query_weight,
    key_weight,
    value_weight,
    output_weight,
    inner_weight,
    outer_weight,
    query_bias,
    value_bias,
    output_bias,
    inner_bias,
    outer_bias,
    first_gain,
    first_shift,
    second_gain,
    second_shift,
    cotangent,
):
    rows, slots, width = tokens.shape
    count = rows * slots
    docs = doc_lengths.shape[1]
    n_fsdp = lax.axis_size("fsdp")
    n_rep = lax.axis_size("rep")
    shard = query_weight.shape[0]
    outer_shard = outer_weight.shape[0]
    inner_width = inner_weight.shape[1]
    direct = n_fsdp == 8 and n_rep == 4 and shard % 16 == 0

    vectors = (
        query_bias,
        value_bias,
        output_bias,
        outer_bias,
        first_gain,
        first_shift,
        second_gain,
        second_shift,
        inner_bias,
    )
    if direct:
        half, outer_half = shard // 2, outer_shard // 2
        blocks = pack(query_weight, key_weight, value_weight, inner_weight, output_weight, outer_weight, vectors)
        one, two = Gather(blocks[0], X, Y), Gather(blocks[1], Y, X)
        blocks = pinned(blocks[2:], one.near, two.near)
        three, four = Gather(blocks[0], X, Y), Gather(blocks[1], Y, X)
        pairs = stacked(one.block, one.near, two.block, two.near)
        one.go(pairs[0])
        two.go(pairs[1])
        pairs = stacked(three.block, three.near, four.block, four.near, pairs)
        three.go(pairs[0])
        four.go(pairs[1])
        chips_x, chips_y = stacked(one.pair, one.far, two.pair, two.far, pairs)
        held_x, held_y = one.held_whole(chips_x), two.held_whole(chips_y)
        qw = part(held_x, 0, shard, shard)
        kw = part(held_x, shard, half, shard) + part(held_y, shard, half, shard, half)
        vw = part(held_y, 0, shard, shard)
        vec, bias_inner = unpack(part(held_x, shard + half, 16, 16), shard, outer_shard)
    else:
        qw, kw, vw, ow, iw, w2 = [
            [(lax.all_gather(w, "fsdp", axis=0, tiled=True), 0, w.shape[0] * n_fsdp, None, 0, 0, 0)]
            for w in (query_weight, key_weight, value_weight, output_weight, inner_weight, outer_weight)
        ]
        small = lax.all_gather(jnp.concatenate(vectors)[None], "fsdp", axis=0, tiled=True).astype(F32)
        vec = small[:, : 8 * shard].reshape(n_fsdp, 8, shard).transpose(1, 0, 2).reshape(8, width)
        bias_inner = small[:, 8 * shard :].reshape(1, inner_width)
        pairs = ()

    places = jnp.arange(docs, dtype=jnp.int32)
    ends = jnp.sum(
        jnp.where(places[None, :, None] >= places[None, None, :], doc_lengths[:, None, :], 0), axis=-1
    )
    slot = jnp.arange(slots, dtype=jnp.int32)
    segment = jnp.sum((slot[None, None, :] >= ends[:, :, None]).astype(jnp.int32), axis=1)
    seg = jnp.broadcast_to(segment[:, None, :].astype(F32), (rows, 8, slots)).reshape(rows * 8, slots)

    flat = tokens.reshape(count, width)
    query, keys, values, mixed_t, tokens_t, lse = attend(flat, seg, vec, (qw, kw, vw), pairs)
    if direct:
        three.far, four.far = pinned((three.far, four.far), lse)
        held_x, held_y = three.held(), four.held()
        iw = part(held_x, 0, half, shard) + part(held_y, 0, half, shard, half)
        ow = [(*piece[:-1], inner_width) for piece in iw]
        w2 = [
            (*piece[:4], outer_shard, which * outer_half + block * half, inner_width + (1 + block) * width)
            for which, held in enumerate((held_x, held_y))
            for block in range(outer_half // half)
            for piece in part(held, 0, half, shard)
        ]
    encoded, hidden_t, activated, d_outer_t, d_inner, d_first, d_branch, d_mixed, table = feed(
        mixed_t, flat, cotangent.reshape(count, width), seg, vec, bias_inner, (ow, iw, w2), docs
    )
    factor = 1.0 / math.sqrt(rows * n_rep * n_fsdp * slots)
    if direct:
        keep_outer, send_outer = outer_grad(d_outer_t, activated, n_fsdp)
        keep_inner, send_inner = inner_grad(hidden_t, d_inner, n_fsdp, (send_outer,))
        wide = Sum((keep_inner, send_inner), (keep_outer, send_outer))
        far = wide.far(1, send_inner)
        far = wide.far(0, far)
        dqkv, table = attend_back(query, keys, values, d_mixed, lse, seg, table, (far,))
        near = wide.near(1, dqkv)
        near = wide.near(0, near)
        keep_one, send_one, keep_two, send_two = square_grad(
            tokens_t, mixed_t, dqkv, d_branch, table, n_fsdp, (near,)
        )
        square = Sum((keep_one, send_one), (keep_two, send_two))
        total = wide.total(send_one)
        far = square.far(0, total)
        far = square.far(1, far)
        wide.rep_first(far)
        near = square.near(0, wide.rep_near())
        near = square.near(1, near)
        part_sum = square.total(near)
        square.rep_first()
        mine = wide.own(part_sum)
        sent = square.rep_near(mine)
        wide.own_near(sent)
        tokens_grad = tokens_back(d_first, dqkv, (qw, kw, vw), (sent,))
        wide_parts = wide.parts(tokens_grad)
        square.own(tokens_grad)
        square.own_near()
        inner_all, outer_all = finish(wide_parts, factor, (inner_weight.shape, outer_weight.shape), True)
        shapes = (query_weight.shape,) * 4 + ((shard,),) * 8 + ((outer_shard,),)
        q_all, k_all, v_all, o_all, *short, long = finish(square.parts(), factor, shapes, False)
    else:
        dqkv, table = attend_back(query, keys, values, d_mixed, lse, seg, table)
        tokens_grad = tokens_back(d_first, dqkv, (qw, kw, vw))

        def shared(left_t, right):
            total = lax.psum_scatter(dot(left_t, right), "fsdp", scatter_dimension=0, tiled=True)
            return up(lax.psum(total.astype(BF), "rep")) * factor

        outer_all = shared(activated.T, d_outer_t.T)
        inner_all = shared(hidden_t, d_inner)
        o_all = shared(mixed_t, d_branch)
        q_all, k_all, v_all = [shared(tokens_t, item) for item in jnp.split(dqkv, 3, axis=1)]
        vectors = all_sum(table[: 8 + inner_width // width]) * factor
        me = lax.axis_index("fsdp")
        short = lax.dynamic_slice_in_dim(vectors[:8], me * shard, shard, axis=1)
        long = lax.dynamic_slice_in_dim(vectors[8:].reshape(inner_width), me * outer_shard, outer_shard, axis=0)
    return (
        encoded.reshape(rows, slots, width),
        tokens_grad.reshape(rows, slots, width),
        q_all,
        k_all,
        v_all,
        o_all,
        inner_all,
        outer_all,
        short[0],
        short[1],
        short[2],
        long,
        short[3],
        short[4],
        short[5],
        short[6],
        short[7],
    )


def solution(mesh):
    data = P(("rep", "fsdp"), None, None)
    matrix, vector = P("fsdp", None), P("fsdp")
    return jax.shard_map(
        body,
        mesh=mesh,
        in_specs=(data, P(("rep", "fsdp"), None)) + (matrix,) * 6 + (vector,) * 9 + (data,),
        out_specs=(data, data) + (matrix,) * 6 + (vector,) * 9,
        check_vma=False,
    )
```

```python
import functools
import math

import jax
import jax.numpy as jnp
from jax import lax
from jax.experimental import pallas as pl
from jax.experimental.pallas import tpu as pltpu
from jax.sharding import PartitionSpec as P

HD = 64
EPSILON = 1e-05
BF = jnp.bfloat16
F32 = jnp.float32
NT = ((1,), (1,))
VMEM_BYTES = 60 * 2**20
CORE, X, Y = 1, 2, 4
ROW_TILE = 256
FF_CHUNK = 1536


def dot(a, b, dims=((1,), (0,))):
    return lax.dot_general(a, b, (dims, ((), ())), preferred_element_type=F32)


def params():
    return pltpu.CompilerParams(
        vmem_limit_bytes=VMEM_BYTES, dimension_semantics=("arbitrary",)
    )


def cost(flops, nbytes, trans=0):
    return pl.CostEstimate(
        flops=int(flops), bytes_accessed=int(nbytes), transcendentals=int(trans)
    )


def whole(shape):
    return pl.BlockSpec(
        shape, lambda *i: (0,) * len(shape), pipeline_mode=pl.Buffered(1)
    )


def anywhere(count):
    return [pl.BlockSpec(memory_space=pl.ANY)] * count


def flip(array, axis, bit):
    size = lax.axis_size(axis)
    return lax.ppermute(array, axis, [(i, i ^ bit) for i in range(size)])


def pinned(values, *others):
    return lax.optimization_barrier((values, others))[0]


def piece_copies(pieces, refs, target, sems, first):
    copies = []
    for slot, (which, start, rows, rel, shard, offset, column) in enumerate(pieces):
        place = 0
        if rel is not None:
            place = pl.multiple_of((lax.axis_index("fsdp") ^ rel) * shard + offset, math.gcd(shard, offset))
        copies.append(
            pltpu.make_async_copy(
                refs[which].at[pl.ds(start, rows), pl.ds(column, target.shape[1])],
                target.at[pl.ds(place, rows), :],
                sems.at[first + slot],
            )
        )
    return copies


def group_copies(numbered, refs, targets, sems):
    copies = []
    for pieces, target in zip(numbered, targets):
        copies.append(piece_copies(pieces, refs, target, sems, sum(len(c) for c in copies)))
    return copies


def index_pieces(weights):
    arrays, numbered = [], []
    for pieces in weights:
        mine = []
        for array, *rest in pieces:
            for n, seen in enumerate(arrays):
                if seen is array:
                    break
            else:
                n = len(arrays)
                arrays.append(array)
            mine.append((n, *rest))
        numbered.append(mine)
    return arrays, numbered


class Gather:
    def __init__(self, block, first, second):
        self.block, self.bits = block, (first, second)
        self.near = flip(block, "fsdp", first)

    def go(self, pair):
        self.pair = pair
        self.far = flip(pair, "fsdp", self.bits[1])
        return pair

    def parts(self):
        first, second = self.bits
        rows = self.block.shape[0]
        return [(self.pair, 0, 0), (self.pair, rows, first), (self.far, 0, second), (self.far, rows, first | second)]

    def held(self):
        other = {id(a): flip(a, "fsdp", CORE) for a in (self.pair, self.far)}
        return self.parts() + [(other[id(a)], at, rel | CORE) for a, at, rel in self.parts()]

    def held_whole(self, chips):
        first, second = self.bits
        rels = (0, first, second, first | second)
        return [
            (array, place * self.block.shape[0], rel | core)
            for core, array in ((0, chips), (CORE, flip(chips, "fsdp", CORE)))
            for place, rel in enumerate(rels)
        ]


def stack_kernel(n_after, one, two, three, four, *refs):
    for out, parts in zip(refs[n_after:], ((one, two), (three, four))):
        at = 0
        for ref in parts:
            rows = ref.shape[0]
            out[at : at + rows, :] = ref[...]
            at += rows


def stacked(one, two, three, four, after=()):
    full = lambda a: pl.BlockSpec(a.shape, lambda g: (0, 0))
    outs = [
        jax.ShapeDtypeStruct((a.shape[0] + b.shape[0], a.shape[1]), BF) for a, b in ((one, two), (three, four))
    ]
    return pl.pallas_call(
        functools.partial(stack_kernel, len(after)),
        grid=(1,),
        in_specs=[full(a) for a in (one, two, three, four)] + anywhere(len(after)),
        out_specs=[full(a) for a in outs],
        out_shape=outs,
        compiler_params=params(),
        cost_estimate=cost(2e9, 3e6),
        name="stacked",
    )(one, two, three, four, *after)


def pack_kernel(half, query_ref, key_ref, value_ref, wi_ref, wo_ref, w2_ref, *refs):
    vectors, (one_ref, two_ref, three_ref, four_ref) = refs[:-4], refs[-4:]
    shard, width = query_ref.shape
    one_ref[:shard, :] = query_ref[...]
    one_ref[shard : shard + half, :] = key_ref[:half, :]
    two_ref[:shard, :] = value_ref[...]
    two_ref[shard:, :] = key_ref[half:, :]
    rows = []
    for ref in vectors:
        size = ref.shape[0]
        rows.append(
            jnp.concatenate([ref[...].astype(F32).reshape(1, size), jnp.zeros((1, width - size), F32)], axis=1)
        )
    rows.append(jnp.zeros((16 - len(rows), width), F32))
    one_ref[shard + half :, :] = jnp.concatenate(rows, axis=0).astype(BF)
    wide = wi_ref.shape[1]
    blocks = w2_ref.shape[0] // (2 * half)
    for place, ref in enumerate((three_ref, four_ref)):
        ref[:, :wide] = wi_ref[place * half : (place + 1) * half, :]
        ref[:, wide : wide + width] = wo_ref[place * half : (place + 1) * half, :]
        for block in range(blocks):
            row, column = (place * blocks + block) * half, wide + (1 + block) * width
            ref[:, column : column + width] = w2_ref[row : row + half, :]


def pack(query, key, value, inner, output, outer, vectors):
    shard, width = query.shape
    half = shard // 2
    wide = inner.shape[1] + width * (1 + outer.shape[0] // (2 * half))
    return pl.pallas_call(
        functools.partial(pack_kernel, half),
        out_shape=[
            jax.ShapeDtypeStruct((shard + half + 16, width), BF),
            jax.ShapeDtypeStruct((shard + half, width), BF),
            jax.ShapeDtypeStruct((half, wide), BF),
            jax.ShapeDtypeStruct((half, wide), BF),
        ],
        compiler_params=pltpu.CompilerParams(vmem_limit_bytes=VMEM_BYTES),
        name="pack",
    )(query, key, value, inner, output, outer, *vectors)


def unpack_kernel(numbered, n_arrays, shard, long, *refs):
    pieces = refs[:n_arrays]
    vec_ref, inner_ref, held_ref, sems = refs[n_arrays:]
    copies = piece_copies(numbered[0], pieces, held_ref, sems, 0)
    for copy in copies:
        copy.start()
    for copy in copies:
        copy.wait()
    n = len(copies)
    parts = [held_ref[16 * i : 16 * i + 16, :] for i in range(n)]
    slot = lax.broadcasted_iota(jnp.int32, (n * 128, n * shard), 0)
    place = lax.broadcasted_iota(jnp.int32, (n * 128, n * shard), 1)
    at = slot % 128
    spread = ((at < shard) & (place == slot // 128 * shard + at)).astype(BF)
    vec_ref[...] = dot(jnp.concatenate([p[:, :128] for p in parts], axis=1), spread)[:8]
    for i, p in enumerate(parts):
        inner_ref[:, i * long : (i + 1) * long] = p[8:9, :long].astype(F32)


def unpack(pieces, shard, long):
    arrays, numbered = index_pieces([pieces])
    n, width = len(pieces), pieces[0][0].shape[1]
    return pl.pallas_call(
        functools.partial(unpack_kernel, numbered, len(arrays), shard, long),
        in_specs=anywhere(len(arrays)),
        out_shape=[
            jax.ShapeDtypeStruct((8, n * shard), F32),
            jax.ShapeDtypeStruct((1, n * long), F32),
        ],
        scratch_shapes=[pltpu.VMEM((16 * n, width), BF), pltpu.SemaphoreType.DMA((n,))],
        name="unpack",
    )(*arrays)


def part(held, start, rows, shard, offset=0):
    return [(a, at + start, rows, rel, shard, offset, 0) for a, at, rel in held]


def column_of(row):
    return jnp.broadcast_to(row, (128, row.shape[1])).T[:, :1]


def split_lanes(pair):
    low = lax.broadcasted_iota(jnp.int32, (1, 2 * HD), 1) < HD
    return jnp.concatenate([jnp.where(low, pair, BF(0)), jnp.where(low, BF(0), pair)], axis=0)


def split_rows(pair_t):
    low = lax.broadcasted_iota(jnp.int32, (2 * HD, 1), 0) < HD
    return jnp.concatenate([jnp.where(low, pair_t, BF(0)), jnp.where(low, BF(0), pair_t)], axis=1)


def attend_kernel(numbered, n_arrays, n_after, heads, tok_ref, seg_ref, vec_ref, *refs):
    pieces = refs[:n_arrays]
    q_ref, k_ref, v_ref, mt_ref, tt_ref, lse_ref, w_ref, bias_ref, qs_ref, sems = refs[n_arrays + n_after :]
    ready = load_weights(numbered, pieces, [w_ref.at[which] for which in range(3)], sems)
    x = tok_ref[...]
    tt_ref[...] = x.T
    seg = seg_ref[0:1, :]
    bias_ref[...] = jnp.where(column_of(seg) == seg, 0.0, -1e30)

    for which in range(3):
        ready(which)
    q = (dot(x, w_ref[0]) + vec_ref[0:1, :]).astype(BF)
    q_ref[...] = q
    qs_ref[...] = q * BF(1.0 / math.sqrt(HD))
    k_ref[...] = dot(x, w_ref[1]).astype(BF)
    v_ref[...] = (dot(x, w_ref[2]) + vec_ref[1:2, :]).astype(BF)
    for pair in range(heads // 2):
        sl = slice(pair * 2 * HD, (pair + 1) * 2 * HD)
        scores = dot(split_lanes(k_ref[:, sl]), qs_ref[:, sl], NT)
        slots = scores.shape[0] // 2
        weights, inverse = [], []
        for half in range(2):
            mine = scores[half * slots : (half + 1) * slots] + bias_ref[...]
            top = jnp.max(mine, axis=0, keepdims=True)
            exps = jnp.exp(mine - top)
            total = jnp.sum(exps, axis=0, keepdims=True)
            head = 2 * pair + half
            lse_ref[head : head + 1, :] = top + jnp.log(total)
            weights.append(exps.astype(BF))
            inverse.append(1.0 / total)
        out = dot(split_rows(v_ref[:, sl].T), jnp.concatenate(weights, axis=0))
        low_rows = lax.broadcasted_iota(jnp.int32, (2 * HD, 1), 0) < HD
        mt_ref[sl, :] = (out * jnp.where(low_rows, inverse[0], inverse[1])).astype(BF)


def attend(tokens, seg, vec, weights, after=()):
    count, width = tokens.shape
    rows = seg.shape[0] // 8
    slots = count // rows
    heads = width // HD
    padded = -(-heads // 8) * 8
    arrays, numbered = index_pieces(weights)
    row = pl.BlockSpec((slots, width), lambda i: (i, 0))
    col = pl.BlockSpec((width, slots), lambda i: (0, i))
    return pl.pallas_call(
        functools.partial(attend_kernel, numbered, len(arrays), len(after), heads),
        grid=(rows,),
        in_specs=[row, pl.BlockSpec((8, slots), lambda i: (i, 0)), whole(vec.shape)]
        + anywhere(len(arrays) + len(after)),
        out_specs=[row, row, row, col, col, pl.BlockSpec((padded, slots), lambda i: (i, 0))],
        out_shape=[jax.ShapeDtypeStruct((count, width), BF)] * 3
        + [jax.ShapeDtypeStruct((width, count), BF)] * 2
        + [jax.ShapeDtypeStruct((rows * padded, slots), F32)],
        scratch_shapes=[
            pltpu.VMEM((3, width, width), BF),
            pltpu.VMEM((slots, slots), F32),
            pltpu.VMEM((slots, width), BF),
            pltpu.SemaphoreType.DMA((sum(len(p) for p in numbered),)),
        ],
        compiler_params=params(),
        cost_estimate=cost(1e9, 1e6),
        name="attend",
    )(tokens, seg, vec, *arrays, *after)


def gelu_pair(v):
    area = 0.5 + 0.5 * lax.erf(v * math.sqrt(0.5))
    density = jnp.exp2(v * v * (-0.5 / math.log(2.0))) * (1.0 / math.sqrt(2.0 * math.pi))
    return v * area, area + v * density


def norm(z):
    center = z - jnp.mean(z, axis=-1, keepdims=True)
    scale = lax.rsqrt(jnp.mean(center * center, axis=-1, keepdims=True) + EPSILON)
    return center * scale, scale


def norm_back(grad, n, scale, gain):
    dn = grad * gain
    return (
        dn - jnp.mean(dn, axis=-1, keepdims=True) - n * jnp.mean(dn * n, axis=-1, keepdims=True)
    ) * scale


def column_sum(x):
    return jnp.sum(x.reshape(x.shape[0] // 8, 8, x.shape[1]), axis=0)


def load_weights(numbered, pieces, targets, sems):
    groups = group_copies(numbered, pieces, targets, sems)
    first_step = pl.program_id(0) == 0

    @pl.when(first_step)
    def _():
        for copies in groups:
            for copy in copies:
                copy.start()

    def ready(which):
        @pl.when(first_step)
        def _():
            for copy in groups[which]:
                copy.wait()

    return ready


def vector(vec_ref, i):
    return vec_ref[i : i + 1, :]


def feed_kernel(numbered, n_arrays, docs, mt_ref, tok_ref, cot_ref, seg_ref, vec_ref, bi_ref, *refs):
    pieces = refs[:n_arrays]
    outs = refs[n_arrays:]
    enc_ref, ht_ref, act_ref, dot_ref, din_ref, dfirst_ref, dbr_ref, dm_ref, total_ref = outs[:9]
    wo_ref, wi_ref, w2_ref, slope_ref, sums_ref, sumi_ref, sems = outs[9:]
    ready = load_weights(numbered, pieces, (wo_ref, wi_ref, w2_ref), sems)

    @pl.when(pl.program_id(0) == 0)
    def _():
        sums_ref[...] = jnp.zeros_like(sums_ref)
        sumi_ref[...] = jnp.zeros_like(sumi_ref)

    width, inner_width = wi_ref.shape
    ready(0)
    z1 = tok_ref[...].astype(F32) + dot(mt_ref[...].T, wo_ref[...]) + vector(vec_ref, 2)
    n1, r1 = norm(z1)
    hidden = n1 * vector(vec_ref, 4) + vector(vec_ref, 5)
    hidden_low = hidden.astype(BF)
    ht_ref[...] = hidden_low.T
    ready(1)
    z2 = hidden + vector(vec_ref, 3)
    for c in range(0, inner_width, FF_CHUNK):
        sl = slice(c, c + FF_CHUNK)
        act, slope = gelu_pair(dot(hidden_low, wi_ref[:, sl]) + bi_ref[:, sl])
        act = act.astype(BF)
        act_ref[:, sl] = act
        slope_ref[:, sl] = slope
        if c == 0:
            ready(2)
        z2 = z2 + dot(act, w2_ref[sl, :])
    n2, r2 = norm(z2)
    gain = vector(vec_ref, 6)
    enc_ref[...] = (n2 * gain + vector(vec_ref, 7)).astype(BF)
    grad = cot_ref[...] * column_of((seg_ref[0:1, :] < docs).astype(F32))
    d_second = norm_back(grad, n2, r2, gain)
    d_outer = d_second.astype(BF)
    dot_ref[...] = d_outer.T
    d_hidden = d_second
    for c in range(0, inner_width, FF_CHUNK):
        sl = slice(c, c + FF_CHUNK)
        d_inner = (dot(d_outer, w2_ref[sl, :], NT) * slope_ref[:, sl]).astype(BF)
        din_ref[:, sl] = d_inner
        sumi_ref[:, sl] += column_sum(d_inner.astype(F32))
        d_hidden = d_hidden + dot(d_inner, wi_ref[:, sl], NT)
    d_first = norm_back(d_hidden, n1, r1, vector(vec_ref, 4))
    dfirst_ref[...] = d_first
    d_branch = d_first.astype(BF)
    dbr_ref[...] = d_branch
    dm_ref[...] = dot(d_branch, wo_ref[...], NT).astype(BF)
    for i, item in enumerate(
        (d_branch.astype(F32), d_outer.astype(F32), d_hidden * n1, d_hidden, grad * n2, grad)
    ):
        sums_ref[i] += column_sum(item)

    @pl.when(pl.program_id(0) == pl.num_programs(0) - 1)
    def _():
        total_ref[...] = jnp.zeros_like(total_ref)
        for i in range(6):
            total_ref[2 + i : 3 + i, :] = jnp.sum(sums_ref[i], axis=0, keepdims=True)
        for i in range(inner_width // width):
            part_sum = jnp.sum(sumi_ref[:, i * width : (i + 1) * width], axis=0, keepdims=True)
            total_ref[8 + i : 9 + i, :] = part_sum


def feed(mixed_t, tokens, cotangent, seg, vec, bias_inner, weights, docs):
    count, width = tokens.shape
    inner_width = bias_inner.shape[1]
    arrays, numbered = index_pieces(weights)
    tile = ROW_TILE
    row = pl.BlockSpec((tile, width), lambda i: (i, 0))
    col = pl.BlockSpec((width, tile), lambda i: (0, i))
    wide = pl.BlockSpec((tile, inner_width), lambda i: (i, 0))
    per_row = seg.shape[1] // tile
    sum_rows = -(-(8 + inner_width // width) // 8) * 8
    out = jax.ShapeDtypeStruct
    return pl.pallas_call(
        functools.partial(feed_kernel, numbered, len(arrays), docs),
        grid=(count // tile,),
        in_specs=[
            col,
            row,
            row,
            pl.BlockSpec((8, tile), lambda i: (i // per_row, i % per_row)),
            whole(vec.shape),
            whole(bias_inner.shape),
        ]
        + anywhere(len(arrays)),
        out_specs=[row, col, wide, col, wide, row, row, row, pl.BlockSpec((sum_rows, width), lambda i: (0, 0))],
        out_shape=[
            out((count, width), BF),
            out((width, count), BF),
            out((count, inner_width), BF),
            out((width, count), BF),
            out((count, inner_width), BF),
            out((count, width), F32),
            out((count, width), BF),
            out((count, width), BF),
            out((sum_rows, width), F32),
        ],
        scratch_shapes=[
            pltpu.VMEM((width, width), BF),
            pltpu.VMEM((width, inner_width), BF),
            pltpu.VMEM((inner_width, width), BF),
            pltpu.VMEM((tile, inner_width), F32),
            pltpu.VMEM((6, 8, width), F32),
            pltpu.VMEM((8, inner_width), F32),
            pltpu.SemaphoreType.DMA((sum(len(p) for p in numbered),)),
        ],
        compiler_params=params(),
        cost_estimate=cost(4e10, 5e7),
        name="feed",
    )(mixed_t, tokens, cotangent, seg, vec, bias_inner, *arrays)


def attend_back_kernel(n_after, q_ref, k_ref, v_ref, dm_ref, lse_ref, seg_ref, table_ref, *refs):
    dqkv_ref, total_ref, bias_ref, sums_ref = refs[n_after:]

    @pl.when(pl.program_id(0) == 0)
    def _():
        sums_ref[...] = jnp.zeros_like(sums_ref)

    width = q_ref.shape[1]
    scale = 1.0 / math.sqrt(HD)
    seg = seg_ref[0:1, :]
    bias_ref[...] = jnp.where(column_of(seg) == seg, 0.0, -1e30)
    low = lax.broadcasted_iota(jnp.int32, (1, 2 * HD), 1) < HD
    slots = q_ref.shape[0]
    halves = lambda a: (a[:slots], a[slots:])
    for pair in range(width // (2 * HD)):
        first = pair * 2 * HD
        sl = slice(first, first + 2 * HD)
        queries = q_ref[:, sl] * BF(scale)
        keys, d_mixed = k_ref[:, sl], dm_ref[:, sl]
        scores = halves(dot(split_lanes(keys), queries, NT))
        d_probs = halves(dot(split_lanes(v_ref[:, sl]), d_mixed, NT))
        probs_low, d_scores = [], []
        for half in range(2):
            head = 2 * pair + half
            probs = jnp.exp(scores[half] + bias_ref[...] - lse_ref[head : head + 1, :])
            probs_low.append(probs.astype(BF))
            weighted = probs * d_probs[half]
            rows = jnp.sum(weighted, axis=0, keepdims=True)
            d_scores.append((weighted - probs * rows).astype(BF))
        d_scores = jnp.concatenate(d_scores, axis=0)
        d_value = jnp.where(low, *halves(dot(jnp.concatenate(probs_low, axis=0), d_mixed))).astype(BF)
        d_key = jnp.where(low, *halves(dot(d_scores, queries))).astype(BF)
        d_query = (dot(split_rows(keys.T), d_scores) * scale).astype(BF).T
        for i, item in enumerate((d_query, d_key, d_value)):
            dqkv_ref[:, i * width + first : i * width + first + 2 * HD] = item
        sums_ref[0, :, sl] += column_sum(d_query.astype(F32))
        sums_ref[1, :, sl] += column_sum(d_value.astype(F32))

    @pl.when(pl.program_id(0) == pl.num_programs(0) - 1)
    def _():
        total_ref[...] = table_ref[...]
        for i in range(2):
            total_ref[i : i + 1, :] = jnp.sum(sums_ref[i], axis=0, keepdims=True)


def attend_back(query, keys, values, d_mixed, lse, seg, table, after=()):
    count, width = query.shape
    rows = seg.shape[0] // 8
    slots = seg.shape[1]
    row = pl.BlockSpec((slots, width), lambda i: (i, 0))
    return pl.pallas_call(
        functools.partial(attend_back_kernel, len(after)),
        grid=(rows,),
        in_specs=[row] * 4
        + [
            pl.BlockSpec((lse.shape[0] // rows, slots), lambda i: (i, 0)),
            pl.BlockSpec((8, slots), lambda i: (i, 0)),
            whole(table.shape),
        ]
        + anywhere(len(after)),
        out_specs=[
            pl.BlockSpec((slots, 3 * width), lambda i: (i, 0)),
            pl.BlockSpec(table.shape, lambda i: (0, 0)),
        ],
        out_shape=[jax.ShapeDtypeStruct((count, 3 * width), BF), jax.ShapeDtypeStruct(table.shape, F32)],
        scratch_shapes=[pltpu.VMEM((slots, slots), F32), pltpu.VMEM((2, 8, width), F32)],
        compiler_params=params(),
        cost_estimate=cost(2.1e10, 1.5e7),
        name="attend_back",
    )(query, keys, values, d_mixed, lse, seg, table, *after)


def tokens_kernel(numbered, n_arrays, n_after, dfirst_ref, dqkv_ref, *refs):
    pieces = refs[:n_arrays]
    out_ref, w_ref, sems = refs[n_arrays + n_after :]
    width = dfirst_ref.shape[1]
    targets = [w_ref.at[:, pl.ds(which * width, width)] for which in range(3)]
    ready = load_weights(numbered, pieces, targets, sems)
    for which in range(3):
        ready(which)
    out_ref[...] = dfirst_ref[...] + dot(dqkv_ref[...], w_ref[...], NT)


def tokens_back(d_first, dqkv, weights, after=()):
    count, width = d_first.shape
    arrays, numbered = index_pieces(weights)
    tile = ROW_TILE
    return pl.pallas_call(
        functools.partial(tokens_kernel, numbered, len(arrays), len(after)),
        grid=(count // tile,),
        in_specs=[
            pl.BlockSpec((tile, width), lambda i: (i, 0)),
            pl.BlockSpec((tile, 3 * width), lambda i: (i, 0)),
        ]
        + anywhere(len(arrays) + len(after)),
        out_specs=pl.BlockSpec((tile, width), lambda i: (i, 0)),
        out_shape=jax.ShapeDtypeStruct((count, width), F32),
        scratch_shapes=[
            pltpu.VMEM((width, 3 * width), BF),
            pltpu.SemaphoreType.DMA((sum(len(p) for p in numbered),)),
        ],
        compiler_params=params(),
        cost_estimate=cost(1e10, 1.5e7),
        name="tokens_back",
    )(d_first, dqkv, *arrays, *after)


ORDER_ONE, ORDER_TWO = (0, Y, X, X | Y), (0, X, Y, X | Y)


def rep_bits():
    me = lax.axis_index("rep")
    return me & 1, me // 2


def arrange(left_ref, left, order):
    size = left.shape[0] // (2 * len(order))
    for which in range(2):
        for place, rel in enumerate(order):
            start = pl.multiple_of((lax.axis_index("fsdp") ^ (rel | which * CORE)) * size, size)
            at = (which * len(order) + place) * size
            left_ref[at : at + size, :] = left[pl.ds(start, size), :]


def place_rows(got, keep, send):
    places, size, _ = keep.shape
    for which, out in enumerate((keep, send)):
        for place in range(places):
            at = (which * places + place) * size
            out[place] = got[at : at + size, :]


def vector_rows(table_ref, shard, size):
    width = table_ref.shape[1]
    row = lax.broadcasted_iota(jnp.int32, (width, 128), 0)
    column = lax.broadcasted_iota(jnp.int32, (width, 128), 1)
    chosen = ((row == shard * size + column) & (column < size)).astype(BF)
    short = dot(table_ref[:8, :].astype(BF), chosen)
    long_size = 4 * size
    per_row = width // long_size
    start = pl.multiple_of(shard % per_row * long_size, 128)
    long = table_ref[pl.ds(8 + shard // per_row, 1), pl.ds(start, long_size)]
    zeros = lambda rows, columns: jnp.zeros((rows, columns), F32)
    return jnp.concatenate(
        [
            jnp.concatenate([short, zeros(8, width - 128)], axis=1),
            jnp.concatenate([long, zeros(1, width - long_size)], axis=1),
            zeros(7, width),
        ],
        axis=0,
    ).astype(BF)


def inner_grad_kernel(n_after, _, left, right, *refs):
    keep, send, left_ref = refs[n_after:]

    @pl.when(pl.program_id(0) == 0)
    def _():
        arrange(left_ref, left, ORDER_ONE)

    place_rows(dot(left_ref[...], right[...]).astype(BF), keep, send)


def inner_grad(left, right, shards, after=()):
    height, depth = left.shape
    wide = right.shape[1]
    chunk = wide // 4
    shape = (4, height // shards, wide)
    one, two = rep_bits()
    parts = jnp.stack([2 * (one ^ (g // 2)) + (two ^ (g % 2)) for g in range(4)]).astype(jnp.int32)
    return pl.pallas_call(
        functools.partial(inner_grad_kernel, len(after)),
        grid_spec=pltpu.PrefetchScalarGridSpec(
            num_scalar_prefetch=1,
            grid=(4,),
            in_specs=[
                pl.BlockSpec((height, depth), lambda g, p: (0, 0), pipeline_mode=pl.Buffered(1)),
                pl.BlockSpec((depth, chunk), lambda g, p: (0, p[g])),
            ]
            + anywhere(len(after)),
            out_specs=[pl.BlockSpec((*shape[:2], chunk), lambda g, p: (0, 0, g))] * 2,
            scratch_shapes=[pltpu.VMEM((height, depth), BF)],
        ),
        out_shape=[jax.ShapeDtypeStruct(shape, BF)] * 2,
        compiler_params=params(),
        cost_estimate=cost(3.5 * height * depth * wide, 4 * height * wide),
        name="inner_grad",
    )(parts, left, right, *after)


def outer_grad_kernel(_, left, right, keep, send, acc_ref):
    acc_ref[...] = dot(left[...], right[...])
    rows = keep.shape[2]
    wide = acc_ref.shape[1] // 2
    core = lax.axis_index("fsdp") & CORE
    one, two = rep_bits()
    blocks = acc_ref.shape[0] // rows
    for which, out in enumerate((keep, send)):
        start = pl.multiple_of((core ^ which) * wide, 128)
        for block in range(blocks):
            half, place = block // (blocks // 2), block % (blocks // 2)
            at = (place // (blocks // 4) ^ two) * (blocks // 4) + place % (blocks // 4)
            rows_part = acc_ref[block * rows : (block + 1) * rows, pl.ds(start, wide)].astype(BF)
            out[half ^ one, 0, :, pl.ds(pl.multiple_of(at * wide, 128), wide)] = rows_part


def outer_grad(left, right, shards):
    height, depth = left.shape
    wide = right.shape[1]
    chips = lax.axis_index("fsdp") // 2
    places = jnp.stack([chips ^ (rel // 2) for rel in ORDER_ONE]).astype(jnp.int32)
    chunk = 2 * wide // shards
    shape = (2, 4, height // shards, wide // 2)
    return pl.pallas_call(
        outer_grad_kernel,
        grid_spec=pltpu.PrefetchScalarGridSpec(
            num_scalar_prefetch=1,
            grid=(4,),
            in_specs=[
                pl.BlockSpec((height, depth), lambda g, p: (0, 0), pipeline_mode=pl.Buffered(1)),
                pl.BlockSpec((depth, chunk), lambda g, p: (0, p[g])),
            ],
            out_specs=[pl.BlockSpec((2, 1, *shape[2:]), lambda g, p: (0, g, 0, 0))] * 2,
            scratch_shapes=[pltpu.VMEM((height, chunk), F32)],
        ),
        out_shape=[jax.ShapeDtypeStruct(shape, BF)] * 2,
        compiler_params=params(),
        cost_estimate=cost(3.5 * height * depth * wide, 4 * height * wide),
        name="outer_grad",
    )(places, left, right)


def square_grad_kernel(n_after, tokens, mixed, dqkv, d_branch, table, *refs):
    keep_one, send_one, keep_two, send_two, left_ref = refs[n_after:]
    step = pl.program_id(0)
    size = keep_two.shape[1]
    for at, left, order in ((0, tokens, ORDER_ONE), (2, tokens, ORDER_TWO), (3, mixed, ORDER_TWO)):

        @pl.when(step == at)
        def _():
            arrange(left_ref, left, order)

    @pl.when(step < 2)
    def _():
        got = dot(left_ref[...], dqkv[...]).astype(BF)
        for which, out in enumerate((keep_one, send_one)):
            for place, rel in enumerate(ORDER_ONE):
                at = (which * len(ORDER_ONE) + place) * size
                out[place, :size, :] = got[at : at + size, :]

                @pl.when(step == 0)
                def _():
                    shard = lax.axis_index("fsdp") ^ (rel | which * CORE)
                    out[place, size:, :] = vector_rows(table, shard, size)

                @pl.when(step == 1)
                def _():
                    out[place, size:, :] = jnp.zeros((16, out.shape[2]), BF)

    @pl.when(step == 2)
    def _():
        place_rows(dot(left_ref[...], dqkv[...]).astype(BF), keep_two, send_two)

    @pl.when(step == 3)
    def _():
        place_rows(dot(left_ref[...], d_branch[...]).astype(BF), keep_two, send_two)


def square_grad(tokens_t, mixed_t, dqkv, d_branch, table, shards, after=()):
    height, depth = tokens_t.shape
    shape = (4, height // shards, 2 * height)
    block = (*shape[:2], height)
    tall = (shape[0], shape[1] + 16, shape[2])
    one = pl.BlockSpec((*tall[:2], height), lambda g: (0, 0, jnp.minimum(g, 1)))
    two = pl.BlockSpec(block, lambda g: (0, 0, jnp.maximum(g - 2, 0)))
    return pl.pallas_call(
        functools.partial(square_grad_kernel, len(after)),
        grid=(4,),
        in_specs=[
            whole((height, depth)),
            whole((height, depth)),
            pl.BlockSpec((depth, height), lambda g: (0, jnp.minimum(g, 2))),
            whole((depth, height)),
            whole(table.shape),
        ]
        + anywhere(len(after)),
        out_specs=[one, one, two, two],
        out_shape=[jax.ShapeDtypeStruct(tall, BF)] * 2 + [jax.ShapeDtypeStruct(shape, BF)] * 2,
        scratch_shapes=[pltpu.VMEM((height, depth), BF)],
        compiler_params=params(),
        cost_estimate=cost(1.1e10, 1.5e7),
        name="square_grad",
    )(tokens_t, mixed_t, dqkv, d_branch, table, *after)


def up(x):
    return x.astype(F32)


def fetch(terms, held_ref, sems):
    copies = [
        pltpu.make_async_copy(ref.at[0], held_ref.at[i, pl.ds(0, ref.shape[1])], sems.at[i])
        for i, ref in enumerate(terms)
    ]
    for copy in copies:
        copy.start()
    for copy in copies:
        copy.wait()


def add_places(terms, places):
    total = up(terms[0][places])
    for term in terms[1:]:
        total = total + up(term[places])
    return total.astype(BF)


def total_kernel(n_after, *refs):
    keep, send, held_ref, sems = refs[8 + n_after :]
    size = keep.shape[2]
    me = lax.axis_index("rep")
    fetch(refs[:8], held_ref, sems)
    for quarter in range(4):
        i, columns = quarter // 2, slice(quarter % 2 * size, (quarter % 2 + 1) * size)
        rows = refs[4 * i].shape[1]
        total = up(held_ref[4 * i, :rows, columns])
        for place in range(4 * i + 1, 4 * i + 4):
            total = total + up(held_ref[place, :rows, columns])
        rel = me ^ quarter
        for bit, out in enumerate((keep, send)):

            @pl.when(rel & 1 == bit)
            def _():
                out[rel // 2, :rows] = total.astype(BF)
                if rows < out.shape[1]:
                    out[rel // 2, rows:] = jnp.zeros((out.shape[1] - rows, size), BF)


def total_places(one, two, after):
    _, rows, wide = one[0].shape
    shape = (2, rows, wide // 2)
    return pl.pallas_call(
        functools.partial(total_kernel, len(after)),
        in_specs=anywhere(8 + len(after)),
        out_shape=[jax.ShapeDtypeStruct(shape, BF)] * 2,
        scratch_shapes=[
            pltpu.VMEM((8, rows, wide), BF),
            pltpu.SemaphoreType.DMA((8,)),
        ],
        compiler_params=pltpu.CompilerParams(vmem_limit_bytes=VMEM_BYTES),
        cost_estimate=cost(3e10, 1e7),
        name="total",
    )(*one, *two, *after)


class PairSum:
    def __init__(self, *groups, after=()):
        self.terms = [[keep, flip(pinned(send, *after), "fsdp", CORE)] for keep, send in groups]
        self.bits = (X, Y), (Y, X)

    def far(self, group, *after):
        terms = pinned(self.terms[group], *after)
        out = add_places(terms, slice(2, 4))
        self.terms[group] = [*terms, flip(out, "fsdp", self.bits[group][0])]
        return out

    def near(self, group, *after):
        terms = pinned(self.terms[group], *after)
        out = add_places(terms, slice(1, 2))
        self.terms[group] = [*terms, flip(out, "fsdp", self.bits[group][1])]
        return out

    def total(self, *after):
        self.part, self.send = total_places(*self.terms, after)
        return self.part

    def rep_first(self, *after):
        self.rep = flip(pinned(self.send, *after), "rep", 1)

    def rep_near(self, *after):
        part_far, rep_far = pinned((self.part, self.rep), *after)
        out = (up(part_far[1]) + up(rep_far[1])).astype(BF)
        self.rep_far = flip(out, "rep", 2)
        return out

    def own(self, *after):
        terms = pinned((self.part[0], self.rep[0], self.rep_far), *after)
        self.mine = add_places([t[None] for t in terms], 0)
        self.two = flip(self.mine, "rep", 2)
        return self.mine

    def own_near(self, *after):
        self.one = flip(pinned(self.mine, *after), "rep", 1)

    def parts(self, *after):
        three = flip(pinned(self.two, *after), "rep", 1)
        return [self.mine, self.one, self.two, three]


class Sum:
    def __init__(self, keep, send):
        self.keep, self.core = keep, flip(send, "fsdp", CORE)
        self.rep_first = keep.ndim == 4
        self.quarter = keep.shape[-1] // (2 if self.rep_first else 4)
        self.got = []

    def add(self, index, terms, *after):
        terms = [(self.keep, index), (self.core, index), *terms]
        arrays = pinned([array for array, _ in terms], *after)
        total = None
        for array, (_, at) in zip(arrays, terms):
            total = up(array[at]) if total is None else total + up(array[at])
        return total.astype(BF)

    def send(self, out, axis, bit):
        self.got.append(flip(out, axis, bit))
        return out

    def first(self, *after):
        if self.rep_first:
            return self.send(self.add((1,), [], *after), "rep", 1)
        return self.send(self.add((slice(2, 4),), [], *after), "fsdp", X)

    def second(self, *after):
        if self.rep_first:
            out = self.add((0, slice(2, 4)), [(self.got[0], slice(2, 4))], *after)
            return self.send(out, "fsdp", X)
        return self.send(self.add((slice(1, 2),), [(self.got[0], slice(1, 2))], *after), "fsdp", Y)

    def third(self, *after):
        if self.rep_first:
            got = [(g, slice(1, 2)) for g in self.got]
            return self.send(self.add((0, slice(1, 2)), got, *after), "fsdp", Y)
        columns = (slice(None), slice(2 * self.quarter, 4 * self.quarter))
        got = [(g, (0, *columns)) for g in self.got]
        return self.send(self.add((0, *columns), got, *after), "rep", 1)

    def rest(self, columns):
        columns = (slice(None), columns)
        if self.rep_first:
            return (0, 0, *columns), [(g, (0, *columns)) for g in self.got[:3]]
        return (0, *columns), [(g, (0, *columns)) for g in self.got[:2]] + [(self.got[2], columns)]

    def fourth(self, *after):
        index, got = self.rest(slice(self.quarter, 2 * self.quarter))
        return self.send(self.add(index, got, *after), "rep", 2)

    def own(self, *after):
        index, got = self.rest(slice(0, self.quarter))
        self.mine = self.add(index, [*got, (self.got[3], slice(None))], *after)
        self.two = flip(self.mine, "rep", 2)
        return self.mine

    def own_near(self, *after):
        self.one = flip(pinned(self.mine, *after), "rep", 1)

    def parts(self, *after):
        three = flip(pinned(self.two, *after), "rep", 1)
        return [self.mine, self.one, self.two, three]


def gathered(parts, held_ref, factor):
    one, two = rep_bits()
    for rel, ref in enumerate(parts):
        place = 2 * (one ^ (rel & 1)) + (two ^ (rel // 2))
        held_ref[place, : ref.shape[0]] = up(ref[...]) * factor


def finish_inner_kernel(factor, *refs):
    parts, out, held_ref = refs[:4], refs[4], refs[5]
    gathered(parts, held_ref, factor)
    size = held_ref.shape[2]
    for i in range(4):
        out[:, i * size : (i + 1) * size] = held_ref[i]


def finish_outer_kernel(factor, *refs):
    parts, out, held_ref = refs[:4], refs[4], refs[5]
    gathered(parts, held_ref, factor)
    rows, size = out.shape[0], held_ref.shape[2]
    blocks = [held_ref[i, :, at : at + rows] for i in range(4) for at in range(0, size, rows)]
    out[...] = jnp.concatenate(blocks, axis=0).T


def finish_square_kernel(factor, *refs):
    parts, outs, held_ref = refs[:4], refs[4:-1], refs[-1]
    me = lax.axis_index("rep")
    for rel, ref in enumerate(parts):
        held_ref[me ^ rel] = up(ref[...]) * factor
    size = outs[0].shape[0]
    for i in range(4):
        outs[i][...] = held_ref[i, :size]
    for i, out in enumerate(outs[4:]):
        out[...] = held_ref[0, size + i, : out.shape[0]]


def finish(kernel, parts, factor, shapes):
    return pl.pallas_call(
        functools.partial(kernel, factor),
        out_shape=[jax.ShapeDtypeStruct(shape, F32) for shape in shapes],
        scratch_shapes=[pltpu.VMEM((4, *parts[0].shape), F32)],
        compiler_params=pltpu.CompilerParams(vmem_limit_bytes=VMEM_BYTES),
        cost_estimate=cost(2e9, 1e7),
        name="finish",
    )(*parts)


def all_sum(values, axes=("fsdp", "rep")):
    for axis in axes:
        n = lax.axis_size(axis)
        if n & (n - 1):
            values = lax.psum(values, axis)
            continue
        bit = 1
        while bit < n:
            values = values + flip(values, axis, bit)
            bit *= 2
    return values


def body(
    tokens,
    doc_lengths,
    query_weight,
    key_weight,
    value_weight,
    output_weight,
    inner_weight,
    outer_weight,
    query_bias,
    value_bias,
    output_bias,
    inner_bias,
    outer_bias,
    first_gain,
    first_shift,
    second_gain,
    second_shift,
    cotangent,
):
    rows, slots, width = tokens.shape
    count = rows * slots
    docs = doc_lengths.shape[1]
    n_fsdp = lax.axis_size("fsdp")
    n_rep = lax.axis_size("rep")
    shard = query_weight.shape[0]
    outer_shard = outer_weight.shape[0]
    inner_width = inner_weight.shape[1]
    direct = n_fsdp == 8 and n_rep == 4 and shard % 16 == 0

    vectors = (
        query_bias,
        value_bias,
        output_bias,
        outer_bias,
        first_gain,
        first_shift,
        second_gain,
        second_shift,
        inner_bias,
    )
    if direct:
        half, outer_half = shard // 2, outer_shard // 2
        blocks = pack(query_weight, key_weight, value_weight, inner_weight, output_weight, outer_weight, vectors)
        one, two = Gather(blocks[0], X, Y), Gather(blocks[1], Y, X)
        blocks = pinned(blocks[2:], one.near, two.near)
        three, four = Gather(blocks[0], X, Y), Gather(blocks[1], Y, X)
        pairs = stacked(one.block, one.near, two.block, two.near)
        one.go(pairs[0])
        two.go(pairs[1])
        pairs = stacked(three.block, three.near, four.block, four.near, pairs)
        three.go(pairs[0])
        four.go(pairs[1])
        chips_x, chips_y = stacked(one.pair, one.far, two.pair, two.far, pairs)
        held_x, held_y = one.held_whole(chips_x), two.held_whole(chips_y)
        qw = part(held_x, 0, shard, shard)
        kw = part(held_x, shard, half, shard) + part(held_y, shard, half, shard, half)
        vw = part(held_y, 0, shard, shard)
        vec, bias_inner = unpack(part(held_x, shard + half, 16, 16), shard, outer_shard)
    else:
        qw, kw, vw, ow, iw, w2 = [
            [(lax.all_gather(w, "fsdp", axis=0, tiled=True), 0, w.shape[0] * n_fsdp, None, 0, 0, 0)]
            for w in (query_weight, key_weight, value_weight, output_weight, inner_weight, outer_weight)
        ]
        small = lax.all_gather(jnp.concatenate(vectors)[None], "fsdp", axis=0, tiled=True).astype(F32)
        vec = small[:, : 8 * shard].reshape(n_fsdp, 8, shard).transpose(1, 0, 2).reshape(8, width)
        bias_inner = small[:, 8 * shard :].reshape(1, inner_width)
        pairs = ()

    places = jnp.arange(docs, dtype=jnp.int32)
    ends = jnp.sum(
        jnp.where(places[None, :, None] >= places[None, None, :], doc_lengths[:, None, :], 0), axis=-1
    )
    slot = jnp.arange(slots, dtype=jnp.int32)
    segment = jnp.sum((slot[None, None, :] >= ends[:, :, None]).astype(jnp.int32), axis=1)
    seg = jnp.broadcast_to(segment[:, None, :].astype(F32), (rows, 8, slots)).reshape(rows * 8, slots)

    flat = tokens.reshape(count, width)
    query, keys, values, mixed_t, tokens_t, lse = attend(flat, seg, vec, (qw, kw, vw), pairs)
    if direct:
        three.far, four.far = pinned((three.far, four.far), lse)
        held_x, held_y = three.held(), four.held()
        iw = part(held_x, 0, half, shard) + part(held_y, 0, half, shard, half)
        ow = [(*piece[:-1], inner_width) for piece in iw]
        w2 = [
            (*piece[:4], outer_shard, which * outer_half + block * half, inner_width + (1 + block) * width)
            for which, held in enumerate((held_x, held_y))
            for block in range(outer_half // half)
            for piece in part(held, 0, half, shard)
        ]
    encoded, hidden_t, activated, d_outer_t, d_inner, d_first, d_branch, d_mixed, table = feed(
        mixed_t, flat, cotangent.reshape(count, width), seg, vec, bias_inner, (ow, iw, w2), docs
    )
    factor = 1.0 / math.sqrt(rows * n_rep * n_fsdp * slots)
    if direct:
        keep_outer, send_outer = outer_grad(d_outer_t, activated, n_fsdp)
        keep_inner, send_inner = inner_grad(hidden_t, d_inner, n_fsdp, (send_outer,))
        outer, inner = Sum(keep_outer, send_outer), Sum(keep_inner, send_inner)
        sent = outer.first(send_inner)
        sent = inner.first(sent)
        dqkv, table = attend_back(query, keys, values, d_mixed, lse, seg, table, (sent,))
        sent = outer.second(dqkv)
        sent = inner.second(sent)
        keep_one, send_one, keep_two, send_two = square_grad(
            tokens_t, mixed_t, dqkv, d_branch, table, n_fsdp, (sent,)
        )
        sent = outer.third(send_one)
        sent = inner.third(sent)
        square = PairSum((keep_one, send_one), (keep_two, send_two), after=(sent,))
        sent = square.far(0, sent)
        sent = square.far(1, sent)
        sent = outer.fourth(sent)
        sent = inner.fourth(sent)
        sent = square.near(0, sent)
        sent = square.near(1, sent)
        sent = outer.own(sent)
        sent = inner.own(sent)
        part_sum = square.total(sent)
        square.rep_first()
        tokens_grad = tokens_back(d_first, dqkv, (qw, kw, vw), (part_sum,))
        sent = square.rep_near(tokens_grad)
        outer.own_near(sent)
        inner.own_near(sent)
        outer_parts = outer.parts(sent)
        inner_parts = inner.parts(sent)
        (outer_all,) = finish(finish_outer_kernel, outer_parts, factor, (outer_weight.shape,))
        (inner_all,) = finish(finish_inner_kernel, inner_parts, factor, (inner_weight.shape,))
        square.own()
        square.own_near()
        shapes = (query_weight.shape,) * 4 + ((shard,),) * 8 + ((outer_shard,),)
        q_all, k_all, v_all, o_all, *short, long = finish(finish_square_kernel, square.parts(), factor, shapes)
    else:
        dqkv, table = attend_back(query, keys, values, d_mixed, lse, seg, table)
        tokens_grad = tokens_back(d_first, dqkv, (qw, kw, vw))

        def shared(left_t, right):
            total = lax.psum_scatter(dot(left_t, right), "fsdp", scatter_dimension=0, tiled=True)
            return up(lax.psum(total.astype(BF), "rep")) * factor

        outer_all = shared(activated.T, d_outer_t.T)
        inner_all = shared(hidden_t, d_inner)
        o_all = shared(mixed_t, d_branch)
        q_all, k_all, v_all = [shared(tokens_t, item) for item in jnp.split(dqkv, 3, axis=1)]
        vectors = all_sum(table[: 8 + inner_width // width]) * factor
        me = lax.axis_index("fsdp")
        short = lax.dynamic_slice_in_dim(vectors[:8], me * shard, shard, axis=1)
        long = lax.dynamic_slice_in_dim(vectors[8:].reshape(inner_width), me * outer_shard, outer_shard, axis=0)
    return (
        encoded.reshape(rows, slots, width),
        tokens_grad.reshape(rows, slots, width),
        q_all,
        k_all,
        v_all,
        o_all,
        inner_all,
        outer_all,
        short[0],
        short[1],
        short[2],
        long,
        short[3],
        short[4],
        short[5],
        short[6],
        short[7],
    )


def solution(mesh):
    data = P(("rep", "fsdp"), None, None)
    matrix, vector = P("fsdp", None), P("fsdp")
    return jax.shard_map(
        body,
        mesh=mesh,
        in_specs=(data, P(("rep", "fsdp"), None)) + (matrix,) * 6 + (vector,) * 9 + (data,),
        out_specs=(data, data) + (matrix,) * 6 + (vector,) * 9,
        check_vma=False,
    )
```

```python
import functools
import math

import jax
import jax.numpy as jnp
from jax import lax
from jax.experimental import pallas as pl
from jax.experimental.pallas import tpu as pltpu
from jax.sharding import PartitionSpec as P

HD = 64
EPSILON = 1e-05
BF = jnp.bfloat16
F32 = jnp.float32
NT = ((1,), (1,))
VMEM_BYTES = 60 * 2**20
CORE, X, Y = 1, 2, 4
ROW_TILE = 256
FF_CHUNK = 1536


def dot(a, b, dims=((1,), (0,))):
    return lax.dot_general(a, b, (dims, ((), ())), preferred_element_type=F32)


def params():
    return pltpu.CompilerParams(
        vmem_limit_bytes=VMEM_BYTES, dimension_semantics=("arbitrary",)
    )


def cost(flops, nbytes, trans=0):
    return pl.CostEstimate(
        flops=int(flops), bytes_accessed=int(nbytes), transcendentals=int(trans)
    )


def whole(shape):
    return pl.BlockSpec(
        shape, lambda *i: (0,) * len(shape), pipeline_mode=pl.Buffered(1)
    )


def anywhere(count):
    return [pl.BlockSpec(memory_space=pl.ANY)] * count


def flip(array, axis, bit):
    size = lax.axis_size(axis)
    return lax.ppermute(array, axis, [(i, i ^ bit) for i in range(size)])


def pinned(values, *others):
    return lax.optimization_barrier((values, others))[0]


def piece_copies(pieces, refs, target, sems, first):
    copies = []
    for slot, (which, start, rows, rel, shard, offset, column) in enumerate(pieces):
        place = 0
        if rel is not None:
            place = pl.multiple_of((lax.axis_index("fsdp") ^ rel) * shard + offset, math.gcd(shard, offset))
        copies.append(
            pltpu.make_async_copy(
                refs[which].at[pl.ds(start, rows), pl.ds(column, target.shape[1])],
                target.at[pl.ds(place, rows), :],
                sems.at[first + slot],
            )
        )
    return copies


def group_copies(numbered, refs, targets, sems):
    copies = []
    for pieces, target in zip(numbered, targets):
        copies.append(piece_copies(pieces, refs, target, sems, sum(len(c) for c in copies)))
    return copies


def index_pieces(weights):
    arrays, numbered = [], []
    for pieces in weights:
        mine = []
        for array, *rest in pieces:
            for n, seen in enumerate(arrays):
                if seen is array:
                    break
            else:
                n = len(arrays)
                arrays.append(array)
            mine.append((n, *rest))
        numbered.append(mine)
    return arrays, numbered


class Gather:
    def __init__(self, block, first, second):
        self.block, self.bits = block, (first, second)
        self.near = flip(block, "fsdp", first)

    def go(self, pair):
        self.pair = pair
        self.far = flip(pair, "fsdp", self.bits[1])
        return pair

    def parts(self):
        first, second = self.bits
        rows = self.block.shape[0]
        return [(self.pair, 0, 0), (self.pair, rows, first), (self.far, 0, second), (self.far, rows, first | second)]

    def held(self):
        other = {id(a): flip(a, "fsdp", CORE) for a in (self.pair, self.far)}
        return self.parts() + [(other[id(a)], at, rel | CORE) for a, at, rel in self.parts()]

    def held_whole(self, chips):
        first, second = self.bits
        rels = (0, first, second, first | second)
        return [
            (array, place * self.block.shape[0], rel | core)
            for core, array in ((0, chips), (CORE, flip(chips, "fsdp", CORE)))
            for place, rel in enumerate(rels)
        ]


def stack_kernel(n_after, one, two, three, four, *refs):
    for out, parts in zip(refs[n_after:], ((one, two), (three, four))):
        at = 0
        for ref in parts:
            rows = ref.shape[0]
            out[at : at + rows, :] = ref[...]
            at += rows


def stacked(one, two, three, four, after=()):
    full = lambda a: pl.BlockSpec(a.shape, lambda g: (0, 0))
    outs = [
        jax.ShapeDtypeStruct((a.shape[0] + b.shape[0], a.shape[1]), BF) for a, b in ((one, two), (three, four))
    ]
    return pl.pallas_call(
        functools.partial(stack_kernel, len(after)),
        grid=(1,),
        in_specs=[full(a) for a in (one, two, three, four)] + anywhere(len(after)),
        out_specs=[full(a) for a in outs],
        out_shape=outs,
        compiler_params=params(),
        cost_estimate=cost(2e9, 3e6),
        name="stacked",
    )(one, two, three, four, *after)


def pack_kernel(half, query_ref, key_ref, value_ref, *refs):
    vectors, (one_ref, two_ref) = refs[:-2], refs[-2:]
    shard, width = query_ref.shape
    one_ref[:shard, :] = query_ref[...]
    one_ref[shard : shard + half, :] = key_ref[:half, :]
    two_ref[:shard, :] = value_ref[...]
    two_ref[shard:, :] = key_ref[half:, :]
    rows = []
    for ref in vectors:
        size = ref.shape[0]
        rows.append(
            jnp.concatenate([ref[...].astype(F32).reshape(1, size), jnp.zeros((1, width - size), F32)], axis=1)
        )
    rows.append(jnp.zeros((16 - len(rows), width), F32))
    one_ref[shard + half :, :] = jnp.concatenate(rows, axis=0).astype(BF)


def pack_wide_kernel(half, wi_ref, wo_ref, w2_ref, three_ref, four_ref):
    wide, width = wi_ref.shape[1], wo_ref.shape[1]
    blocks = w2_ref.shape[0] // (2 * half)
    for place, ref in enumerate((three_ref, four_ref)):
        ref[:, :wide] = wi_ref[place * half : (place + 1) * half, :]
        ref[:, wide : wide + width] = wo_ref[place * half : (place + 1) * half, :]
        for block in range(blocks):
            row, column = (place * blocks + block) * half, wide + (1 + block) * width
            ref[:, column : column + width] = w2_ref[row : row + half, :]


def pack(query, key, value, vectors):
    shard, width = query.shape
    half = shard // 2
    return pl.pallas_call(
        functools.partial(pack_kernel, half),
        out_shape=[
            jax.ShapeDtypeStruct((shard + half + 16, width), BF),
            jax.ShapeDtypeStruct((shard + half, width), BF),
        ],
        compiler_params=pltpu.CompilerParams(vmem_limit_bytes=VMEM_BYTES),
        name="pack",
    )(query, key, value, *vectors)


def pack_wide(inner, output, outer):
    half, width = inner.shape[0] // 2, output.shape[1]
    wide = inner.shape[1] + width * (1 + outer.shape[0] // (2 * half))
    return pl.pallas_call(
        functools.partial(pack_wide_kernel, half),
        out_shape=[jax.ShapeDtypeStruct((half, wide), BF)] * 2,
        compiler_params=pltpu.CompilerParams(vmem_limit_bytes=VMEM_BYTES),
        name="pack_wide",
    )(inner, output, outer)


def unpack_kernel(numbered, n_arrays, shard, long, *refs):
    pieces = refs[:n_arrays]
    vec_ref, inner_ref, held_ref, sems = refs[n_arrays:]
    copies = piece_copies(numbered[0], pieces, held_ref, sems, 0)
    for copy in copies:
        copy.start()
    for copy in copies:
        copy.wait()
    n = len(copies)
    parts = [held_ref[16 * i : 16 * i + 16, :] for i in range(n)]
    slot = lax.broadcasted_iota(jnp.int32, (n * 128, n * shard), 0)
    place = lax.broadcasted_iota(jnp.int32, (n * 128, n * shard), 1)
    at = slot % 128
    spread = ((at < shard) & (place == slot // 128 * shard + at)).astype(BF)
    vec_ref[...] = dot(jnp.concatenate([p[:, :128] for p in parts], axis=1), spread)[:8]
    for i, p in enumerate(parts):
        inner_ref[:, i * long : (i + 1) * long] = p[8:9, :long].astype(F32)


def unpack(pieces, shard, long):
    arrays, numbered = index_pieces([pieces])
    n, width = len(pieces), pieces[0][0].shape[1]
    return pl.pallas_call(
        functools.partial(unpack_kernel, numbered, len(arrays), shard, long),
        in_specs=anywhere(len(arrays)),
        out_shape=[
            jax.ShapeDtypeStruct((8, n * shard), F32),
            jax.ShapeDtypeStruct((1, n * long), F32),
        ],
        scratch_shapes=[pltpu.VMEM((16 * n, width), BF), pltpu.SemaphoreType.DMA((n,))],
        name="unpack",
    )(*arrays)


def part(held, start, rows, shard, offset=0):
    return [(a, at + start, rows, rel, shard, offset, 0) for a, at, rel in held]


def column_of(row):
    return jnp.broadcast_to(row, (128, row.shape[1])).T[:, :1]


def split_lanes(pair):
    low = lax.broadcasted_iota(jnp.int32, (1, 2 * HD), 1) < HD
    return jnp.concatenate([jnp.where(low, pair, BF(0)), jnp.where(low, BF(0), pair)], axis=0)


def split_rows(pair_t):
    low = lax.broadcasted_iota(jnp.int32, (2 * HD, 1), 0) < HD
    return jnp.concatenate([jnp.where(low, pair_t, BF(0)), jnp.where(low, BF(0), pair_t)], axis=1)


def attend_kernel(numbered, n_arrays, n_after, heads, tok_ref, seg_ref, vec_ref, *refs):
    pieces = refs[:n_arrays]
    q_ref, k_ref, v_ref, mt_ref, tt_ref, lse_ref, w_ref, bias_ref, qs_ref, sems = refs[n_arrays + n_after :]
    width = tok_ref.shape[1]
    targets = [w_ref.at[:, pl.ds(which * width, width)] for which in range(3)]
    ready = load_weights(numbered, pieces, targets, sems)
    x = tok_ref[...]
    tt_ref[...] = x.T
    seg = seg_ref[0:1, :]
    bias_ref[...] = jnp.where(column_of(seg) == seg, 0.0, -1e30)

    for which in range(3):
        ready(which)
    qkv = dot(x, w_ref[...])
    q = (qkv[:, :width] + vec_ref[0:1, :]).astype(BF)
    q_ref[...] = q
    qs_ref[...] = q * BF(1.0 / math.sqrt(HD))
    k_ref[...] = qkv[:, width : 2 * width].astype(BF)
    v_ref[...] = (qkv[:, 2 * width :] + vec_ref[1:2, :]).astype(BF)
    for pair in range(heads // 2):
        sl = slice(pair * 2 * HD, (pair + 1) * 2 * HD)
        scores = dot(split_lanes(k_ref[:, sl]), qs_ref[:, sl], NT)
        slots = scores.shape[0] // 2
        weights, inverse = [], []
        for half in range(2):
            mine = scores[half * slots : (half + 1) * slots] + bias_ref[...]
            top = jnp.max(mine, axis=0, keepdims=True)
            exps = jnp.exp(mine - top)
            total = jnp.sum(exps, axis=0, keepdims=True)
            head = 2 * pair + half
            lse_ref[head : head + 1, :] = top + jnp.log(total)
            weights.append(exps.astype(BF))
            inverse.append(1.0 / total)
        out = dot(split_rows(v_ref[:, sl].T), jnp.concatenate(weights, axis=0))
        low_rows = lax.broadcasted_iota(jnp.int32, (2 * HD, 1), 0) < HD
        mt_ref[sl, :] = (out * jnp.where(low_rows, inverse[0], inverse[1])).astype(BF)


def attend(tokens, seg, vec, weights, after=()):
    count, width = tokens.shape
    rows = seg.shape[0] // 8
    slots = count // rows
    heads = width // HD
    padded = -(-heads // 8) * 8
    arrays, numbered = index_pieces(weights)
    row = pl.BlockSpec((slots, width), lambda i: (i, 0))
    col = pl.BlockSpec((width, slots), lambda i: (0, i))
    return pl.pallas_call(
        functools.partial(attend_kernel, numbered, len(arrays), len(after), heads),
        grid=(rows,),
        in_specs=[row, pl.BlockSpec((8, slots), lambda i: (i, 0)), whole(vec.shape)]
        + anywhere(len(arrays) + len(after)),
        out_specs=[row, row, row, col, col, pl.BlockSpec((padded, slots), lambda i: (i, 0))],
        out_shape=[jax.ShapeDtypeStruct((count, width), BF)] * 3
        + [jax.ShapeDtypeStruct((width, count), BF)] * 2
        + [jax.ShapeDtypeStruct((rows * padded, slots), F32)],
        scratch_shapes=[
            pltpu.VMEM((width, 3 * width), BF),
            pltpu.VMEM((slots, slots), F32),
            pltpu.VMEM((slots, width), BF),
            pltpu.SemaphoreType.DMA((sum(len(p) for p in numbered),)),
        ],
        compiler_params=params(),
        cost_estimate=cost(1e9, 1e6),
        name="attend",
    )(tokens, seg, vec, *arrays, *after)


def gelu_pair(v):
    area = 0.5 + 0.5 * lax.erf(v * math.sqrt(0.5))
    density = jnp.exp2(v * v * (-0.5 / math.log(2.0))) * (1.0 / math.sqrt(2.0 * math.pi))
    return v * area, area + v * density


def norm(z):
    center = z - jnp.mean(z, axis=-1, keepdims=True)
    scale = lax.rsqrt(jnp.mean(center * center, axis=-1, keepdims=True) + EPSILON)
    return center * scale, scale


def norm_back(grad, n, scale, gain):
    dn = grad * gain
    return (
        dn - jnp.mean(dn, axis=-1, keepdims=True) - n * jnp.mean(dn * n, axis=-1, keepdims=True)
    ) * scale


def column_sum(x):
    return jnp.sum(x.reshape(x.shape[0] // 8, 8, x.shape[1]), axis=0)


def load_weights(numbered, pieces, targets, sems):
    groups = group_copies(numbered, pieces, targets, sems)
    first_step = pl.program_id(0) == 0

    @pl.when(first_step)
    def _():
        for copies in groups:
            for copy in copies:
                copy.start()

    def ready(which):
        @pl.when(first_step)
        def _():
            for copy in groups[which]:
                copy.wait()

    return ready


def vector(vec_ref, i):
    return vec_ref[i : i + 1, :]


def feed_kernel(numbered, n_arrays, docs, mt_ref, tok_ref, cot_ref, seg_ref, vec_ref, bi_ref, *refs):
    pieces = refs[:n_arrays]
    outs = refs[n_arrays:]
    enc_ref, ht_ref, act_ref, dot_ref, din_ref, dfirst_ref, dbr_ref, dm_ref, total_ref = outs[:9]
    wo_ref, wi_ref, w2_ref, slope_ref, sums_ref, sumi_ref, sems = outs[9:]
    ready = load_weights(numbered, pieces, (wo_ref, wi_ref, w2_ref), sems)

    @pl.when(pl.program_id(0) == 0)
    def _():
        sums_ref[...] = jnp.zeros_like(sums_ref)
        sumi_ref[...] = jnp.zeros_like(sumi_ref)

    width, inner_width = wi_ref.shape
    ready(0)
    z1 = tok_ref[...].astype(F32) + dot(mt_ref[...].T, wo_ref[...]) + vector(vec_ref, 2)
    n1, r1 = norm(z1)
    hidden = n1 * vector(vec_ref, 4) + vector(vec_ref, 5)
    hidden_low = hidden.astype(BF)
    ht_ref[...] = hidden_low.T
    ready(1)
    z2 = hidden + vector(vec_ref, 3)
    for c in range(0, inner_width, FF_CHUNK):
        sl = slice(c, c + FF_CHUNK)
        act, slope = gelu_pair(dot(hidden_low, wi_ref[:, sl]) + bi_ref[:, sl])
        act = act.astype(BF)
        act_ref[:, sl] = act
        slope_ref[:, sl] = slope
        if c == 0:
            ready(2)
        z2 = z2 + dot(act, w2_ref[sl, :])
    n2, r2 = norm(z2)
    gain = vector(vec_ref, 6)
    enc_ref[...] = (n2 * gain + vector(vec_ref, 7)).astype(BF)
    grad = cot_ref[...] * column_of((seg_ref[0:1, :] < docs).astype(F32))
    d_second = norm_back(grad, n2, r2, gain)
    d_outer = d_second.astype(BF)
    dot_ref[...] = d_outer.T
    d_hidden = d_second
    for c in range(0, inner_width, FF_CHUNK):
        sl = slice(c, c + FF_CHUNK)
        d_inner = (dot(d_outer, w2_ref[sl, :], NT) * slope_ref[:, sl]).astype(BF)
        din_ref[:, sl] = d_inner
        sumi_ref[:, sl] += column_sum(d_inner.astype(F32))
        d_hidden = d_hidden + dot(d_inner, wi_ref[:, sl], NT)
    d_first = norm_back(d_hidden, n1, r1, vector(vec_ref, 4))
    dfirst_ref[...] = d_first
    d_branch = d_first.astype(BF)
    dbr_ref[...] = d_branch
    dm_ref[...] = dot(d_branch, wo_ref[...], NT).astype(BF)
    for i, item in enumerate(
        (d_branch.astype(F32), d_outer.astype(F32), d_hidden * n1, d_hidden, grad * n2, grad)
    ):
        sums_ref[i] += column_sum(item)

    @pl.when(pl.program_id(0) == pl.num_programs(0) - 1)
    def _():
        total_ref[...] = jnp.zeros_like(total_ref)
        for i in range(6):
            total_ref[2 + i : 3 + i, :] = jnp.sum(sums_ref[i], axis=0, keepdims=True)
        for i in range(inner_width // width):
            part_sum = jnp.sum(sumi_ref[:, i * width : (i + 1) * width], axis=0, keepdims=True)
            total_ref[8 + i : 9 + i, :] = part_sum


def feed(mixed_t, tokens, cotangent, seg, vec, bias_inner, weights, docs):
    count, width = tokens.shape
    inner_width = bias_inner.shape[1]
    arrays, numbered = index_pieces(weights)
    tile = ROW_TILE
    row = pl.BlockSpec((tile, width), lambda i: (i, 0))
    col = pl.BlockSpec((width, tile), lambda i: (0, i))
    wide = pl.BlockSpec((tile, inner_width), lambda i: (i, 0))
    per_row = seg.shape[1] // tile
    sum_rows = -(-(8 + inner_width // width) // 8) * 8
    out = jax.ShapeDtypeStruct
    return pl.pallas_call(
        functools.partial(feed_kernel, numbered, len(arrays), docs),
        grid=(count // tile,),
        in_specs=[
            col,
            row,
            row,
            pl.BlockSpec((8, tile), lambda i: (i // per_row, i % per_row)),
            whole(vec.shape),
            whole(bias_inner.shape),
        ]
        + anywhere(len(arrays)),
        out_specs=[row, col, wide, col, wide, row, row, row, pl.BlockSpec((sum_rows, width), lambda i: (0, 0))],
        out_shape=[
            out((count, width), BF),
            out((width, count), BF),
            out((count, inner_width), BF),
            out((width, count), BF),
            out((count, inner_width), BF),
            out((count, width), F32),
            out((count, width), BF),
            out((count, width), BF),
            out((sum_rows, width), F32),
        ],
        scratch_shapes=[
            pltpu.VMEM((width, width), BF),
            pltpu.VMEM((width, inner_width), BF),
            pltpu.VMEM((inner_width, width), BF),
            pltpu.VMEM((tile, inner_width), F32),
            pltpu.VMEM((6, 8, width), F32),
            pltpu.VMEM((8, inner_width), F32),
            pltpu.SemaphoreType.DMA((sum(len(p) for p in numbered),)),
        ],
        compiler_params=params(),
        cost_estimate=cost(4e10, 5e7),
        name="feed",
    )(mixed_t, tokens, cotangent, seg, vec, bias_inner, *arrays)


def attend_back_kernel(n_after, q_ref, k_ref, v_ref, dm_ref, lse_ref, seg_ref, table_ref, *refs):
    dqkv_ref, total_ref, bias_ref, sums_ref = refs[n_after:]

    @pl.when(pl.program_id(0) == 0)
    def _():
        sums_ref[...] = jnp.zeros_like(sums_ref)

    width = q_ref.shape[1]
    scale = 1.0 / math.sqrt(HD)
    seg = seg_ref[0:1, :]
    bias_ref[...] = jnp.where(column_of(seg) == seg, 0.0, -1e30)
    low = lax.broadcasted_iota(jnp.int32, (1, 2 * HD), 1) < HD
    slots = q_ref.shape[0]
    halves = lambda a: (a[:slots], a[slots:])
    for pair in range(width // (2 * HD)):
        first = pair * 2 * HD
        sl = slice(first, first + 2 * HD)
        queries = q_ref[:, sl] * BF(scale)
        keys, d_mixed = k_ref[:, sl], dm_ref[:, sl]
        scores = halves(dot(split_lanes(keys), queries, NT))
        d_probs = halves(dot(split_lanes(v_ref[:, sl]), d_mixed, NT))
        probs_low, d_scores = [], []
        for half in range(2):
            head = 2 * pair + half
            probs = jnp.exp(scores[half] + bias_ref[...] - lse_ref[head : head + 1, :])
            probs_low.append(probs.astype(BF))
            weighted = probs * d_probs[half]
            rows = jnp.sum(weighted, axis=0, keepdims=True)
            d_scores.append((weighted - probs * rows).astype(BF))
        d_scores = jnp.concatenate(d_scores, axis=0)
        d_value = jnp.where(low, *halves(dot(jnp.concatenate(probs_low, axis=0), d_mixed))).astype(BF)
        d_key = jnp.where(low, *halves(dot(d_scores, queries))).astype(BF)
        d_query = (dot(split_rows(keys.T), d_scores) * scale).astype(BF).T
        for i, item in enumerate((d_query, d_key, d_value)):
            dqkv_ref[:, i * width + first : i * width + first + 2 * HD] = item
        sums_ref[0, :, sl] += column_sum(d_query.astype(F32))
        sums_ref[1, :, sl] += column_sum(d_value.astype(F32))

    @pl.when(pl.program_id(0) == pl.num_programs(0) - 1)
    def _():
        total_ref[...] = table_ref[...]
        for i in range(2):
            total_ref[i : i + 1, :] = jnp.sum(sums_ref[i], axis=0, keepdims=True)


def attend_back(query, keys, values, d_mixed, lse, seg, table, after=()):
    count, width = query.shape
    rows = seg.shape[0] // 8
    slots = seg.shape[1]
    row = pl.BlockSpec((slots, width), lambda i: (i, 0))
    return pl.pallas_call(
        functools.partial(attend_back_kernel, len(after)),
        grid=(rows,),
        in_specs=[row] * 4
        + [
            pl.BlockSpec((lse.shape[0] // rows, slots), lambda i: (i, 0)),
            pl.BlockSpec((8, slots), lambda i: (i, 0)),
            whole(table.shape),
        ]
        + anywhere(len(after)),
        out_specs=[
            pl.BlockSpec((slots, 3 * width), lambda i: (i, 0)),
            pl.BlockSpec(table.shape, lambda i: (0, 0)),
        ],
        out_shape=[jax.ShapeDtypeStruct((count, 3 * width), BF), jax.ShapeDtypeStruct(table.shape, F32)],
        scratch_shapes=[pltpu.VMEM((slots, slots), F32), pltpu.VMEM((2, 8, width), F32)],
        compiler_params=params(),
        cost_estimate=cost(2.1e10, 1.5e7),
        name="attend_back",
    )(query, keys, values, d_mixed, lse, seg, table, *after)


def tokens_kernel(numbered, n_arrays, n_after, dfirst_ref, dqkv_ref, *refs):
    pieces = refs[:n_arrays]
    out_ref, w_ref, sems = refs[n_arrays + n_after :]
    width = dfirst_ref.shape[1]
    targets = [w_ref.at[:, pl.ds(which * width, width)] for which in range(3)]
    ready = load_weights(numbered, pieces, targets, sems)
    for which in range(3):
        ready(which)
    out_ref[...] = dfirst_ref[...] + dot(dqkv_ref[...], w_ref[...], NT)


def tokens_back(d_first, dqkv, weights, after=()):
    count, width = d_first.shape
    arrays, numbered = index_pieces(weights)
    tile = ROW_TILE
    return pl.pallas_call(
        functools.partial(tokens_kernel, numbered, len(arrays), len(after)),
        grid=(count // tile,),
        in_specs=[
            pl.BlockSpec((tile, width), lambda i: (i, 0)),
            pl.BlockSpec((tile, 3 * width), lambda i: (i, 0)),
        ]
        + anywhere(len(arrays) + len(after)),
        out_specs=pl.BlockSpec((tile, width), lambda i: (i, 0)),
        out_shape=jax.ShapeDtypeStruct((count, width), F32),
        scratch_shapes=[
            pltpu.VMEM((width, 3 * width), BF),
            pltpu.SemaphoreType.DMA((sum(len(p) for p in numbered),)),
        ],
        compiler_params=params(),
        cost_estimate=cost(1e10, 1.5e7),
        name="tokens_back",
    )(d_first, dqkv, *arrays, *after)


ORDER_ONE, ORDER_TWO = (0, Y, X, X | Y), (0, X, Y, X | Y)


def rep_bits():
    me = lax.axis_index("rep")
    return me & 1, me // 2


def arrange(left_ref, left, order):
    size = left.shape[0] // (2 * len(order))
    for which in range(2):
        for place, rel in enumerate(order):
            start = pl.multiple_of((lax.axis_index("fsdp") ^ (rel | which * CORE)) * size, size)
            at = (which * len(order) + place) * size
            left_ref[at : at + size, :] = left[pl.ds(start, size), :]


def place_rows(got, keep, send):
    places, size, _ = keep.shape
    for which, out in enumerate((keep, send)):
        for place in range(places):
            at = (which * places + place) * size
            out[place] = got[at : at + size, :]


def vector_rows(table_ref, shard, size):
    width = table_ref.shape[1]
    row = lax.broadcasted_iota(jnp.int32, (width, 128), 0)
    column = lax.broadcasted_iota(jnp.int32, (width, 128), 1)
    chosen = ((row == shard * size + column) & (column < size)).astype(BF)
    short = dot(table_ref[:8, :].astype(BF), chosen)
    long_size = 4 * size
    per_row = width // long_size
    start = pl.multiple_of(shard % per_row * long_size, 128)
    long = table_ref[pl.ds(8 + shard // per_row, 1), pl.ds(start, long_size)]
    zeros = lambda rows, columns: jnp.zeros((rows, columns), F32)
    return jnp.concatenate(
        [
            jnp.concatenate([short, zeros(8, width - 128)], axis=1),
            jnp.concatenate([long, zeros(1, width - long_size)], axis=1),
            zeros(7, width),
        ],
        axis=0,
    ).astype(BF)


def inner_grad_kernel(n_after, _, left, right, *refs):
    keep, send, left_ref = refs[n_after:]

    @pl.when(pl.program_id(0) == 0)
    def _():
        arrange(left_ref, left, ORDER_ONE)

    place_rows(dot(left_ref[...], right[...]).astype(BF), keep, send)


def inner_grad(left, right, shards, after=()):
    height, depth = left.shape
    wide = right.shape[1]
    chunk = wide // 4
    shape = (4, height // shards, wide)
    one, two = rep_bits()
    parts = jnp.stack([2 * (one ^ (g // 2)) + (two ^ (g % 2)) for g in range(4)]).astype(jnp.int32)
    return pl.pallas_call(
        functools.partial(inner_grad_kernel, len(after)),
        grid_spec=pltpu.PrefetchScalarGridSpec(
            num_scalar_prefetch=1,
            grid=(4,),
            in_specs=[
                pl.BlockSpec((height, depth), lambda g, p: (0, 0), pipeline_mode=pl.Buffered(1)),
                pl.BlockSpec((depth, chunk), lambda g, p: (0, p[g])),
            ]
            + anywhere(len(after)),
            out_specs=[pl.BlockSpec((*shape[:2], chunk), lambda g, p: (0, 0, g))] * 2,
            scratch_shapes=[pltpu.VMEM((height, depth), BF)],
        ),
        out_shape=[jax.ShapeDtypeStruct(shape, BF)] * 2,
        compiler_params=params(),
        cost_estimate=cost(3.5 * height * depth * wide, 4 * height * wide),
        name="inner_grad",
    )(parts, left, right, *after)


def outer_grad_kernel(_, left, right_keep, right_send, keep, send):
    rows = keep.shape[2]
    wide = right_keep.shape[1]
    got = dot(left[...], jnp.concatenate([right_keep[...], right_send[...]], axis=1)).astype(BF)
    one, two = rep_bits()
    blocks = got.shape[0] // rows
    for which, out in enumerate((keep, send)):
        for block in range(blocks):
            half, place = block // (blocks // 2), block % (blocks // 2)
            at = (place // (blocks // 4) ^ two) * (blocks // 4) + place % (blocks // 4)
            rows_part = got[block * rows : (block + 1) * rows, which * wide : (which + 1) * wide]
            out[half ^ one, 0, :, pl.ds(pl.multiple_of(at * wide, 128), wide)] = rows_part


def outer_grad(left, right, shards):
    height, depth = left.shape
    wide = right.shape[1]
    me = lax.axis_index("fsdp")
    places = jnp.stack([me ^ (rel | core) for core in (0, CORE) for rel in ORDER_ONE]).astype(jnp.int32)
    chunk = wide // shards
    shape = (2, 4, height // shards, wide // 2)
    return pl.pallas_call(
        outer_grad_kernel,
        grid_spec=pltpu.PrefetchScalarGridSpec(
            num_scalar_prefetch=1,
            grid=(4,),
            in_specs=[
                pl.BlockSpec((height, depth), lambda g, p: (0, 0), pipeline_mode=pl.Buffered(1)),
                pl.BlockSpec((depth, chunk), lambda g, p: (0, p[g])),
                pl.BlockSpec((depth, chunk), lambda g, p: (0, p[4 + g])),
            ],
            out_specs=[pl.BlockSpec((2, 1, *shape[2:]), lambda g, p: (0, g, 0, 0))] * 2,
        ),
        out_shape=[jax.ShapeDtypeStruct(shape, BF)] * 2,
        compiler_params=params(),
        cost_estimate=cost(3.5 * height * depth * wide, 4 * height * wide),
        name="outer_grad",
    )(places, left, right, right)


def square_grad_kernel(n_after, tokens, mixed, dqkv, d_branch, table, *refs):
    keep_one, send_one, keep_two, send_two, left_ref = refs[n_after:]
    step = pl.program_id(0)
    size = keep_two.shape[1]
    for at, left, order in ((0, tokens, ORDER_ONE), (2, tokens, ORDER_TWO), (3, mixed, ORDER_TWO)):

        @pl.when(step == at)
        def _():
            arrange(left_ref, left, order)

    @pl.when(step < 2)
    def _():
        got = dot(left_ref[...], dqkv[...]).astype(BF)
        for which, out in enumerate((keep_one, send_one)):
            for place, rel in enumerate(ORDER_ONE):
                at = (which * len(ORDER_ONE) + place) * size
                out[place, :size, :] = got[at : at + size, :]

                @pl.when(step == 0)
                def _():
                    shard = lax.axis_index("fsdp") ^ (rel | which * CORE)
                    out[place, size:, :] = vector_rows(table, shard, size)

                @pl.when(step == 1)
                def _():
                    out[place, size:, :] = jnp.zeros((16, out.shape[2]), BF)

    @pl.when(step == 2)
    def _():
        place_rows(dot(left_ref[...], dqkv[...]).astype(BF), keep_two, send_two)

    @pl.when(step == 3)
    def _():
        place_rows(dot(left_ref[...], d_branch[...]).astype(BF), keep_two, send_two)


def square_grad(tokens_t, mixed_t, dqkv, d_branch, table, shards, after=()):
    height, depth = tokens_t.shape
    shape = (4, height // shards, 2 * height)
    block = (*shape[:2], height)
    tall = (shape[0], shape[1] + 16, shape[2])
    one = pl.BlockSpec((*tall[:2], height), lambda g: (0, 0, jnp.minimum(g, 1)))
    two = pl.BlockSpec(block, lambda g: (0, 0, jnp.maximum(g - 2, 0)))
    return pl.pallas_call(
        functools.partial(square_grad_kernel, len(after)),
        grid=(4,),
        in_specs=[
            whole((height, depth)),
            whole((height, depth)),
            pl.BlockSpec((depth, height), lambda g: (0, jnp.minimum(g, 2))),
            whole((depth, height)),
            whole(table.shape),
        ]
        + anywhere(len(after)),
        out_specs=[one, one, two, two],
        out_shape=[jax.ShapeDtypeStruct(tall, BF)] * 2 + [jax.ShapeDtypeStruct(shape, BF)] * 2,
        scratch_shapes=[pltpu.VMEM((height, depth), BF)],
        compiler_params=params(),
        cost_estimate=cost(1.1e10, 1.5e7),
        name="square_grad",
    )(tokens_t, mixed_t, dqkv, d_branch, table, *after)


def up(x):
    return x.astype(F32)


def fetch(terms, held_ref, sems):
    copies = [
        pltpu.make_async_copy(ref.at[0], held_ref.at[i, pl.ds(0, ref.shape[1])], sems.at[i])
        for i, ref in enumerate(terms)
    ]
    for copy in copies:
        copy.start()
    for copy in copies:
        copy.wait()


def add_places(terms, places):
    total = up(terms[0][places])
    for term in terms[1:]:
        total = total + up(term[places])
    return total.astype(BF)


def total_kernel(n_after, *refs):
    keep, send, held_ref, sems = refs[8 + n_after :]
    size = keep.shape[2]
    me = lax.axis_index("rep")
    fetch(refs[:8], held_ref, sems)
    for quarter in range(4):
        i, columns = quarter // 2, slice(quarter % 2 * size, (quarter % 2 + 1) * size)
        rows = refs[4 * i].shape[1]
        total = up(held_ref[4 * i, :rows, columns])
        for place in range(4 * i + 1, 4 * i + 4):
            total = total + up(held_ref[place, :rows, columns])
        rel = me ^ quarter
        for bit, out in enumerate((keep, send)):

            @pl.when(rel & 1 == bit)
            def _():
                out[rel // 2, :rows] = total.astype(BF)
                if rows < out.shape[1]:
                    out[rel // 2, rows:] = jnp.zeros((out.shape[1] - rows, size), BF)


def total_places(one, two, after):
    _, rows, wide = one[0].shape
    shape = (2, rows, wide // 2)
    return pl.pallas_call(
        functools.partial(total_kernel, len(after)),
        in_specs=anywhere(8 + len(after)),
        out_shape=[jax.ShapeDtypeStruct(shape, BF)] * 2,
        scratch_shapes=[
            pltpu.VMEM((8, rows, wide), BF),
            pltpu.SemaphoreType.DMA((8,)),
        ],
        compiler_params=pltpu.CompilerParams(vmem_limit_bytes=VMEM_BYTES),
        cost_estimate=cost(3e10, 1e7),
        name="total",
    )(*one, *two, *after)


class PairSum:
    def __init__(self, *groups, after=()):
        self.terms = [[keep, flip(pinned(send, *after), "fsdp", CORE)] for keep, send in groups]
        self.bits = (X, Y), (Y, X)

    def far(self, group, *after):
        terms = pinned(self.terms[group], *after)
        out = add_places(terms, slice(2, 4))
        self.terms[group] = [*terms, flip(out, "fsdp", self.bits[group][0])]
        return out

    def near(self, group, *after):
        terms = pinned(self.terms[group], *after)
        out = add_places(terms, slice(1, 2))
        self.terms[group] = [*terms, flip(out, "fsdp", self.bits[group][1])]
        return out

    def total(self, *after):
        self.part, self.send = total_places(*self.terms, after)
        return self.part

    def rep_first(self, *after):
        self.rep = flip(pinned(self.send, *after), "rep", 1)

    def rep_near(self, *after):
        part_far, rep_far = pinned((self.part, self.rep), *after)
        out = (up(part_far[1]) + up(rep_far[1])).astype(BF)
        self.rep_far = flip(out, "rep", 2)
        return out

    def own(self, *after):
        terms = pinned((self.part[0], self.rep[0], self.rep_far), *after)
        self.mine = add_places([t[None] for t in terms], 0)
        self.two = flip(self.mine, "rep", 2)
        return self.mine

    def own_near(self, *after):
        self.one = flip(pinned(self.mine, *after), "rep", 1)

    def parts(self, *after):
        three = flip(pinned(self.two, *after), "rep", 1)
        return [self.mine, self.one, self.two, three]


class Sum:
    def __init__(self, keep, send):
        self.keep, self.core = keep, flip(send, "fsdp", CORE)
        self.rep_first = keep.ndim == 4
        self.quarter = keep.shape[-1] // (2 if self.rep_first else 4)
        self.got = []

    def add(self, index, terms, *after):
        terms = [(self.keep, index), (self.core, index), *terms]
        arrays = pinned([array for array, _ in terms], *after)
        total = None
        for array, (_, at) in zip(arrays, terms):
            total = up(array[at]) if total is None else total + up(array[at])
        return total.astype(BF)

    def send(self, out, axis, bit):
        self.got.append(flip(out, axis, bit))
        return out

    def first(self, *after):
        if self.rep_first:
            return self.send(self.add((1,), [], *after), "rep", 1)
        return self.send(self.add((slice(2, 4),), [], *after), "fsdp", X)

    def second(self, *after):
        if self.rep_first:
            out = self.add((0, slice(2, 4)), [(self.got[0], slice(2, 4))], *after)
            return self.send(out, "fsdp", X)
        return self.send(self.add((slice(1, 2),), [(self.got[0], slice(1, 2))], *after), "fsdp", Y)

    def third(self, *after):
        if self.rep_first:
            got = [(g, slice(1, 2)) for g in self.got]
            return self.send(self.add((0, slice(1, 2)), got, *after), "fsdp", Y)
        columns = (slice(None), slice(2 * self.quarter, 4 * self.quarter))
        got = [(g, (0, *columns)) for g in self.got]
        return self.send(self.add((0, *columns), got, *after), "rep", 1)

    def rest(self, columns):
        columns = (slice(None), columns)
        if self.rep_first:
            return (0, 0, *columns), [(g, (0, *columns)) for g in self.got[:3]]
        return (0, *columns), [(g, (0, *columns)) for g in self.got[:2]] + [(self.got[2], columns)]

    def fourth(self, *after):
        index, got = self.rest(slice(self.quarter, 2 * self.quarter))
        return self.send(self.add(index, got, *after), "rep", 2)

    def own(self, *after):
        index, got = self.rest(slice(0, self.quarter))
        self.mine = self.add(index, [*got, (self.got[3], slice(None))], *after)
        self.two = flip(self.mine, "rep", 2)
        return self.mine

    def own_near(self, *after):
        self.one = flip(pinned(self.mine, *after), "rep", 1)

    def parts(self, *after):
        three = flip(pinned(self.two, *after), "rep", 1)
        return [self.mine, self.one, self.two, three]


def gathered(parts, held_ref, factor):
    one, two = rep_bits()
    for rel, ref in enumerate(parts):
        place = 2 * (one ^ (rel & 1)) + (two ^ (rel // 2))
        held_ref[place, : ref.shape[0]] = up(ref[...]) * factor


def finish_inner_kernel(factor, *refs):
    parts, out, held_ref = refs[:4], refs[4], refs[5]
    gathered(parts, held_ref, factor)
    size = held_ref.shape[2]
    for i in range(4):
        out[:, i * size : (i + 1) * size] = held_ref[i]


def finish_outer_kernel(factor, *refs):
    parts, out, held_ref = refs[:4], refs[4], refs[5]
    gathered(parts, held_ref, factor)
    rows, size = out.shape[0], held_ref.shape[2]
    blocks = [held_ref[i, :, at : at + rows] for i in range(4) for at in range(0, size, rows)]
    out[...] = jnp.concatenate(blocks, axis=0).T


def finish_square_kernel(factor, *refs):
    parts, outs, held_ref = refs[:4], refs[4:-1], refs[-1]
    me = lax.axis_index("rep")
    for rel, ref in enumerate(parts):
        held_ref[me ^ rel] = up(ref[...]) * factor
    size = outs[0].shape[0]
    for i in range(4):
        outs[i][...] = held_ref[i, :size]
    for i, out in enumerate(outs[4:]):
        out[...] = held_ref[0, size + i, : out.shape[0]]


def finish(kernel, parts, factor, shapes):
    return pl.pallas_call(
        functools.partial(kernel, factor),
        out_shape=[jax.ShapeDtypeStruct(shape, F32) for shape in shapes],
        scratch_shapes=[pltpu.VMEM((4, *parts[0].shape), F32)],
        compiler_params=pltpu.CompilerParams(vmem_limit_bytes=VMEM_BYTES),
        cost_estimate=cost(2e9, 1e7),
        name="finish",
    )(*parts)


def all_sum(values, axes=("fsdp", "rep")):
    for axis in axes:
        n = lax.axis_size(axis)
        if n & (n - 1):
            values = lax.psum(values, axis)
            continue
        bit = 1
        while bit < n:
            values = values + flip(values, axis, bit)
            bit *= 2
    return values


def body(
    tokens,
    doc_lengths,
    query_weight,
    key_weight,
    value_weight,
    output_weight,
    inner_weight,
    outer_weight,
    query_bias,
    value_bias,
    output_bias,
    inner_bias,
    outer_bias,
    first_gain,
    first_shift,
    second_gain,
    second_shift,
    cotangent,
):
    rows, slots, width = tokens.shape
    count = rows * slots
    docs = doc_lengths.shape[1]
    n_fsdp = lax.axis_size("fsdp")
    n_rep = lax.axis_size("rep")
    shard = query_weight.shape[0]
    outer_shard = outer_weight.shape[0]
    inner_width = inner_weight.shape[1]
    direct = n_fsdp == 8 and n_rep == 4 and shard % 16 == 0

    vectors = (
        query_bias,
        value_bias,
        output_bias,
        outer_bias,
        first_gain,
        first_shift,
        second_gain,
        second_shift,
        inner_bias,
    )
    if direct:
        half, outer_half = shard // 2, outer_shard // 2
        blocks = pack(query_weight, key_weight, value_weight, vectors)
        one, two = Gather(blocks[0], X, Y), Gather(blocks[1], Y, X)
        blocks = pack_wide(*pinned((inner_weight, output_weight, outer_weight), *blocks))
        blocks = pinned(blocks, one.near, two.near)
        three, four = Gather(blocks[0], X, Y), Gather(blocks[1], Y, X)
        pairs = stacked(one.block, one.near, two.block, two.near)
        one.go(pairs[0])
        two.go(pairs[1])
        pairs = stacked(three.block, three.near, four.block, four.near, pairs)
        three.go(pairs[0])
        four.go(pairs[1])
        chips_x, chips_y = [
            jnp.concatenate(pinned((item.pair, item.far), pairs), axis=0) for item in (one, two)
        ]
        held_x, held_y = one.held_whole(chips_x), two.held_whole(chips_y)
        qw = part(held_x, 0, shard, shard)
        kw = part(held_x, shard, half, shard) + part(held_y, shard, half, shard, half)
        vw = part(held_y, 0, shard, shard)
        vec, bias_inner = unpack(part(held_x, shard + half, 16, 16), shard, outer_shard)
    else:
        qw, kw, vw, ow, iw, w2 = [
            [(lax.all_gather(w, "fsdp", axis=0, tiled=True), 0, w.shape[0] * n_fsdp, None, 0, 0, 0)]
            for w in (query_weight, key_weight, value_weight, output_weight, inner_weight, outer_weight)
        ]
        small = lax.all_gather(jnp.concatenate(vectors)[None], "fsdp", axis=0, tiled=True).astype(F32)
        vec = small[:, : 8 * shard].reshape(n_fsdp, 8, shard).transpose(1, 0, 2).reshape(8, width)
        bias_inner = small[:, 8 * shard :].reshape(1, inner_width)
        pairs = ()

    places = jnp.arange(docs, dtype=jnp.int32)
    ends = jnp.sum(
        jnp.where(places[None, :, None] >= places[None, None, :], doc_lengths[:, None, :], 0), axis=-1
    )
    slot = jnp.arange(slots, dtype=jnp.int32)
    segment = jnp.sum((slot[None, None, :] >= ends[:, :, None]).astype(jnp.int32), axis=1)
    seg = jnp.broadcast_to(segment[:, None, :].astype(F32), (rows, 8, slots)).reshape(rows * 8, slots)

    flat = tokens.reshape(count, width)
    query, keys, values, mixed_t, tokens_t, lse = attend(flat, seg, vec, (qw, kw, vw), pairs)
    if direct:
        three.far, four.far = pinned((three.far, four.far), lse)
        held_x, held_y = three.held(), four.held()
        iw = part(held_x, 0, half, shard) + part(held_y, 0, half, shard, half)
        ow = [(*piece[:-1], inner_width) for piece in iw]
        w2 = [
            (*piece[:4], outer_shard, which * outer_half + block * half, inner_width + (1 + block) * width)
            for which, held in enumerate((held_x, held_y))
            for block in range(outer_half // half)
            for piece in part(held, 0, half, shard)
        ]
    encoded, hidden_t, activated, d_outer_t, d_inner, d_first, d_branch, d_mixed, table = feed(
        mixed_t, flat, cotangent.reshape(count, width), seg, vec, bias_inner, (ow, iw, w2), docs
    )
    factor = 1.0 / math.sqrt(rows * n_rep * n_fsdp * slots)
    if direct:
        keep_outer, send_outer = outer_grad(d_outer_t, activated, n_fsdp)
        keep_inner, send_inner = inner_grad(hidden_t, d_inner, n_fsdp, (send_outer,))
        outer, inner = Sum(keep_outer, send_outer), Sum(keep_inner, send_inner)
        sent = outer.first(send_inner)
        sent = inner.first(sent)
        dqkv, table = attend_back(query, keys, values, d_mixed, lse, seg, table, (sent,))
        sent = outer.second(dqkv)
        sent = inner.second(sent)
        keep_one, send_one, keep_two, send_two = square_grad(
            tokens_t, mixed_t, dqkv, d_branch, table, n_fsdp, (sent,)
        )
        sent = outer.third(send_one)
        sent = inner.third(sent)
        square = PairSum((keep_one, send_one), (keep_two, send_two), after=(sent,))
        sent = square.far(0, sent)
        sent = square.far(1, sent)
        sent = outer.fourth(sent)
        sent = inner.fourth(sent)
        sent = square.near(0, sent)
        sent = square.near(1, sent)
        sent = outer.own(sent)
        sent = inner.own(sent)
        part_sum = square.total(sent)
        square.rep_first()
        tokens_grad = tokens_back(d_first, dqkv, (qw, kw, vw), (part_sum,))
        sent = square.rep_near(tokens_grad)
        outer.own_near(sent)
        inner.own_near(sent)
        outer_parts = outer.parts(sent)
        inner_parts = inner.parts(sent)
        (outer_all,) = finish(finish_outer_kernel, outer_parts, factor, (outer_weight.shape,))
        (inner_all,) = finish(finish_inner_kernel, inner_parts, factor, (inner_weight.shape,))
        square.own()
        square.own_near()
        shapes = (query_weight.shape,) * 4 + ((shard,),) * 8 + ((outer_shard,),)
        q_all, k_all, v_all, o_all, *short, long = finish(finish_square_kernel, square.parts(), factor, shapes)
    else:
        dqkv, table = attend_back(query, keys, values, d_mixed, lse, seg, table)
        tokens_grad = tokens_back(d_first, dqkv, (qw, kw, vw))

        def shared(left_t, right):
            total = lax.psum_scatter(dot(left_t, right), "fsdp", scatter_dimension=0, tiled=True)
            return up(lax.psum(total.astype(BF), "rep")) * factor

        outer_all = shared(activated.T, d_outer_t.T)
        inner_all = shared(hidden_t, d_inner)
        o_all = shared(mixed_t, d_branch)
        q_all, k_all, v_all = [shared(tokens_t, item) for item in jnp.split(dqkv, 3, axis=1)]
        vectors = all_sum(table[: 8 + inner_width // width]) * factor
        me = lax.axis_index("fsdp")
        short = lax.dynamic_slice_in_dim(vectors[:8], me * shard, shard, axis=1)
        long = lax.dynamic_slice_in_dim(vectors[8:].reshape(inner_width), me * outer_shard, outer_shard, axis=0)
    return (
        encoded.reshape(rows, slots, width),
        tokens_grad.reshape(rows, slots, width),
        q_all,
        k_all,
        v_all,
        o_all,
        inner_all,
        outer_all,
        short[0],
        short[1],
        short[2],
        long,
        short[3],
        short[4],
        short[5],
        short[6],
        short[7],
    )


def solution(mesh):
    data = P(("rep", "fsdp"), None, None)
    matrix, vector = P("fsdp", None), P("fsdp")
    return jax.shard_map(
        body,
        mesh=mesh,
        in_specs=(data, P(("rep", "fsdp"), None)) + (matrix,) * 6 + (vector,) * 9 + (data,),
        out_specs=(data, data) + (matrix,) * 6 + (vector,) * 9,
        check_vma=False,
    )
```

```python
import functools
import math

import jax
import jax.numpy as jnp
from jax import lax
from jax.experimental import pallas as pl
from jax.experimental.pallas import tpu as pltpu
from jax.sharding import PartitionSpec as P

HD = 64
EPSILON = 1e-05
BF = jnp.bfloat16
F32 = jnp.float32
NT = ((1,), (1,))
VMEM_BYTES = 60 * 2**20
CORE, X, Y = 1, 2, 4
ROW_TILE = 256
FF_CHUNK = 1536


def dot(a, b, dims=((1,), (0,))):
    return lax.dot_general(a, b, (dims, ((), ())), preferred_element_type=F32)


def params(limit=VMEM_BYTES):
    return pltpu.CompilerParams(
        vmem_limit_bytes=limit, dimension_semantics=("arbitrary",)
    )


def cost(flops, nbytes, trans=0):
    return pl.CostEstimate(
        flops=int(flops), bytes_accessed=int(nbytes), transcendentals=int(trans)
    )


def whole(shape):
    return pl.BlockSpec(
        shape, lambda *i: (0,) * len(shape), pipeline_mode=pl.Buffered(1)
    )


def anywhere(count):
    return [pl.BlockSpec(memory_space=pl.ANY)] * count


def flip(array, axis, bit):
    size = lax.axis_size(axis)
    return lax.ppermute(array, axis, [(i, i ^ bit) for i in range(size)])


def pinned(values, *others):
    return lax.optimization_barrier((values, others))[0]


def piece_copies(pieces, refs, target, sems, first):
    copies = []
    for slot, (which, start, rows, rel, shard, offset, column) in enumerate(pieces):
        place = 0
        if rel is not None:
            place = pl.multiple_of((lax.axis_index("fsdp") ^ rel) * shard + offset, math.gcd(shard, offset))
        copies.append(
            pltpu.make_async_copy(
                refs[which].at[pl.ds(start, rows), pl.ds(column, target.shape[1])],
                target.at[pl.ds(place, rows), :],
                sems.at[first + slot],
            )
        )
    return copies


def group_copies(numbered, refs, targets, sems):
    copies = []
    for pieces, target in zip(numbered, targets):
        copies.append(piece_copies(pieces, refs, target, sems, sum(len(c) for c in copies)))
    return copies


def index_pieces(weights):
    arrays, numbered = [], []
    for pieces in weights:
        mine = []
        for array, *rest in pieces:
            for n, seen in enumerate(arrays):
                if seen is array:
                    break
            else:
                n = len(arrays)
                arrays.append(array)
            mine.append((n, *rest))
        numbered.append(mine)
    return arrays, numbered


class Gather:
    def __init__(self, block, first, second):
        self.block, self.bits = block, (first, second)
        self.near = flip(block, "fsdp", first)

    def go(self, pair):
        self.pair = pair
        self.far = flip(pair, "fsdp", self.bits[1])
        return pair

    def parts(self):
        first, second = self.bits
        rows = self.block.shape[0]
        return [(self.pair, 0, 0), (self.pair, rows, first), (self.far, 0, second), (self.far, rows, first | second)]

    def held(self):
        other = {id(a): flip(a, "fsdp", CORE) for a in (self.pair, self.far)}
        return self.parts() + [(other[id(a)], at, rel | CORE) for a, at, rel in self.parts()]

    def held_whole(self, chips):
        first, second = self.bits
        rels = (0, first, second, first | second)
        return [
            (array, place * self.block.shape[0], rel | core)
            for core, array in ((0, chips), (CORE, flip(chips, "fsdp", CORE)))
            for place, rel in enumerate(rels)
        ]


def stack_kernel(n_after, one, two, three, four, *refs):
    for out, parts in zip(refs[n_after:], ((one, two), (three, four))):
        at = 0
        for ref in parts:
            rows = ref.shape[0]
            out[at : at + rows, :] = ref[...]
            at += rows


def stacked(one, two, three, four, after=()):
    full = lambda a: pl.BlockSpec(a.shape, lambda g: (0, 0))
    outs = [
        jax.ShapeDtypeStruct((a.shape[0] + b.shape[0], a.shape[1]), BF) for a, b in ((one, two), (three, four))
    ]
    return pl.pallas_call(
        functools.partial(stack_kernel, len(after)),
        grid=(1,),
        in_specs=[full(a) for a in (one, two, three, four)] + anywhere(len(after)),
        out_specs=[full(a) for a in outs],
        out_shape=outs,
        compiler_params=params(),
        cost_estimate=cost(2e9, 3e6),
        name="stacked",
    )(one, two, three, four, *after)


def pack_kernel(half, query_ref, key_ref, value_ref, *refs):
    vectors, (one_ref, two_ref) = refs[:-2], refs[-2:]
    shard, width = query_ref.shape
    one_ref[:shard, :] = query_ref[...]
    one_ref[shard : shard + half, :] = key_ref[:half, :]
    two_ref[:shard, :] = value_ref[...]
    two_ref[shard:, :] = key_ref[half:, :]
    rows = []
    for ref in vectors:
        size = ref.shape[0]
        rows.append(
            jnp.concatenate([ref[...].astype(F32).reshape(1, size), jnp.zeros((1, width - size), F32)], axis=1)
        )
    rows.append(jnp.zeros((16 - len(rows), width), F32))
    one_ref[shard + half :, :] = jnp.concatenate(rows, axis=0).astype(BF)


def pack_wide_kernel(half, wi_ref, wo_ref, w2_ref, three_ref, four_ref):
    wide, width = wi_ref.shape[1], wo_ref.shape[1]
    blocks = w2_ref.shape[0] // (2 * half)
    for place, ref in enumerate((three_ref, four_ref)):
        ref[:, :wide] = wi_ref[place * half : (place + 1) * half, :]
        ref[:, wide : wide + width] = wo_ref[place * half : (place + 1) * half, :]
        for block in range(blocks):
            row, column = (place * blocks + block) * half, wide + (1 + block) * width
            ref[:, column : column + width] = w2_ref[row : row + half, :]


def pack(query, key, value, vectors):
    shard, width = query.shape
    half = shard // 2
    return pl.pallas_call(
        functools.partial(pack_kernel, half),
        out_shape=[
            jax.ShapeDtypeStruct((shard + half + 16, width), BF),
            jax.ShapeDtypeStruct((shard + half, width), BF),
        ],
        compiler_params=pltpu.CompilerParams(vmem_limit_bytes=VMEM_BYTES),
        name="pack",
    )(query, key, value, *vectors)


def pack_wide(inner, output, outer):
    half, width = inner.shape[0] // 2, output.shape[1]
    wide = inner.shape[1] + width * (1 + outer.shape[0] // (2 * half))
    return pl.pallas_call(
        functools.partial(pack_wide_kernel, half),
        out_shape=[jax.ShapeDtypeStruct((half, wide), BF)] * 2,
        compiler_params=pltpu.CompilerParams(vmem_limit_bytes=VMEM_BYTES),
        name="pack_wide",
    )(inner, output, outer)


def unpack_kernel(numbered, n_arrays, shard, long, *refs):
    pieces = refs[:n_arrays]
    vec_ref, inner_ref, held_ref, sems = refs[n_arrays:]
    copies = piece_copies(numbered[0], pieces, held_ref, sems, 0)
    for copy in copies:
        copy.start()
    for copy in copies:
        copy.wait()
    n = len(copies)
    parts = [held_ref[16 * i : 16 * i + 16, :] for i in range(n)]
    slot = lax.broadcasted_iota(jnp.int32, (n * 128, n * shard), 0)
    place = lax.broadcasted_iota(jnp.int32, (n * 128, n * shard), 1)
    at = slot % 128
    spread = ((at < shard) & (place == slot // 128 * shard + at)).astype(BF)
    vec_ref[...] = dot(jnp.concatenate([p[:, :128] for p in parts], axis=1), spread)[:8]
    for i, p in enumerate(parts):
        inner_ref[:, i * long : (i + 1) * long] = p[8:9, :long].astype(F32)


def unpack(pieces, shard, long):
    arrays, numbered = index_pieces([pieces])
    n, width = len(pieces), pieces[0][0].shape[1]
    return pl.pallas_call(
        functools.partial(unpack_kernel, numbered, len(arrays), shard, long),
        in_specs=anywhere(len(arrays)),
        out_shape=[
            jax.ShapeDtypeStruct((8, n * shard), F32),
            jax.ShapeDtypeStruct((1, n * long), F32),
        ],
        scratch_shapes=[pltpu.VMEM((16 * n, width), BF), pltpu.SemaphoreType.DMA((n,))],
        name="unpack",
    )(*arrays)


def part(held, start, rows, shard, offset=0):
    return [(a, at + start, rows, rel, shard, offset, 0) for a, at, rel in held]


def column_of(row):
    return jnp.broadcast_to(row, (128, row.shape[1])).T[:, :1]


def split_lanes(pair):
    low = lax.broadcasted_iota(jnp.int32, (1, 2 * HD), 1) < HD
    return jnp.concatenate([jnp.where(low, pair, BF(0)), jnp.where(low, BF(0), pair)], axis=0)


def split_rows(pair_t):
    low = lax.broadcasted_iota(jnp.int32, (2 * HD, 1), 0) < HD
    return jnp.concatenate([jnp.where(low, pair_t, BF(0)), jnp.where(low, BF(0), pair_t)], axis=1)


def attend_kernel(numbered, n_arrays, n_after, heads, tok_ref, seg_ref, vec_ref, *refs):
    pieces = refs[:n_arrays]
    q_ref, k_ref, v_ref, mt_ref, tt_ref, lse_ref, w_ref, bias_ref, qs_ref, sems = refs[n_arrays + n_after :]
    width = tok_ref.shape[1]
    targets = [w_ref.at[:, pl.ds(which * width, width)] for which in range(3)]
    ready = load_weights(numbered, pieces, targets, sems)
    x = tok_ref[...]
    tt_ref[...] = x.T
    seg = seg_ref[0:1, :]
    bias_ref[...] = jnp.where(column_of(seg) == seg, 0.0, -1e30)

    for which in range(3):
        ready(which)
    qkv = dot(x, w_ref[...])
    q = (qkv[:, :width] + vec_ref[0:1, :]).astype(BF)
    q_ref[...] = q
    qs_ref[...] = q * BF(1.0 / math.sqrt(HD))
    k_ref[...] = qkv[:, width : 2 * width].astype(BF)
    v_ref[...] = (qkv[:, 2 * width :] + vec_ref[1:2, :]).astype(BF)
    for pair in range(heads // 2):
        sl = slice(pair * 2 * HD, (pair + 1) * 2 * HD)
        scores = dot(split_lanes(k_ref[:, sl]), qs_ref[:, sl], NT)
        slots = scores.shape[0] // 2
        weights, inverse = [], []
        for half in range(2):
            mine = scores[half * slots : (half + 1) * slots] + bias_ref[...]
            top = jnp.max(mine, axis=0, keepdims=True)
            exps = jnp.exp(mine - top)
            total = jnp.sum(exps, axis=0, keepdims=True)
            head = 2 * pair + half
            lse_ref[head : head + 1, :] = top + jnp.log(total)
            weights.append(exps.astype(BF))
            inverse.append(1.0 / total)
        out = dot(split_rows(v_ref[:, sl].T), jnp.concatenate(weights, axis=0))
        low_rows = lax.broadcasted_iota(jnp.int32, (2 * HD, 1), 0) < HD
        mt_ref[sl, :] = (out * jnp.where(low_rows, inverse[0], inverse[1])).astype(BF)


def attend(tokens, seg, vec, weights, after=()):
    count, width = tokens.shape
    rows = seg.shape[0] // 8
    slots = count // rows
    heads = width // HD
    padded = -(-heads // 8) * 8
    arrays, numbered = index_pieces(weights)
    row = pl.BlockSpec((slots, width), lambda i: (i, 0))
    col = pl.BlockSpec((width, slots), lambda i: (0, i))
    return pl.pallas_call(
        functools.partial(attend_kernel, numbered, len(arrays), len(after), heads),
        grid=(rows,),
        in_specs=[row, pl.BlockSpec((8, slots), lambda i: (i, 0)), whole(vec.shape)]
        + anywhere(len(arrays) + len(after)),
        out_specs=[row, row, row, col, col, pl.BlockSpec((padded, slots), lambda i: (i, 0))],
        out_shape=[jax.ShapeDtypeStruct((count, width), BF)] * 3
        + [jax.ShapeDtypeStruct((width, count), BF)] * 2
        + [jax.ShapeDtypeStruct((rows * padded, slots), F32)],
        scratch_shapes=[
            pltpu.VMEM((width, 3 * width), BF),
            pltpu.VMEM((slots, slots), F32),
            pltpu.VMEM((slots, width), BF),
            pltpu.SemaphoreType.DMA((sum(len(p) for p in numbered),)),
        ],
        compiler_params=params(),
        cost_estimate=cost(1e9, 1e6),
        name="attend",
    )(tokens, seg, vec, *arrays, *after)


def gelu_pair(v):
    area = 0.5 + 0.5 * lax.erf(v * math.sqrt(0.5))
    density = jnp.exp2(v * v * (-0.5 / math.log(2.0))) * (1.0 / math.sqrt(2.0 * math.pi))
    return v * area, area + v * density


def norm(z):
    center = z - jnp.mean(z, axis=-1, keepdims=True)
    scale = lax.rsqrt(jnp.mean(center * center, axis=-1, keepdims=True) + EPSILON)
    return center * scale, scale


def norm_back(grad, n, scale, gain):
    dn = grad * gain
    return (
        dn - jnp.mean(dn, axis=-1, keepdims=True) - n * jnp.mean(dn * n, axis=-1, keepdims=True)
    ) * scale


def column_sum(x):
    return jnp.sum(x.reshape(x.shape[0] // 8, 8, x.shape[1]), axis=0)


def load_weights(numbered, pieces, targets, sems):
    groups = group_copies(numbered, pieces, targets, sems)
    first_step = pl.program_id(0) == 0

    @pl.when(first_step)
    def _():
        for copies in groups:
            for copy in copies:
                copy.start()

    def ready(which):
        @pl.when(first_step)
        def _():
            for copy in groups[which]:
                copy.wait()

    return ready


def vector(vec_ref, i):
    return vec_ref[i : i + 1, :]


def feed_kernel(numbered, n_arrays, docs, mt_ref, tok_ref, cot_ref, seg_ref, vec_ref, bi_ref, *refs):
    pieces = refs[:n_arrays]
    outs = refs[n_arrays:]
    enc_ref, ht_ref, act_ref, dot_ref, din_ref, dfirst_ref, dbr_ref, dm_ref, total_ref = outs[:9]
    wo_ref, wi_ref, w2_ref, slope_ref, sums_ref, sumi_ref, sems = outs[9:]
    ready = load_weights(numbered, pieces, (wo_ref, wi_ref, w2_ref), sems)

    @pl.when(pl.program_id(0) == 0)
    def _():
        sums_ref[...] = jnp.zeros_like(sums_ref)
        sumi_ref[...] = jnp.zeros_like(sumi_ref)

    width, inner_width = wi_ref.shape
    ready(0)
    z1 = tok_ref[...].astype(F32) + dot(mt_ref[...].T, wo_ref[...]) + vector(vec_ref, 2)
    n1, r1 = norm(z1)
    hidden = n1 * vector(vec_ref, 4) + vector(vec_ref, 5)
    hidden_low = hidden.astype(BF)
    ht_ref[...] = hidden_low.T
    ready(1)
    z2 = hidden + vector(vec_ref, 3)
    for c in range(0, inner_width, FF_CHUNK):
        sl = slice(c, c + FF_CHUNK)
        act, slope = gelu_pair(dot(hidden_low, wi_ref[:, sl]) + bi_ref[:, sl])
        act = act.astype(BF)
        act_ref[:, sl] = act
        slope_ref[:, sl] = slope
        if c == 0:
            ready(2)
        z2 = z2 + dot(act, w2_ref[sl, :])
    n2, r2 = norm(z2)
    gain = vector(vec_ref, 6)
    enc_ref[...] = (n2 * gain + vector(vec_ref, 7)).astype(BF)
    grad = cot_ref[...] * column_of((seg_ref[0:1, :] < docs).astype(F32))
    d_second = norm_back(grad, n2, r2, gain)
    d_outer = d_second.astype(BF)
    dot_ref[...] = d_outer.T
    d_hidden = d_second
    for c in range(0, inner_width, FF_CHUNK):
        sl = slice(c, c + FF_CHUNK)
        d_inner = (dot(d_outer, w2_ref[sl, :], NT) * slope_ref[:, sl]).astype(BF)
        din_ref[:, sl] = d_inner
        sumi_ref[:, sl] += column_sum(d_inner.astype(F32))
        d_hidden = d_hidden + dot(d_inner, wi_ref[:, sl], NT)
    d_first = norm_back(d_hidden, n1, r1, vector(vec_ref, 4))
    dfirst_ref[...] = d_first
    d_branch = d_first.astype(BF)
    dbr_ref[...] = d_branch
    dm_ref[...] = dot(d_branch, wo_ref[...], NT).astype(BF)
    for i, item in enumerate(
        (d_branch.astype(F32), d_outer.astype(F32), d_hidden * n1, d_hidden, grad * n2, grad)
    ):
        sums_ref[i] += column_sum(item)

    @pl.when(pl.program_id(0) == pl.num_programs(0) - 1)
    def _():
        total_ref[...] = jnp.zeros_like(total_ref)
        for i in range(6):
            total_ref[2 + i : 3 + i, :] = jnp.sum(sums_ref[i], axis=0, keepdims=True)
        for i in range(inner_width // width):
            part_sum = jnp.sum(sumi_ref[:, i * width : (i + 1) * width], axis=0, keepdims=True)
            total_ref[8 + i : 9 + i, :] = part_sum


def feed(mixed_t, tokens, cotangent, seg, vec, bias_inner, weights, docs):
    count, width = tokens.shape
    inner_width = bias_inner.shape[1]
    arrays, numbered = index_pieces(weights)
    tile = ROW_TILE
    row = pl.BlockSpec((tile, width), lambda i: (i, 0))
    col = pl.BlockSpec((width, tile), lambda i: (0, i))
    wide = pl.BlockSpec((tile, inner_width), lambda i: (i, 0))
    per_row = seg.shape[1] // tile
    sum_rows = -(-(8 + inner_width // width) // 8) * 8
    out = jax.ShapeDtypeStruct
    return pl.pallas_call(
        functools.partial(feed_kernel, numbered, len(arrays), docs),
        grid=(count // tile,),
        in_specs=[
            col,
            row,
            row,
            pl.BlockSpec((8, tile), lambda i: (i // per_row, i % per_row)),
            whole(vec.shape),
            whole(bias_inner.shape),
        ]
        + anywhere(len(arrays)),
        out_specs=[row, col, wide, col, wide, row, row, row, pl.BlockSpec((sum_rows, width), lambda i: (0, 0))],
        out_shape=[
            out((count, width), BF),
            out((width, count), BF),
            out((count, inner_width), BF),
            out((width, count), BF),
            out((count, inner_width), BF),
            out((count, width), F32),
            out((count, width), BF),
            out((count, width), BF),
            out((sum_rows, width), F32),
        ],
        scratch_shapes=[
            pltpu.VMEM((width, width), BF),
            pltpu.VMEM((width, inner_width), BF),
            pltpu.VMEM((inner_width, width), BF),
            pltpu.VMEM((tile, inner_width), F32),
            pltpu.VMEM((6, 8, width), F32),
            pltpu.VMEM((8, inner_width), F32),
            pltpu.SemaphoreType.DMA((sum(len(p) for p in numbered),)),
        ],
        compiler_params=params(),
        cost_estimate=cost(4e10, 5e7),
        name="feed",
    )(mixed_t, tokens, cotangent, seg, vec, bias_inner, *arrays)


def attend_back_kernel(n_after, q_ref, k_ref, v_ref, dm_ref, lse_ref, seg_ref, table_ref, *refs):
    dqkv_ref, total_ref, bias_ref, sums_ref = refs[n_after:]

    @pl.when(pl.program_id(0) == 0)
    def _():
        sums_ref[...] = jnp.zeros_like(sums_ref)

    width = q_ref.shape[1]
    scale = 1.0 / math.sqrt(HD)
    seg = seg_ref[0:1, :]
    bias_ref[...] = jnp.where(column_of(seg) == seg, 0.0, -1e30)
    low = lax.broadcasted_iota(jnp.int32, (1, 2 * HD), 1) < HD
    slots = q_ref.shape[0]
    halves = lambda a: (a[:slots], a[slots:])
    for pair in range(width // (2 * HD)):
        first = pair * 2 * HD
        sl = slice(first, first + 2 * HD)
        queries = q_ref[:, sl] * BF(scale)
        keys, d_mixed = k_ref[:, sl], dm_ref[:, sl]
        scores = halves(dot(split_lanes(keys), queries, NT))
        d_probs = halves(dot(split_lanes(v_ref[:, sl]), d_mixed, NT))
        probs_low, d_scores = [], []
        for half in range(2):
            head = 2 * pair + half
            probs = jnp.exp(scores[half] + bias_ref[...] - lse_ref[head : head + 1, :])
            probs_low.append(probs.astype(BF))
            weighted = probs * d_probs[half]
            rows = jnp.sum(weighted, axis=0, keepdims=True)
            d_scores.append((weighted - probs * rows).astype(BF))
        d_scores = jnp.concatenate(d_scores, axis=0)
        d_value = jnp.where(low, *halves(dot(jnp.concatenate(probs_low, axis=0), d_mixed))).astype(BF)
        d_key = jnp.where(low, *halves(dot(d_scores, queries))).astype(BF)
        d_query = (dot(split_rows(keys.T), d_scores) * scale).astype(BF).T
        for i, item in enumerate((d_query, d_key, d_value)):
            dqkv_ref[:, i * width + first : i * width + first + 2 * HD] = item
        sums_ref[0, :, sl] += column_sum(d_query.astype(F32))
        sums_ref[1, :, sl] += column_sum(d_value.astype(F32))

    @pl.when(pl.program_id(0) == pl.num_programs(0) - 1)
    def _():
        total_ref[...] = table_ref[...]
        for i in range(2):
            total_ref[i : i + 1, :] = jnp.sum(sums_ref[i], axis=0, keepdims=True)


def attend_back(query, keys, values, d_mixed, lse, seg, table, after=()):
    count, width = query.shape
    rows = seg.shape[0] // 8
    slots = seg.shape[1]
    row = pl.BlockSpec((slots, width), lambda i: (i, 0))
    return pl.pallas_call(
        functools.partial(attend_back_kernel, len(after)),
        grid=(rows,),
        in_specs=[row] * 4
        + [
            pl.BlockSpec((lse.shape[0] // rows, slots), lambda i: (i, 0)),
            pl.BlockSpec((8, slots), lambda i: (i, 0)),
            whole(table.shape),
        ]
        + anywhere(len(after)),
        out_specs=[
            pl.BlockSpec((slots, 3 * width), lambda i: (i, 0)),
            pl.BlockSpec(table.shape, lambda i: (0, 0)),
        ],
        out_shape=[jax.ShapeDtypeStruct((count, 3 * width), BF), jax.ShapeDtypeStruct(table.shape, F32)],
        scratch_shapes=[pltpu.VMEM((slots, slots), F32), pltpu.VMEM((2, 8, width), F32)],
        compiler_params=params(VMEM_BYTES * 3 // 5),
        cost_estimate=cost(2.1e10, 1.5e7),
        name="attend_back",
    )(query, keys, values, d_mixed, lse, seg, table, *after)


def tokens_kernel(numbered, n_arrays, n_after, dfirst_ref, dqkv_ref, *refs):
    pieces = refs[:n_arrays]
    out_ref, w_ref, sems = refs[n_arrays + n_after :]
    width = dfirst_ref.shape[1]
    targets = [w_ref.at[:, pl.ds(which * width, width)] for which in range(3)]
    ready = load_weights(numbered, pieces, targets, sems)
    for which in range(3):
        ready(which)
    out_ref[...] = dfirst_ref[...] + dot(dqkv_ref[...], w_ref[...], NT)


def tokens_back(d_first, dqkv, weights, after=()):
    count, width = d_first.shape
    arrays, numbered = index_pieces(weights)
    tile = ROW_TILE
    return pl.pallas_call(
        functools.partial(tokens_kernel, numbered, len(arrays), len(after)),
        grid=(count // tile,),
        in_specs=[
            pl.BlockSpec((tile, width), lambda i: (i, 0)),
            pl.BlockSpec((tile, 3 * width), lambda i: (i, 0)),
        ]
        + anywhere(len(arrays) + len(after)),
        out_specs=pl.BlockSpec((tile, width), lambda i: (i, 0)),
        out_shape=jax.ShapeDtypeStruct((count, width), F32),
        scratch_shapes=[
            pltpu.VMEM((width, 3 * width), BF),
            pltpu.SemaphoreType.DMA((sum(len(p) for p in numbered),)),
        ],
        compiler_params=params(VMEM_BYTES * 3 // 5),
        cost_estimate=cost(1e10, 1.5e7),
        name="tokens_back",
    )(d_first, dqkv, *arrays, *after)


ORDER_ONE, ORDER_TWO = (0, Y, X, X | Y), (0, X, Y, X | Y)


def rep_bits():
    me = lax.axis_index("rep")
    return me & 1, me // 2


def arrange(left_ref, left, order):
    size = left.shape[0] // (2 * len(order))
    for which in range(2):
        for place, rel in enumerate(order):
            start = pl.multiple_of((lax.axis_index("fsdp") ^ (rel | which * CORE)) * size, size)
            at = (which * len(order) + place) * size
            left_ref[at : at + size, :] = left[pl.ds(start, size), :]


def place_rows(got, keep, send):
    places, size, _ = keep.shape
    for which, out in enumerate((keep, send)):
        for place in range(places):
            at = (which * places + place) * size
            out[place] = got[at : at + size, :]


def vector_rows(table_ref, shard, size):
    width = table_ref.shape[1]
    row = lax.broadcasted_iota(jnp.int32, (width, 128), 0)
    column = lax.broadcasted_iota(jnp.int32, (width, 128), 1)
    chosen = ((row == shard * size + column) & (column < size)).astype(BF)
    short = dot(table_ref[:8, :].astype(BF), chosen)
    long_size = 4 * size
    per_row = width // long_size
    start = pl.multiple_of(shard % per_row * long_size, 128)
    long = table_ref[pl.ds(8 + shard // per_row, 1), pl.ds(start, long_size)]
    zeros = lambda rows, columns: jnp.zeros((rows, columns), F32)
    return jnp.concatenate(
        [
            jnp.concatenate([short, zeros(8, width - 128)], axis=1),
            jnp.concatenate([long, zeros(1, width - long_size)], axis=1),
            zeros(7, width),
        ],
        axis=0,
    ).astype(BF)


def inner_grad_kernel(n_after, _, left, right, *refs):
    keep, send, left_ref = refs[n_after:]

    @pl.when(pl.program_id(0) == 0)
    def _():
        arrange(left_ref, left, ORDER_ONE)

    place_rows(dot(left_ref[...], right[...]).astype(BF), keep, send)


def inner_grad(left, right, shards, after=()):
    height, depth = left.shape
    wide = right.shape[1]
    chunk = wide // 4
    shape = (4, height // shards, wide)
    one, two = rep_bits()
    parts = jnp.stack([2 * (one ^ (g // 2)) + (two ^ (g % 2)) for g in range(4)]).astype(jnp.int32)
    return pl.pallas_call(
        functools.partial(inner_grad_kernel, len(after)),
        grid_spec=pltpu.PrefetchScalarGridSpec(
            num_scalar_prefetch=1,
            grid=(4,),
            in_specs=[
                pl.BlockSpec((height, depth), lambda g, p: (0, 0), pipeline_mode=pl.Buffered(1)),
                pl.BlockSpec((depth, chunk), lambda g, p: (0, p[g])),
            ]
            + anywhere(len(after)),
            out_specs=[pl.BlockSpec((*shape[:2], chunk), lambda g, p: (0, 0, g))] * 2,
            scratch_shapes=[pltpu.VMEM((height, depth), BF)],
        ),
        out_shape=[jax.ShapeDtypeStruct(shape, BF)] * 2,
        compiler_params=params(),
        cost_estimate=cost(3.5 * height * depth * wide, 4 * height * wide),
        name="inner_grad",
    )(parts, left, right, *after)


def outer_grad_kernel(_, left, right_keep, right_send, keep, send):
    rows = keep.shape[2]
    wide = right_keep.shape[1]
    got = dot(left[...], jnp.concatenate([right_keep[...], right_send[...]], axis=1)).astype(BF)
    one, two = rep_bits()
    blocks = got.shape[0] // rows
    for which, out in enumerate((keep, send)):
        for block in range(blocks):
            half, place = block // (blocks // 2), block % (blocks // 2)
            at = (place // (blocks // 4) ^ two) * (blocks // 4) + place % (blocks // 4)
            rows_part = got[block * rows : (block + 1) * rows, which * wide : (which + 1) * wide]
            out[half ^ one, 0, :, pl.ds(pl.multiple_of(at * wide, 128), wide)] = rows_part


def outer_grad(left, right, shards):
    height, depth = left.shape
    wide = right.shape[1]
    me = lax.axis_index("fsdp")
    places = jnp.stack([me ^ (rel | core) for core in (0, CORE) for rel in ORDER_ONE]).astype(jnp.int32)
    chunk = wide // shards
    shape = (2, 4, height // shards, wide // 2)
    return pl.pallas_call(
        outer_grad_kernel,
        grid_spec=pltpu.PrefetchScalarGridSpec(
            num_scalar_prefetch=1,
            grid=(4,),
            in_specs=[
                pl.BlockSpec((height, depth), lambda g, p: (0, 0), pipeline_mode=pl.Buffered(1)),
                pl.BlockSpec((depth, chunk), lambda g, p: (0, p[g])),
                pl.BlockSpec((depth, chunk), lambda g, p: (0, p[4 + g])),
            ],
            out_specs=[pl.BlockSpec((2, 1, *shape[2:]), lambda g, p: (0, g, 0, 0))] * 2,
        ),
        out_shape=[jax.ShapeDtypeStruct(shape, BF)] * 2,
        compiler_params=params(),
        cost_estimate=cost(3.5 * height * depth * wide, 4 * height * wide),
        name="outer_grad",
    )(places, left, right, right)


def square_grad_kernel(n_after, tokens, mixed, dqkv, d_branch, table, *refs):
    keep_one, send_one, keep_two, send_two, left_ref = refs[n_after:]
    step = pl.program_id(0)
    size = keep_two.shape[1]
    for at, left, order in ((0, tokens, ORDER_ONE), (2, tokens, ORDER_TWO), (3, mixed, ORDER_TWO)):

        @pl.when(step == at)
        def _():
            arrange(left_ref, left, order)

    @pl.when(step < 2)
    def _():
        got = dot(left_ref[...], dqkv[...]).astype(BF)
        for which, out in enumerate((keep_one, send_one)):
            for place, rel in enumerate(ORDER_ONE):
                at = (which * len(ORDER_ONE) + place) * size
                out[place, :size, :] = got[at : at + size, :]

                @pl.when(step == 0)
                def _():
                    shard = lax.axis_index("fsdp") ^ (rel | which * CORE)
                    out[place, size:, :] = vector_rows(table, shard, size)

                @pl.when(step == 1)
                def _():
                    out[place, size:, :] = jnp.zeros((16, out.shape[2]), BF)

    @pl.when(step == 2)
    def _():
        place_rows(dot(left_ref[...], dqkv[...]).astype(BF), keep_two, send_two)

    @pl.when(step == 3)
    def _():
        place_rows(dot(left_ref[...], d_branch[...]).astype(BF), keep_two, send_two)


def square_grad(tokens_t, mixed_t, dqkv, d_branch, table, shards, after=()):
    height, depth = tokens_t.shape
    shape = (4, height // shards, 2 * height)
    block = (*shape[:2], height)
    tall = (shape[0], shape[1] + 16, shape[2])
    one = pl.BlockSpec((*tall[:2], height), lambda g: (0, 0, jnp.minimum(g, 1)))
    two = pl.BlockSpec(block, lambda g: (0, 0, jnp.maximum(g - 2, 0)))
    return pl.pallas_call(
        functools.partial(square_grad_kernel, len(after)),
        grid=(4,),
        in_specs=[
            whole((height, depth)),
            whole((height, depth)),
            pl.BlockSpec((depth, height), lambda g: (0, jnp.minimum(g, 2))),
            whole((depth, height)),
            whole(table.shape),
        ]
        + anywhere(len(after)),
        out_specs=[one, one, two, two],
        out_shape=[jax.ShapeDtypeStruct(tall, BF)] * 2 + [jax.ShapeDtypeStruct(shape, BF)] * 2,
        scratch_shapes=[pltpu.VMEM((height, depth), BF)],
        compiler_params=params(VMEM_BYTES * 3 // 5),
        cost_estimate=cost(1.1e10, 1.5e7),
        name="square_grad",
    )(tokens_t, mixed_t, dqkv, d_branch, table, *after)


def up(x):
    return x.astype(F32)


def fetch(terms, held_ref, sems):
    copies = [
        pltpu.make_async_copy(ref.at[0], held_ref.at[i, pl.ds(0, ref.shape[1])], sems.at[i])
        for i, ref in enumerate(terms)
    ]
    for copy in copies:
        copy.start()
    for copy in copies:
        copy.wait()


def add_places(terms, places):
    total = up(terms[0][places])
    for term in terms[1:]:
        total = total + up(term[places])
    return total.astype(BF)


def total_kernel(n_after, *refs):
    keep, send, held_ref, sems = refs[8 + n_after :]
    size = keep.shape[2]
    me = lax.axis_index("rep")
    fetch(refs[:8], held_ref, sems)
    for quarter in range(4):
        i, columns = quarter // 2, slice(quarter % 2 * size, (quarter % 2 + 1) * size)
        rows = refs[4 * i].shape[1]
        total = up(held_ref[4 * i, :rows, columns])
        for place in range(4 * i + 1, 4 * i + 4):
            total = total + up(held_ref[place, :rows, columns])
        rel = me ^ quarter
        for bit, out in enumerate((keep, send)):

            @pl.when(rel & 1 == bit)
            def _():
                out[rel // 2, :rows] = total.astype(BF)
                if rows < out.shape[1]:
                    out[rel // 2, rows:] = jnp.zeros((out.shape[1] - rows, size), BF)


def total_places(one, two, after):
    _, rows, wide = one[0].shape
    shape = (2, rows, wide // 2)
    return pl.pallas_call(
        functools.partial(total_kernel, len(after)),
        in_specs=anywhere(8 + len(after)),
        out_shape=[jax.ShapeDtypeStruct(shape, BF)] * 2,
        scratch_shapes=[
            pltpu.VMEM((8, rows, wide), BF),
            pltpu.SemaphoreType.DMA((8,)),
        ],
        compiler_params=pltpu.CompilerParams(vmem_limit_bytes=VMEM_BYTES // 4),
        cost_estimate=cost(3e10, 1e7),
        name="total",
    )(*one, *two, *after)


class PairSum:
    def __init__(self, *groups, after=()):
        self.terms = [[keep, flip(pinned(send, *after), "fsdp", CORE)] for keep, send in groups]
        self.bits = (X, Y), (Y, X)

    def far(self, group, *after):
        terms = pinned(self.terms[group], *after)
        out = add_places(terms, slice(2, 4))
        self.terms[group] = [*terms, flip(out, "fsdp", self.bits[group][0])]
        return out

    def near(self, group, *after):
        terms = pinned(self.terms[group], *after)
        out = add_places(terms, slice(1, 2))
        self.terms[group] = [*terms, flip(out, "fsdp", self.bits[group][1])]
        return out

    def total(self, *after):
        self.part, self.send = total_places(*self.terms, after)
        return self.part

    def rep_first(self, *after):
        self.rep = flip(pinned(self.send, *after), "rep", 1)

    def rep_near(self, *after):
        part_far, rep_far = pinned((self.part, self.rep), *after)
        out = (up(part_far[1]) + up(rep_far[1])).astype(BF)
        self.rep_far = flip(out, "rep", 2)
        return out

    def own(self, *after):
        terms = pinned((self.part[0], self.rep[0], self.rep_far), *after)
        self.mine = add_places([t[None] for t in terms], 0)
        self.two = flip(self.mine, "rep", 2)
        return self.mine

    def own_near(self, *after):
        self.one = flip(pinned(self.mine, *after), "rep", 1)

    def parts(self, *after):
        three = flip(pinned(self.two, *after), "rep", 1)
        return [self.mine, self.one, self.two, three]


class Sum:
    def __init__(self, keep, send):
        self.keep, self.core = keep, flip(send, "fsdp", CORE)
        self.rep_first = keep.ndim == 4
        self.quarter = keep.shape[-1] // (2 if self.rep_first else 4)
        self.got = []

    def add(self, index, terms, *after):
        terms = [(self.keep, index), (self.core, index), *terms]
        arrays = pinned([array for array, _ in terms], *after)
        total = None
        for array, (_, at) in zip(arrays, terms):
            total = up(array[at]) if total is None else total + up(array[at])
        return total.astype(BF)

    def send(self, out, axis, bit):
        self.got.append(flip(out, axis, bit))
        return out

    def first(self, *after):
        if self.rep_first:
            return self.send(self.add((1,), [], *after), "rep", 1)
        return self.send(self.add((slice(2, 4),), [], *after), "fsdp", X)

    def second(self, *after):
        if self.rep_first:
            out = self.add((0, slice(2, 4)), [(self.got[0], slice(2, 4))], *after)
            return self.send(out, "fsdp", X)
        return self.send(self.add((slice(1, 2),), [(self.got[0], slice(1, 2))], *after), "fsdp", Y)

    def third(self, *after):
        if self.rep_first:
            got = [(g, slice(1, 2)) for g in self.got]
            return self.send(self.add((0, slice(1, 2)), got, *after), "fsdp", Y)
        columns = (slice(None), slice(2 * self.quarter, 4 * self.quarter))
        got = [(g, (0, *columns)) for g in self.got]
        return self.send(self.add((0, *columns), got, *after), "rep", 1)

    def rest(self, columns):
        columns = (slice(None), columns)
        if self.rep_first:
            return (0, 0, *columns), [(g, (0, *columns)) for g in self.got[:3]]
        return (0, *columns), [(g, (0, *columns)) for g in self.got[:2]] + [(self.got[2], columns)]

    def fourth(self, *after):
        index, got = self.rest(slice(self.quarter, 2 * self.quarter))
        return self.send(self.add(index, got, *after), "rep", 2)

    def own(self, *after):
        index, got = self.rest(slice(0, self.quarter))
        self.mine = self.add(index, [*got, (self.got[3], slice(None))], *after)
        self.two = flip(self.mine, "rep", 2)
        return self.mine

    def own_near(self, *after):
        self.one = flip(pinned(self.mine, *after), "rep", 1)

    def parts(self, *after):
        three = flip(pinned(self.two, *after), "rep", 1)
        return [self.mine, self.one, self.two, three]


def gathered(parts, held_ref, factor):
    one, two = rep_bits()
    for rel, ref in enumerate(parts):
        place = 2 * (one ^ (rel & 1)) + (two ^ (rel // 2))
        held_ref[place, : ref.shape[0]] = up(ref[...]) * factor


def finish_inner_kernel(factor, *refs):
    parts, out, held_ref = refs[:4], refs[4], refs[5]
    gathered(parts, held_ref, factor)
    size = held_ref.shape[2]
    for i in range(4):
        out[:, i * size : (i + 1) * size] = held_ref[i]


def finish_outer_kernel(factor, *refs):
    parts, out, held_ref = refs[:4], refs[4], refs[5]
    gathered(parts, held_ref, factor)
    rows, size = out.shape[0], held_ref.shape[2]
    blocks = [held_ref[i, :, at : at + rows] for i in range(4) for at in range(0, size, rows)]
    out[...] = jnp.concatenate(blocks, axis=0).T


def finish_square_kernel(factor, *refs):
    parts, outs, held_ref = refs[:4], refs[4:-1], refs[-1]
    me = lax.axis_index("rep")
    for rel, ref in enumerate(parts):
        held_ref[me ^ rel] = up(ref[...]) * factor
    size = outs[0].shape[0]
    for i in range(4):
        outs[i][...] = held_ref[i, :size]
    for i, out in enumerate(outs[4:]):
        out[...] = held_ref[0, size + i, : out.shape[0]]


def finish(kernel, parts, factor, shapes):
    return pl.pallas_call(
        functools.partial(kernel, factor),
        out_shape=[jax.ShapeDtypeStruct(shape, F32) for shape in shapes],
        scratch_shapes=[pltpu.VMEM((4, *parts[0].shape), F32)],
        compiler_params=pltpu.CompilerParams(vmem_limit_bytes=VMEM_BYTES // 4),
        cost_estimate=cost(2e9, 1e7),
        name="finish",
    )(*parts)


def all_sum(values, axes=("fsdp", "rep")):
    for axis in axes:
        n = lax.axis_size(axis)
        if n & (n - 1):
            values = lax.psum(values, axis)
            continue
        bit = 1
        while bit < n:
            values = values + flip(values, axis, bit)
            bit *= 2
    return values


def body(
    tokens,
    doc_lengths,
    query_weight,
    key_weight,
    value_weight,
    output_weight,
    inner_weight,
    outer_weight,
    query_bias,
    value_bias,
    output_bias,
    inner_bias,
    outer_bias,
    first_gain,
    first_shift,
    second_gain,
    second_shift,
    cotangent,
):
    rows, slots, width = tokens.shape
    count = rows * slots
    docs = doc_lengths.shape[1]
    n_fsdp = lax.axis_size("fsdp")
    n_rep = lax.axis_size("rep")
    shard = query_weight.shape[0]
    outer_shard = outer_weight.shape[0]
    inner_width = inner_weight.shape[1]
    direct = n_fsdp == 8 and n_rep == 4 and shard % 16 == 0

    vectors = (
        query_bias,
        value_bias,
        output_bias,
        outer_bias,
        first_gain,
        first_shift,
        second_gain,
        second_shift,
        inner_bias,
    )
    if direct:
        half, outer_half = shard // 2, outer_shard // 2
        blocks = pack(query_weight, key_weight, value_weight, vectors)
        one, two = Gather(blocks[0], X, Y), Gather(blocks[1], Y, X)
        blocks = pack_wide(*pinned((inner_weight, output_weight, outer_weight), *blocks))
        blocks = pinned(blocks, one.near, two.near)
        three, four = Gather(blocks[0], X, Y), Gather(blocks[1], Y, X)
        pairs = stacked(one.block, one.near, two.block, two.near)
        one.go(pairs[0])
        two.go(pairs[1])
        pairs = stacked(three.block, three.near, four.block, four.near, pairs)
        three.go(pairs[0])
        four.go(pairs[1])
        chips_x, chips_y = [
            jnp.concatenate(pinned((item.pair, item.far), pairs), axis=0) for item in (one, two)
        ]
        held_x, held_y = one.held_whole(chips_x), two.held_whole(chips_y)
        qw = part(held_x, 0, shard, shard)
        kw = part(held_x, shard, half, shard) + part(held_y, shard, half, shard, half)
        vw = part(held_y, 0, shard, shard)
        vec, bias_inner = unpack(part(held_x, shard + half, 16, 16), shard, outer_shard)
    else:
        qw, kw, vw, ow, iw, w2 = [
            [(lax.all_gather(w, "fsdp", axis=0, tiled=True), 0, w.shape[0] * n_fsdp, None, 0, 0, 0)]
            for w in (query_weight, key_weight, value_weight, output_weight, inner_weight, outer_weight)
        ]
        small = lax.all_gather(jnp.concatenate(vectors)[None], "fsdp", axis=0, tiled=True).astype(F32)
        vec = small[:, : 8 * shard].reshape(n_fsdp, 8, shard).transpose(1, 0, 2).reshape(8, width)
        bias_inner = small[:, 8 * shard :].reshape(1, inner_width)
        pairs = ()

    places = jnp.arange(docs, dtype=jnp.int32)
    ends = jnp.sum(
        jnp.where(places[None, :, None] >= places[None, None, :], doc_lengths[:, None, :], 0), axis=-1
    )
    slot = jnp.arange(slots, dtype=jnp.int32)
    segment = jnp.sum((slot[None, None, :] >= ends[:, :, None]).astype(jnp.int32), axis=1)
    seg = jnp.broadcast_to(segment[:, None, :].astype(F32), (rows, 8, slots)).reshape(rows * 8, slots)

    flat = tokens.reshape(count, width)
    query, keys, values, mixed_t, tokens_t, lse = attend(flat, seg, vec, (qw, kw, vw), pairs)
    if direct:
        three.far, four.far = pinned((three.far, four.far), lse)
        held_x, held_y = three.held(), four.held()
        iw = part(held_x, 0, half, shard) + part(held_y, 0, half, shard, half)
        ow = [(*piece[:-1], inner_width) for piece in iw]
        w2 = [
            (*piece[:4], outer_shard, which * outer_half + block * half, inner_width + (1 + block) * width)
            for which, held in enumerate((held_x, held_y))
            for block in range(outer_half // half)
            for piece in part(held, 0, half, shard)
        ]
    encoded, hidden_t, activated, d_outer_t, d_inner, d_first, d_branch, d_mixed, table = feed(
        mixed_t, flat, cotangent.reshape(count, width), seg, vec, bias_inner, (ow, iw, w2), docs
    )
    factor = 1.0 / math.sqrt(rows * n_rep * n_fsdp * slots)
    if direct:
        keep_outer, send_outer = outer_grad(d_outer_t, activated, n_fsdp)
        keep_inner, send_inner = inner_grad(hidden_t, d_inner, n_fsdp, (send_outer,))
        outer, inner = Sum(keep_outer, send_outer), Sum(keep_inner, send_inner)
        sent = outer.first(send_inner)
        sent = inner.first(sent)
        dqkv, table = attend_back(query, keys, values, d_mixed, lse, seg, table, (sent,))
        sent = outer.second(dqkv)
        sent = inner.second(sent)
        keep_one, send_one, keep_two, send_two = square_grad(
            tokens_t, mixed_t, dqkv, d_branch, table, n_fsdp, (sent,)
        )
        sent = outer.third(send_one)
        sent = inner.third(sent)
        square = PairSum((keep_one, send_one), (keep_two, send_two), after=(sent,))
        sent = square.far(0, sent)
        sent = square.far(1, sent)
        sent = outer.fourth(sent)
        sent = inner.fourth(sent)
        sent = square.near(0, sent)
        sent = square.near(1, sent)
        sent = outer.own(sent)
        sent = inner.own(sent)
        part_sum = square.total(sent)
        square.rep_first()
        tokens_grad = tokens_back(d_first, dqkv, (qw, kw, vw), (part_sum,))
        sent = square.rep_near(tokens_grad)
        outer.own_near(sent)
        inner.own_near(sent)
        outer_parts = outer.parts(sent)
        inner_parts = inner.parts(sent)
        (outer_all,) = finish(finish_outer_kernel, outer_parts, factor, (outer_weight.shape,))
        (inner_all,) = finish(finish_inner_kernel, inner_parts, factor, (inner_weight.shape,))
        square.own()
        square.own_near()
        shapes = (query_weight.shape,) * 4 + ((shard,),) * 8 + ((outer_shard,),)
        q_all, k_all, v_all, o_all, *short, long = finish(finish_square_kernel, square.parts(), factor, shapes)
    else:
        dqkv, table = attend_back(query, keys, values, d_mixed, lse, seg, table)
        tokens_grad = tokens_back(d_first, dqkv, (qw, kw, vw))

        def shared(left_t, right):
            total = lax.psum_scatter(dot(left_t, right), "fsdp", scatter_dimension=0, tiled=True)
            return up(lax.psum(total.astype(BF), "rep")) * factor

        outer_all = shared(activated.T, d_outer_t.T)
        inner_all = shared(hidden_t, d_inner)
        o_all = shared(mixed_t, d_branch)
        q_all, k_all, v_all = [shared(tokens_t, item) for item in jnp.split(dqkv, 3, axis=1)]
        vectors = all_sum(table[: 8 + inner_width // width]) * factor
        me = lax.axis_index("fsdp")
        short = lax.dynamic_slice_in_dim(vectors[:8], me * shard, shard, axis=1)
        long = lax.dynamic_slice_in_dim(vectors[8:].reshape(inner_width), me * outer_shard, outer_shard, axis=0)
    return (
        encoded.reshape(rows, slots, width),
        tokens_grad.reshape(rows, slots, width),
        q_all,
        k_all,
        v_all,
        o_all,
        inner_all,
        outer_all,
        short[0],
        short[1],
        short[2],
        long,
        short[3],
        short[4],
        short[5],
        short[6],
        short[7],
    )


def solution(mesh):
    data = P(("rep", "fsdp"), None, None)
    matrix, vector = P("fsdp", None), P("fsdp")
    return jax.shard_map(
        body,
        mesh=mesh,
        in_specs=(data, P(("rep", "fsdp"), None)) + (matrix,) * 6 + (vector,) * 9 + (data,),
        out_specs=(data, data) + (matrix,) * 6 + (vector,) * 9,
        check_vma=False,
    )
```
